32 devices in a mesh: sph: 8 (over z, core), fv: 4 (over y, x).
Axes of the slice: x: 2, y: 2, z: 4, core: 2. Of those that a mesh axis runs over, the one named last changes fastest.
Arguments:
- positions: float32 [3, 65536], P(None, ('sph', 'fv')), may hold values from -6 to 6
- particle_temp: float32 [65536], P(('sph', 'fv')), may hold values from -6 to 6
- volume: float32 [65536], P(('sph', 'fv')), may hold values from 0.001953125 to 0.0078125
- nbr_blocks: int32 [256, 16], P(('sph', 'fv')), may hold values from 0 to 255, as said below
- nbr_count: int32 [256], P(('sph', 'fv')), may hold values from 1 to 16, as said below
- iface_part: int32 [32768], P(('sph', 'fv')), may hold values from 0 to 2047
- iface_owner: int32 [32768, 1], P(('sph', 'fv')), may hold values from 0 to 31; in each aligned block of 1024 rows (0 to 1023, 1024 to 2047, ...) at most 64 rows name the same one
- iface_cell: int32 [32768], P(('sph', 'fv')), may hold values from 0 to 8191
- substrate_temp: float32 [32, 256, 1024], P(None, 'sph', 'fv'), may hold values from -6 to 6
- conduct: float32 [32, 256, 1024], P(None, 'sph', 'fv'), may hold values from 0.5 to 1
- laser_cells: int32 [256], replicated, may hold values from 0 to 262143
- laser_power: float32 [256], replicated, may hold values from 0.5 to 4
Outputs:
- particle_out: float32 [65536], P(('sph', 'fv'))
- substrate_out: float32 [32, 256, 1024], P(None, 'sph', 'fv')
The draws below stay inside these ranges and needn't reach their ends.
Inputs may be any that keep to these rules, and one draw needn't show every extreme that they name: `nbr_blocks`: row b lists global block numbers within 8 of b; its first nbr_count[b] entries are distinct and begin with b, the others equal b. `nbr_count`: blocks near the beam have up to 16 live slots, the others far fewer; some block has exactly 16. `iface_owner`: among the 1024 entries of one device at most 64 name the same owner, and in some device exactly 64 do.
All inputs are finite; a program needn't handle non-finite values.
Results may differ from the reference program's by a relative error of at most 0.0001.
Values sent between devices are 32-bit elements; how exact they have to be, the bound alone decides.
No kernel may reach another device: no remote copies, remote signals or barrier semaphores. Data moves between devices by JAX's collectives and lax.ppermute only.
A program may use at most 128 MiB of HBM per device.

```python
import math
import jax
import jax.numpy as jnp
import numpy as np
from jax import lax

PB = 256
BLK_DEV = 8
KN = 16
IF_DEV = 1024
CX = 32
CY = 256
GZ = 32
SUB = 4
TRACK = 256
OWNERS = 32
CAP = 64
P_DEV = 2048
NBLK = 256
NP = 65536
IFACE = 32768
GX = 256
GY = 1024
N_FV = 4


def neighbour_table(rng_key):
    window = 2 * BLK_DEV + 1
    beam_block = jax.random.randint(jax.random.fold_in(rng_key, 11), (), BLK_DEV, NBLK - BLK_DEV)
    keys_all = jax.random.split(jax.random.fold_in(rng_key, 12), NBLK)
    shuffled = jax.vmap(lambda one_key: jax.random.permutation(one_key, window))(keys_all).astype(jnp.int32)
    offsets = jnp.arange(window, dtype=jnp.int32) - BLK_DEV
    block_ids = jnp.arange(NBLK, dtype=jnp.int32)
    candidate = block_ids[:, None] + offsets[None, :]
    inside = (candidate >= 0) & (candidate < NBLK)
    scores = jnp.where(offsets[None, :] == 0, -1, jnp.where(inside, shuffled, window + shuffled))
    order_ids = jnp.argsort(scores, axis=1)
    chosen = jnp.take_along_axis(candidate, order_ids, 1)[:, :KN]
    usable = jnp.sum(inside.astype(jnp.int32), axis=1)
    quiet_count = jax.random.randint(jax.random.fold_in(rng_key, 13), (NBLK,), max(1, KN // 8), KN // 4 + 1)
    near_beam = jnp.abs(block_ids - beam_block) <= BLK_DEV // 2
    live_count = jnp.minimum(jnp.where(near_beam, KN, quiet_count), usable)
    slot_ids = jnp.arange(KN, dtype=jnp.int32)
    block_table = jnp.where(slot_ids[None, :] < live_count[:, None], chosen, block_ids[:, None])
    return (block_table.astype(jnp.int32), live_count.astype(jnp.int32))


def draw_nbr_blocks(key, part):
    return neighbour_table(key)[0]


def draw_nbr_count(key, part):
    return neighbour_table(key)[1]


def plant(array, rng, smallest, high):
    shape = array.shape
    spot = [jax.random.randint(jax.random.fold_in(rng, axis), (), 0, shape[axis]) for axis in range(len(shape))]
    array = array.at[tuple(spot)].set(smallest)
    longest = shape.index(max(shape))
    spot[longest] = (spot[longest] + 1) % shape[longest]
    return array.at[tuple(spot)].set(high)


def steps_of(key, shape, cuts, least, high):
    def one(axis_at, blocks):
        draws = jax.random.uniform(jax.random.fold_in(jax.random.fold_in(key, 6), axis_at), (blocks,), jnp.float32, least / len(cuts), high / len(cuts))
        return jnp.repeat(jnp.exp(draws), shape[axis_at] // blocks).reshape((-1,) + (1,) * (len(shape) - axis_at - 1))

    gain = one(*cuts[0])
    for cut in cuts[1:]:
        gain = gain * one(*cut)
    return gain


def shared_out(rng, own, number, rows, amount, top, most, slope):
    order = jax.random.permutation(rng, amount)
    crowded, ordinary = portions_of(amount, rows * top, most, slope, True), portions_of(amount, rows * top, most, slope, False)
    places = jnp.arange(amount)

    def named(tallies, turn):
        used = int((tallies > 0).sum())
        fixed = max(1, used // 4)
        passed = fixed + (places - fixed + turn * (used - fixed)) % max(1, amount - fixed)
        return jnp.zeros((amount,), jnp.int32).at[order[jnp.where(places < fixed, places, passed)]].set(jnp.asarray(tallies, jnp.int32))

    tallies = jnp.where(number % 4 == 0, named(crowded, number // 4), named(ordinary, number - number // 4 - 1))
    mixed = jax.random.permutation(jax.random.fold_in(own, 3), amount)
    donor, sink = mixed[0:amount // 2 * 2:2], mixed[1:amount // 2 * 2:2]
    room = jnp.minimum(tallies[donor] - 1, most - tallies[sink]) // 2
    room = jnp.where((donor == order[0]) | (sink == order[0]) | (tallies[sink] == 0), 0, jnp.maximum(room, 0))
    passed = jax.random.randint(jax.random.fold_in(own, 4), (amount // 2,), 0, 1 << 20) % (room + 1)
    tallies = tallies.at[donor].add(-passed).at[sink].add(passed)
    items = jnp.searchsorted(jnp.cumsum(tallies), jnp.arange(rows * top), side="right").astype(jnp.int32)
    grid = items.reshape(top, rows).T
    grid = grid[jax.random.permutation(jax.random.fold_in(own, 1), rows)]
    turn = jax.random.randint(jax.random.fold_in(own, 2), (rows, 1), 0, top)
    return jnp.take_along_axis(grid, (jnp.arange(top)[None, :] + turn) % top, axis=1)


def portions_of(amount, total, bound, skew, full):
    weights = [(1 << 20) // math.isqrt(grade ** skew) + 1 for grade in range(1, amount + 1)]
    largest = bound if full else min(bound, max(-(-total // amount), total * weights[0] // sum(weights)))
    least = 1 if total - largest >= amount - 1 else 0
    holding, spare = [largest] + [least] * (amount - 1), total - largest - least * (amount - 1)
    while spare > 0:
        free = [i for i in range(1, amount) if holding[i] < largest] or [i for i in range(1, amount) if holding[i] < bound]
        whole, remaining = sum([weights[i] for i in free]), spare
        for i in free:
            more = min(bound - holding[i], max(1, remaining * weights[i] // whole), spare)
            holding[i] = holding[i] + more
            spare = spare - more
    return np.array(holding)


def centred(key, shape, scale, most, shards=(), kind=jnp.bfloat16):
    level = steps_of(key, shape, shards, -0.22, 0.18) if shards else 1.0
    array = jax.random.normal(key, shape, jnp.float32) * scale * level
    return jnp.minimum(jnp.maximum(array, -most), most).astype(kind)


def setup_inputs(seed: int = 0) -> dict:
    splits = jax.random.split(jax.random.key(seed), 13)
    positions = centred(splits[0], (3, NP), 1.0, 6.0, ((1, 32),), jnp.float32)
    particle_temp = centred(splits[1], (NP,), 1.0, 6.0, ((0, 32),), jnp.float32)
    volume = jnp.clip(jnp.exp(math.log(0.0078125) - 1.3862944 * jax.random.uniform(splits[2], (NP,), jnp.float32) ** steps_of(splits[2], (NP,), ((0, 32),), -0.2, 0.2)), 0.001953125, 0.0078125)
    nbr_blocks = draw_nbr_blocks(jax.random.fold_in(splits[12], 71), 0)
    nbr_count = draw_nbr_count(jax.random.fold_in(splits[12], 71), 0)
    iface_part = plant(jax.random.randint(splits[5], (IFACE,), 0, P_DEV), jax.random.fold_in(splits[5], 1), 0, P_DEV - 1).astype(jnp.int32)
    iface_owner_keys = jax.random.split(jax.random.fold_in(splits[6], 1), IFACE // IF_DEV)
    iface_owner_turns = jax.random.permutation(jax.random.fold_in(splits[6], 3), IFACE // IF_DEV)
    iface_owner = jax.vmap(lambda own, number: shared_out(jax.random.fold_in(splits[6], 2), own, number, IF_DEV, OWNERS, 1, CAP, 2))(iface_owner_keys, iface_owner_turns).reshape((IFACE, 1))
    iface_cell = plant(jax.random.randint(splits[7], (IFACE,), 0, CX * CY), jax.random.fold_in(splits[7], 1), 0, (CX * CY) - 1).astype(jnp.int32)
    substrate_temp = centred(splits[8], (GZ, GX, GY), 1.0, 6.0, ((1, 8), (2, 4)), jnp.float32)
    conduct = jnp.clip(0.5 + 0.5 * jax.random.uniform(splits[9], (GZ, GX, GY), jnp.float32) ** steps_of(splits[9], (GZ, GX, GY), ((1, 8), (2, 4)), -0.2, 0.2), 0.5, 1.0)
    laser_cells = plant(jax.random.randint(splits[10], (TRACK,), 0, GX * GY), jax.random.fold_in(splits[10], 1), 0, (GX * GY) - 1).astype(jnp.int32)
    laser_power = jnp.clip(jnp.exp(jax.random.uniform(splits[11], (TRACK,), jnp.float32, math.log(0.5), math.log(4.0))), 0.5, 4.0)
    return {"positions": positions, "particle_temp": particle_temp, "volume": volume, "nbr_blocks": nbr_blocks, "nbr_count": nbr_count, "iface_part": iface_part, "iface_owner": iface_owner, "iface_cell": iface_cell, "substrate_temp": substrate_temp, "conduct": conduct, "laser_cells": laser_cells, "laser_power": laser_power}


KERNEL_SCALE = 0.5
SPH_STEP = 0.05
CONTACT_GAIN = 1.0
PARTICLE_SHARE = 0.5
SURFACE_GAIN = 0.5
LAMBDA_STEP = 0.1


def pair_heat(own_blocks, other_blocks):
    diff_x = own_blocks[:, 0, :, None] - other_blocks[:, 0, None, :]
    diff_y = own_blocks[:, 1, :, None] - other_blocks[:, 1, None, :]
    diff_z = own_blocks[:, 2, :, None] - other_blocks[:, 2, None, :]
    distance = diff_x * diff_x + diff_y * diff_y + diff_z * diff_z
    kernel = jnp.exp(-distance * KERNEL_SCALE) * (2.0 * KERNEL_SCALE)
    own_k = 1.0 + 0.5 * jnp.tanh(own_blocks[:, 3])
    other_k = 1.0 + 0.5 * jnp.tanh(other_blocks[:, 3])
    harmonic = 2.0 * own_k[:, :, None] * other_k[:, None, :] / (own_k[:, :, None] + other_k[:, None, :])
    change = other_blocks[:, 3, None, :] - own_blocks[:, 3, :, None]
    return jnp.sum(other_blocks[:, 4, None, :] * harmonic * change * kernel, axis=2)


def conduct_step(field, coef):
    conduct_now = coef * (1.0 + 0.5 * jnp.tanh(field))
    center = field[:, 1:-1, 1:-1]
    center_k = conduct_now[:, 1:-1, 1:-1]
    summed = jnp.zeros_like(center)
    lateral = ((field[:, 2:, 1:-1], conduct_now[:, 2:, 1:-1]), (field[:, :-2, 1:-1], conduct_now[:, :-2, 1:-1]),
               (field[:, 1:-1, 2:], conduct_now[:, 1:-1, 2:]), (field[:, 1:-1, :-2], conduct_now[:, 1:-1, :-2]))
    for side_u, side_k in lateral:
        summed = summed + 0.5 * (center_k + side_k) * (side_u - center)
    below = jnp.concatenate([center[1:], jnp.zeros_like(center[:1])], 0)
    below_k = jnp.concatenate([center_k[1:], center_k[-1:]], 0)
    summed = summed + 0.5 * (center_k + below_k) * (below - center)
    above = jnp.concatenate([center[:1], center[:-1]], 0)
    above_k = jnp.concatenate([center_k[:1], center_k[:-1]], 0)
    summed = summed + 0.5 * (center_k + above_k) * (above - center)
    return center + LAMBDA_STEP * summed


def pair_group(grouped):
    return pair_heat(grouped[0], grouped[1])


def reference(positions, particle_temp, volume, nbr_blocks, nbr_count, iface_part, iface_owner, iface_cell, substrate_temp, conduct, laser_cells, laser_power):
    packed = jnp.concatenate([positions, particle_temp[None], volume[None]], 0)
    blocks = packed.reshape(5, NBLK, PB).transpose(1, 0, 2)
    groups = NBLK // BLK_DEV

    def add_slot(slot, summed):
        column = lax.dynamic_index_in_dim(nbr_blocks, slot, 1, keepdims=False)
        other = jnp.take(blocks, column, axis=0)
        paired = lax.map(pair_group, (blocks.reshape(groups, BLK_DEV, 5, PB), other.reshape(groups, BLK_DEV, 5, PB)))
        live = slot < nbr_count
        return summed + jnp.where(live[:, None], paired.reshape(NBLK, PB), 0.0)

    heat_in = lax.fori_loop(0, KN, add_slot, jnp.zeros((NBLK, PB), jnp.float32)).reshape(NP)

    owner_dev = iface_owner[:, 0]
    grid_x = (owner_dev // N_FV) * CX + iface_cell // CY
    grid_y = (owner_dev % N_FV) * CY + iface_cell % CY
    flat_cell = (grid_x * GY + grid_y).astype(jnp.int32)
    ghost_temp = jnp.take(substrate_temp[0].reshape(GX * GY), flat_cell)
    particle_ids = ((jnp.arange(IFACE, dtype=jnp.int32) // IF_DEV) * P_DEV + iface_part).astype(jnp.int32)
    contact = CONTACT_GAIN * (jnp.take(particle_temp, particle_ids) - ghost_temp)
    cell_flux = jnp.zeros((GX * GY,), jnp.float32).at[flat_cell].add(contact)
    laser_heat = jnp.zeros((GX * GY,), jnp.float32).at[laser_cells].add(laser_power)
    top_layer = substrate_temp[0] + SURFACE_GAIN * (cell_flux + laser_heat).reshape(GX, GY)
    field = jnp.concatenate([top_layer[None], substrate_temp[1:]], 0)
    coef_pad = jnp.pad(conduct, ((0, 0), (1, 1), (1, 1)))
    for section in range(SUB):
        field = conduct_step(jnp.pad(field, ((0, 0), (1, 1), (1, 1))), coef_pad)
    particle_flux = jnp.zeros((NP,), jnp.float32).at[particle_ids].add(contact)
    particle_out = particle_temp + SPH_STEP * heat_in - PARTICLE_SHARE * particle_flux
    return particle_out, field
```

```python
import functools

import jax
import jax.numpy as jnp
from jax import lax
from jax.experimental import pallas as pl
from jax.experimental.pallas import tpu as pltpu
from jax.sharding import PartitionSpec as P

SUB = 4
KERNEL_SCALE = 0.5
SPH_STEP = 0.05
CONTACT_GAIN = 1.0
PARTICLE_SHARE = 0.5
SURFACE_GAIN = 0.5
LAMBDA_STEP = 0.1

F32 = jnp.float32
BF16 = jnp.bfloat16
I32 = jnp.int32
LANE = 128
SUBL = 8
HALO = SUB
PAIR = 2 * HALO
LOG2E = 1.4426950408889634
VMEM_LIMIT = 48 * 1024 * 1024


def split3(x):
    high = x.astype(BF16).astype(F32)
    rest = x - high
    mid = rest.astype(BF16).astype(F32)
    low = (rest - mid).astype(BF16).astype(F32)
    return high, mid, low


def wide(rows):
    return jnp.concatenate([rows[i : i + 1] for i in range(rows.shape[0])], axis=1)


def tall(row):
    return jnp.concatenate(
        [row[:, i * LANE : (i + 1) * LANE] for i in range(row.shape[1] // LANE)], axis=0
    )


def iota(shape, dim):
    return lax.broadcasted_iota(I32, shape, dim)


def rolled(x, shift, axis):
    size = x.shape[axis]
    shift = shift % size
    return x if shift == 0 else pltpu.roll(x, shift, axis)


def dot_nn(a, b):
    return lax.dot_general(a, b, (((1,), (0,)), ((), ())), preferred_element_type=F32)


def dot_nt(a, b):
    return lax.dot_general(a, b, (((1,), (1,)), ((), ())), preferred_element_type=F32)


def hits(number_row, count):
    return iota((count, number_row.shape[1]), 0) == number_row


def chosen(mask, row):
    return jnp.where(mask, row, 0.0).astype(BF16)


def prep_kernel(cap, pos, temp, vol, temp2d, part, owner, cell, u, c,
                request, to_n, to_s, to_e, to_w, rank_out, surface):
    owners = request.shape[0]
    layers, rows_x, rows_y = u.shape
    lane = iota((1, LANE), 1)
    part_row, owner_row, cell_row = wide(part[...]), wide(owner[...]), wide(cell[...])
    entries = part_row.shape[1]
    t_rows = temp2d.shape[0]
    own_hit = hits(owner_row, owners)
    own_f = jnp.where(own_hit, 1.0, 0.0).astype(F32)
    upper = jnp.where(iota((LANE, LANE), 0) <= iota((LANE, LANE), 1), 1.0, 0.0).astype(BF16)
    tiles = entries // LANE
    stacked = jnp.concatenate([own_f[:, i * LANE : (i + 1) * LANE] for i in range(tiles)], axis=0)
    within = dot_nn(stacked.astype(BF16), upper)
    before = jnp.full((owners, 1), -1.0, F32)
    ranks = []
    for i in range(tiles):
        here = within[i * owners : (i + 1) * owners]
        ranks.append(
            jnp.sum(own_f[:, i * LANE : (i + 1) * LANE] * (here + before), axis=0, keepdims=True)
        )
        before = before + here[:, LANE - 1 : LANE]
    rank_row = jnp.concatenate(ranks, axis=1).astype(I32)
    rank_out[...] = tall(rank_row)
    temp_t = jnp.transpose(jnp.concatenate(split3(temp2d[...]), axis=0)).astype(BF16)
    high_hit = jnp.where(hits(part_row // LANE, t_rows), 1.0, 0.0).astype(F32)
    candidates = dot_nn(temp_t, jnp.concatenate([high_hit] * 3, axis=0).astype(BF16))
    own_temp = jnp.sum(
        jnp.where(hits(part_row % LANE, LANE), candidates, 0.0), axis=0, keepdims=True
    )
    t_h, t_m, t_l = split3(own_temp)
    left = jnp.concatenate(
        [
            jnp.where(own_hit, row, 0.0)
            for row in ((cell_row // 64).astype(F32), (cell_row % 64).astype(F32), t_h, t_m, t_l)
        ]
        + [own_f],
        axis=0,
    ).astype(BF16)
    right = jnp.where(hits(rank_row, LANE), 1.0, 0.0).astype(BF16)
    out = dot_nt(left, right)
    piece = [out[i * owners : (i + 1) * owners] for i in range(6)]
    cells = piece[0] * 64.0 + piece[1] + (piece[5] - 1.0)
    temps = piece[2] + piece[3] + piece[4]
    request[...] = jnp.where(lane < cap, cells, rolled(temps, cap, 1))[:, : 2 * cap]
    surface[...] = u[0]
    for z in range(layers):
        top_u, top_c = u[z, 0:SUBL, :], c[z, 0:SUBL, :]
        end_u, end_c = u[z, rows_x - SUBL :, :], c[z, rows_x - SUBL :, :]
        first = iota((SUBL, rows_y), 0) < HALO
        to_n[z] = jnp.where(first, top_u, rolled(top_c, HALO, 0))
        to_s[z] = jnp.where(first, rolled(end_c, HALO, 0), end_u)
    per = LANE // PAIR
    row_tiles = rows_x // SUBL
    low = lane % PAIR < HALO
    particles = temp.shape[1]
    for g in range(layers // per):
        for t in range(row_tiles):
            rows = slice(t * SUBL, (t + 1) * SUBL)
            acc_u = jnp.zeros((SUBL, LANE), F32)
            acc_c = jnp.zeros((SUBL, LANE), F32)
            for k in range(per):
                z = g * per + k
                place = (lane + HALO - PAIR * k) % LANE < PAIR
                edge_u = jnp.where(lane < LANE // 2, u[z, rows, 0:LANE], u[z, rows, rows_y - LANE :])
                edge_c = jnp.where(lane < LANE // 2, c[z, rows, 0:LANE], c[z, rows, rows_y - LANE :])
                acc_u = jnp.where(place, rolled(edge_u, PAIR * k, 1), acc_u)
                acc_c = jnp.where(place, rolled(edge_c, PAIR * k, 1), acc_c)
            acc_c = rolled(acc_c, HALO, 1)
            at = particles + (g * row_tiles + t) * LANE
            to_w[:, at : at + LANE] = jnp.where(low, acc_u, acc_c)
            to_e[:, at : at + LANE] = jnp.where(low, acc_c, acc_u)
    rows = jnp.concatenate(
        [pos[...], temp[...], vol[...], jnp.zeros((3, particles), F32)], axis=0
    )
    to_e[:, :particles] = rows
    to_w[:, :particles] = rows


def surface_kernel(cap, layers, grid_y, n_sph, n_fv, arrived, surface, laser_cells, laser_power,
                   strip_e, strip_w, slots, heated):
    owners = arrived.shape[0]
    rows_x, rows_y = surface.shape
    halo_size = slots.shape[1] - cap
    lane = iota((1, LANE), 1)
    s, f = lax.axis_index("sph"), lax.axis_index("fv")
    fold = LANE // cap
    group = owners // fold
    full = arrived[...]
    if full.shape[1] < LANE:
        full = jnp.concatenate([full, jnp.zeros((owners, LANE - full.shape[1]), F32)], axis=1)
    cells = jnp.zeros((group, LANE), F32)
    temps = jnp.zeros((group, LANE), F32)
    for g in range(fold):
        rows = full[g * group : (g + 1) * group]
        place = (lane >= g * cap) & (lane < (g + 1) * cap)
        cells = jnp.where(place, rolled(rows, g * cap, 1), cells)
        temps = jnp.where(place, rolled(rows, (g - 1) * cap, 1), temps)
    cells = cells.astype(I32)
    used = cells >= 0
    y_tiles = rows_y // LANE
    cell_x, cell_y = cells // rows_y, cells % rows_y
    high = jnp.where(used, (cell_y // LANE) * rows_x + cell_x, -1)
    low = jnp.where(used, cell_y % LANE, -1)
    laser = laser_cells[...]
    laser_x = laser // grid_y - s * rows_x
    laser_y = laser % grid_y - f * rows_y
    mine = (laser_x >= 0) & (laser_x < rows_x) & (laser_y >= 0) & (laser_y < rows_y)
    l_high = jnp.where(mine, (laser_y // LANE) * rows_x + laser_x, -1)
    l_low = jnp.where(mine, laser_y % LANE, -1)
    here = surface[...]
    tall_surface = jnp.concatenate(
        [here[:, i * LANE : (i + 1) * LANE] for i in range(y_tiles)], axis=0
    )
    highs = y_tiles * rows_x
    surf_t = jnp.transpose(jnp.concatenate(split3(tall_surface), axis=0)).astype(BF16)
    flux = jnp.zeros((3 * highs, LANE), F32)
    contact_rows = []
    step = 2
    for p in range(0, group, step):
        hit_h = hits(wide(high[p : p + step]), highs)
        hit_l = hits(wide(low[p : p + step]), LANE)
        one = jnp.where(hit_h, 1.0, 0.0).astype(BF16)
        candidates = dot_nn(surf_t, jnp.concatenate([one] * 3, axis=0))
        ghost = jnp.sum(jnp.where(hit_l, candidates, 0.0), axis=0, keepdims=True)
        contact = jnp.where(
            wide(high[p : p + step]) >= 0, CONTACT_GAIN * (wide(temps[p : p + step]) - ghost), 0.0
        )
        contact_rows.append(contact)
        left = jnp.concatenate([chosen(hit_h, part) for part in split3(contact)], axis=0)
        flux = flux + dot_nt(left, jnp.where(hit_l, 1.0, 0.0).astype(BF16))
    hit_h, hit_l = hits(wide(l_high), highs), hits(wide(l_low), LANE)
    left = jnp.concatenate([chosen(hit_h, part) for part in split3(wide(laser_power[...]))], axis=0)
    flux = flux + dot_nt(left, jnp.where(hit_l, 1.0, 0.0).astype(BF16))
    flux = flux[:highs] + flux[highs : 2 * highs] + flux[2 * highs :]
    flux = jnp.concatenate([flux[i * rows_x : (i + 1) * rows_x] for i in range(y_tiles)], axis=1)
    hot = here + SURFACE_GAIN * flux
    heated[...] = hot
    contact = tall(jnp.concatenate(contact_rows, axis=1))
    slots[:, :halo_size] = jnp.zeros((owners, halo_size), F32)
    for g in range(fold):
        slots[g * group : (g + 1) * group, halo_size:] = rolled(contact, -g * cap, 1)[:, :cap]

    def send(ds, df, row):
        ok = (s + ds >= 0) & (s + ds < n_sph) & (f + df >= 0) & (f + df < n_fv)

        @pl.when(ok)
        def _():
            slots[pl.ds((s + ds) * n_fv + f + df, 1), : row.shape[1]] = row

    send(-1, 0, wide_rows(hot, 0))
    send(1, 0, wide_rows(hot, rows_x - HALO))
    row_tiles = rows_x // SUBL
    west = jnp.zeros((SUBL, LANE), F32)
    east = jnp.zeros((SUBL, LANE), F32)
    for t in range(row_tiles):
        rows = slice(t * SUBL, (t + 1) * SUBL)
        place = (lane >= t * HALO) & (lane < (t + 1) * HALO)
        west = jnp.where(place, rolled(hot[rows, 0:LANE], t * HALO, 1), west)
        east = jnp.where(place, rolled(hot[rows, rows_y - LANE :], (t + 1) * HALO, 1), east)
    send(0, -1, wide(west))
    send(0, 1, wide(east))
    groups = layers * PAIR // LANE
    start = strip_e.shape[1] - groups * row_tiles * LANE
    for strip, df, tile, mark in (
        (strip_w, -1, hot[:, 0:LANE], lane < HALO),
        (strip_e, 1, hot[:, rows_y - LANE :], lane >= LANE - HALO),
    ):
        for ds, t, rows in ((-1, 0, slice(0, HALO)), (1, row_tiles - 1, slice(SUBL - HALO, SUBL))):
            parts = []
            for g in range(groups):
                at = start + (g * row_tiles + t) * LANE
                block = strip[:, at : at + LANE]
                if g == 0:
                    block = jnp.where(mark, tile[t * SUBL : (t + 1) * SUBL], block)
                parts.append(wide(block[rows]))
            send(ds, df, jnp.concatenate(parts, axis=1))


def wide_rows(hot, start):
    return jnp.concatenate([hot[i : i + 1] for i in range(start, start + HALO)], axis=1)


def pair_kernel(n_fv, nbr, count, pos, temp, vol, before, after, heat, left, right, inv_k, temps):
    blocks = count.shape[0]
    particles = temp.shape[1]
    per = particles // blocks
    device = lax.axis_index("sph") * n_fv + lax.axis_index("fv")
    own = jnp.concatenate([pos[...], temp[...], vol[...], jnp.zeros((3, particles), F32)], axis=0)
    row = iota((SUBL, particles), 0)
    for at, rows in enumerate((before[:, :particles], own, after[:, :particles])):
        xyz = jnp.where(row < 3, rows, 0.0)
        norm = jnp.sum(xyz * xyz, axis=0, keepdims=True) * (-KERNEL_SCALE * LOG2E)
        t_row, v_row = rows[3:4], rows[4:5]
        inv = 1.0 / (1.0 + 0.5 * jnp.tanh(t_row))
        weight = jnp.log2(jnp.where(v_row > 0.0, v_row, 1.0) * (4.0 * KERNEL_SCALE))
        j_side = jnp.where(row == 3, norm + weight, jnp.where(row == 4, 1.0, xyz))
        h, m, l = split3(j_side)
        extra = jnp.where(row == 0, inv, jnp.where(row == 1, t_row, 0.0))
        turned = jnp.transpose(jnp.concatenate([h, h, m, h, l, m, extra, extra], axis=0))
        here = slice(at * particles, (at + 1) * particles)
        left[here, :] = turned[:, : 6 * SUBL].astype(BF16)
        inv_k[here, :] = jnp.broadcast_to(turned[:, 6 * SUBL : 6 * SUBL + 1], (particles, LANE))
        temps[here, :] = jnp.broadcast_to(turned[:, 6 * SUBL + 1 : 6 * SUBL + 2], (particles, LANE))
        if at == 1:
            i_side = jnp.where(row == 3, 1.0, jnp.where(row == 4, norm, xyz * (2 * KERNEL_SCALE * LOG2E)))
            h, m, l = split3(i_side)
            right[...] = jnp.concatenate([h, m, h, l, h, m], axis=0).astype(BF16)
            own_inv, own_temp = inv, t_row
    halves = per // LANE
    for b in range(blocks):
        own_right = right[:, b * per : (b + 1) * per]
        cols = [slice(b * per + i * LANE, b * per + (i + 1) * LANE) for i in range(halves)]
        inv_i = [jnp.broadcast_to(own_inv[:, k], (SUBL, LANE)) for k in cols]
        temp_i = [jnp.broadcast_to(own_temp[:, k], (SUBL, LANE)) for k in cols]

        def slot(n, accs):
            j0 = pl.multiple_of((nbr[b, n] - (device - 1) * blocks) * per, per)
            exponent = dot_nn(left[pl.ds(j0, per), :], own_right)
            out = list(accs)
            for r in range(per // SUBL):
                inv_j = inv_k[pl.ds(j0 + r * SUBL, SUBL), :]
                temp_j = temps[pl.ds(j0 + r * SUBL, SUBL), :]
                for i in range(halves):
                    part = exponent[r * SUBL : (r + 1) * SUBL, i * LANE : (i + 1) * LANE]
                    kernel = jnp.exp2(part) * pl.reciprocal(inv_j + inv_i[i], approx=True)
                    out[i] = out[i] + kernel * (temp_j - temp_i[i])
            return tuple(out)

        zero = jnp.zeros((SUBL, LANE), F32)
        accs = lax.fori_loop(0, count[b], slot, (zero,) * halves)
        for i in range(halves):
            heat[b * halves + i : b * halves + i + 1, :] = jnp.sum(accs[i], axis=0, keepdims=True)


def finish_kernel(cap, n_sph, n_fv, u, c, heated, from_n, from_s, from_w, from_e, got,
                  heat, temp2d, part, owner, rank, particle_out, u_out, field, coef, cond):
    layers, rows_x, rows_y = u.shape
    owners = got.shape[0]
    halo_size = got.shape[1] - cap
    s, f = lax.axis_index("sph"), lax.axis_index("fv")
    lane = iota((1, LANE), 1)
    ext_x, ext_y = rows_x + SUBL, rows_y + LANE
    row_tiles = rows_x // SUBL
    per = LANE // PAIR
    groups = layers // per
    scale = LAMBDA_STEP * 0.5 * 0.5

    def slot(ds, df):
        at = jnp.clip(s + ds, 0, n_sph - 1) * n_fv + jnp.clip(f + df, 0, n_fv - 1)
        return got[pl.ds(at, 1), :]

    def flag(ok):
        return jnp.where(ok, 1.0, 0.0).astype(F32)

    has_n, has_s = flag(s > 0), flag(s < n_sph - 1)
    has_w, has_e = flag(f > 0), flag(f < n_fv - 1)
    row_mask = jnp.where(iota((SUBL, 1), 0) < HALO, has_s, has_n)
    lane_mask = jnp.where(lane < LANE // 2, has_e, has_w)
    first = iota((SUBL, rows_y), 0) < HALO

    part_row, owner_row, rank_row = wide(part[...]), wide(owner[...]), wide(rank[...])
    back = got[:, halo_size:]
    if cap < LANE:
        back = jnp.concatenate([back, jnp.zeros((owners, LANE - cap), F32)], axis=1)
    back_t = jnp.transpose(jnp.concatenate(split3(back), axis=0)).astype(BF16)
    own_one = jnp.where(hits(owner_row, owners), 1.0, 0.0).astype(BF16)
    candidates = dot_nn(back_t, jnp.concatenate([own_one] * 3, axis=0))
    contact = jnp.sum(jnp.where(hits(rank_row, LANE), candidates, 0.0), axis=0, keepdims=True)
    t_rows = temp2d.shape[0]
    hit_h = hits(part_row // LANE, t_rows)
    lefts = jnp.concatenate([jnp.where(hit_h, p, 0.0) for p in split3(contact)], axis=0).astype(BF16)
    flux = dot_nt(lefts, jnp.where(hits(part_row % LANE, LANE), 1.0, 0.0).astype(BF16))
    flux = flux[:t_rows] + flux[t_rows : 2 * t_rows] + flux[2 * t_rows :]
    particle_out[...] = temp2d[...] + SPH_STEP * heat[...] - PARTICLE_SHARE * flux

    def from_slots(a, b):
        return jnp.concatenate([tall(slot(*a)[:, : 2 * HALO * LANE]), tall(slot(*b)[:, : 2 * HALO * LANE])], axis=0)

    low = lane % PAIR < HALO
    strips_u, strips_c = [], []
    start = from_e.shape[1] - groups * row_tiles * LANE
    corner_e = [tall(slot(ds, 1)[:, : groups * HALO * LANE]) for ds in (1, -1)]
    corner_w = [tall(slot(ds, -1)[:, : groups * HALO * LANE]) for ds in (1, -1)]
    for g in range(groups):
        tiles_u, tiles_c = [], []
        for t in range(row_tiles + 1):
            if t < row_tiles:
                at = start + (g * row_tiles + t) * LANE
                east, west = from_e[:, at : at + LANE], from_w[:, at : at + LANE]
            else:
                rows = slice(g * HALO, (g + 1) * HALO)
                east = jnp.concatenate([k[rows] for k in corner_e], axis=0)
                west = jnp.concatenate([k[rows] for k in corner_w], axis=0)
            tiles_u.append(jnp.where(low, east, west))
            tiles_c.append(jnp.where(low, west, east))
        strips_u.append(tiles_u)
        strips_c.append(tiles_c)
    for z in range(layers):
        g, k = z // per, z % per
        for t in range(row_tiles + 1):
            rows = slice(t * SUBL, (t + 1) * SUBL)
            mask = lane_mask if t < row_tiles else lane_mask * row_mask
            field[z, rows, rows_y:] = rolled(strips_u[g][t], -PAIR * k, 1) * mask
            coef[z, rows, rows_y:] = rolled(strips_c[g][t], -PAIR * k - HALO, 1) * (mask * scale)
        coef[z, :rows_x, :rows_y] = c[z] * scale
        coef[z, rows_x:, :rows_y] = rolled(jnp.where(first, from_n[z], from_s[z]), HALO, 0) * (row_mask * scale)
        if z > 0:
            field[z, :rows_x, :rows_y] = u[z]
            field[z, rows_x:, :rows_y] = jnp.where(first, from_s[z], from_n[z]) * row_mask
    field[0, :rows_x, :rows_y] = heated[...]
    south, north = slot(1, 0), slot(-1, 0)
    ends = jnp.concatenate(
        [k[:, i * rows_y : (i + 1) * rows_y] for k in (south, north) for i in range(HALO)], axis=0
    )
    field[0, rows_x:, :rows_y] = ends * row_mask
    east, west = tall(slot(0, 1)[:, : SUBL * LANE]), tall(slot(0, -1)[:, : SUBL * LANE])
    for t in range(row_tiles):
        side = jnp.where(lane < LANE // 2, rolled(east, -t * HALO, 1), rolled(west, -HALO - t * HALO, 1))
        field[0, t * SUBL : (t + 1) * SUBL, rows_y:] = side * lane_mask

    tail_mask = jnp.concatenate([jnp.ones((1, rows_y), F32), lane_mask], axis=1)
    for section in range(SUB):
        last = section == SUB - 1

        def conductivity(z, carry):
            cond[z] = coef[z] * (2.0 + jnp.tanh(field[z]))
            return carry

        lax.fori_loop(0, layers, conductivity, 0)

        def update(z, down, bottom):
            here, here_k = field[z], cond[z]
            if bottom:
                flux_z = -2.0 * here_k * here
            else:
                flux_z = (here_k + cond[z + 1]) * (field[z + 1] - here)
            flux_x = (here_k + rolled(here_k, -1, 0)) * (rolled(here, -1, 0) - here)
            flux_y = (here_k + rolled(here_k, -1, 1)) * (rolled(here, -1, 1) - here)
            new = here + (
                (flux_x - rolled(flux_x, 1, 0)) + (flux_y - rolled(flux_y, 1, 1)) + (flux_z - down)
            )
            if last:
                u_out[z] = new[:rows_x, :rows_y]
            else:
                field[z, :rows_x, :rows_y] = new[:rows_x, :rows_y]
                field[z, :rows_x, rows_y:] = new[:rows_x, rows_y:] * lane_mask
                field[z, rows_x:, :] = new[rows_x:] * (row_mask * tail_mask)
            return flux_z

        down = lax.fori_loop(
            0, layers - 1, lambda z, d: update(z, d, False), jnp.zeros((ext_x, ext_y), F32)
        )
        update(layers - 1, down, True)


def call(kernel, outs, ins, scratch=(), specs=None, cost=None):
    vmem = pl.BlockSpec(memory_space=pltpu.VMEM)
    return pl.pallas_call(
        kernel,
        out_shape=outs,
        in_specs=specs or [vmem] * len(ins),
        out_specs=jax.tree.map(lambda _: vmem, outs),
        scratch_shapes=list(scratch),
        compiler_params=pltpu.CompilerParams(vmem_limit_bytes=VMEM_LIMIT),
        cost_estimate=cost,
    )(*ins)


def body(
    positions,
    particle_temp,
    volume,
    nbr_blocks,
    nbr_count,
    iface_part,
    iface_owner,
    iface_cell,
    substrate_temp,
    conduct,
    laser_cells,
    laser_power,
):
    blocks_here = nbr_count.shape[0]
    particles = particle_temp.shape[0]
    per_block = particles // blocks_here
    layers, rows_x, rows_y = substrate_temp.shape
    n_sph, n_fv = lax.axis_size("sph"), lax.axis_size("fv")
    owners = n_sph * n_fv
    entries = iface_part.shape[0]
    cap = max(2, (2 * entries + owners - 1) // owners)
    grid_y = rows_y * n_fv
    ring = ("sph", "fv")
    shape = jax.ShapeDtypeStruct

    def as_tiles(x):
        return x.reshape(-1, LANE)

    pos = positions
    temp_row, vol_row = particle_temp.reshape(1, particles), volume.reshape(1, particles)
    temp2d = as_tiles(particle_temp)
    part2d, owner2d, cell2d = as_tiles(iface_part), as_tiles(iface_owner), as_tiles(iface_cell)
    strip = rows_x * layers * PAIR // SUBL
    message = shape((SUBL, particles + strip), F32)
    edge = shape((layers, SUBL, rows_y), F32)
    request, to_n, to_s, to_e, to_w, rank, surface = call(
        functools.partial(prep_kernel, cap),
        (shape((owners, 2 * cap), F32), edge, edge, message, message, shape(part2d.shape, I32),
         shape((rows_x, rows_y), F32)),
        (pos, temp_row, vol_row, temp2d, part2d, owner2d, cell2d, substrate_temp, conduct),
    )
    arrived = lax.all_to_all(request, ring, split_axis=0, concat_axis=0, tiled=True)
    forth = [(i, i + 1) for i in range(n_sph - 1)]
    back = [(i + 1, i) for i in range(n_sph - 1)]
    from_n = lax.ppermute(to_s, "sph", forth)
    from_s = lax.ppermute(to_n, "sph", back)
    from_w = lax.ppermute(to_e, ring, [(i, i + 1) for i in range(owners - 1)])
    from_e = lax.ppermute(to_w, ring, [(i + 1, i) for i in range(owners - 1)])

    vmem = pl.BlockSpec(memory_space=pltpu.VMEM)
    smem = pl.BlockSpec(memory_space=pltpu.SMEM)
    halo_size = max(HALO * rows_y, layers * PAIR // LANE * HALO * LANE)
    slots, heated = call(
        functools.partial(surface_kernel, cap, layers, grid_y, n_sph, n_fv),
        (shape((owners, halo_size + cap), F32), shape((rows_x, rows_y), F32)),
        (arrived, surface, as_tiles(laser_cells), as_tiles(laser_power), to_e, to_w),
    )
    got = lax.all_to_all(slots, ring, split_axis=0, concat_axis=0, tiled=True)
    heat = call(
        functools.partial(pair_kernel, n_fv),
        shape(temp2d.shape, F32),
        (nbr_blocks, nbr_count, pos, temp_row, vol_row, from_w, from_e),
        scratch=(
            pltpu.VMEM((3 * particles, 6 * SUBL), BF16),
            pltpu.VMEM((6 * SUBL, particles), BF16),
            pltpu.VMEM((3 * particles, LANE), F32),
            pltpu.VMEM((3 * particles, LANE), F32),
        ),
        specs=[smem, smem] + [vmem] * 5,
        cost=pl.CostEstimate(flops=40 * blocks_here * 4 * per_block * per_block, bytes_accessed=1 << 20, transcendentals=1 << 22),
    )
    ext = pltpu.VMEM((layers, rows_x + SUBL, rows_y + LANE), F32)
    particle_out, field = call(
        functools.partial(finish_kernel, cap, n_sph, n_fv),
        (shape(temp2d.shape, F32), shape(substrate_temp.shape, F32)),
        (substrate_temp, conduct, heated, from_n, from_s, from_w, from_e, got, heat, temp2d,
         part2d, owner2d, rank),
        scratch=(ext, ext, ext),
    )
    return (particle_out.reshape(particles), field)


def solution(mesh):
    in_specs = (
        P(None, ("sph", "fv")),
        P(("sph", "fv")),
        P(("sph", "fv")),
        P(("sph", "fv"), None),
        P(("sph", "fv")),
        P(("sph", "fv")),
        P(("sph", "fv"), None),
        P(("sph", "fv")),
        P(None, "sph", "fv"),
        P(None, "sph", "fv"),
        P(),
        P(),
    )
    out_specs = (P(("sph", "fv")), P(None, "sph", "fv"))
    return jax.shard_map(body, mesh=mesh, in_specs=in_specs, out_specs=out_specs, check_vma=False)
```

```python
import functools

import jax
import jax.numpy as jnp
from jax import lax
from jax.experimental import pallas as pl
from jax.experimental.pallas import tpu as pltpu
from jax.sharding import PartitionSpec as P

SUB = 4
KERNEL_SCALE = 0.5
SPH_STEP = 0.05
CONTACT_GAIN = 1.0
PARTICLE_SHARE = 0.5
SURFACE_GAIN = 0.5
LAMBDA_STEP = 0.1

F32 = jnp.float32
BF16 = jnp.bfloat16
I32 = jnp.int32
LANE = 128
SUBL = 8
HALO = SUB
PAIR = 2 * HALO
LOG2E = 1.4426950408889634
VMEM_LIMIT = 48 * 1024 * 1024
FULL_VMEM = 63 * 1024 * 1024


def split3(x):
    high = x.astype(BF16).astype(F32)
    rest = x - high
    mid = rest.astype(BF16).astype(F32)
    low = (rest - mid).astype(BF16).astype(F32)
    return high, mid, low


def wide(rows):
    return jnp.concatenate([rows[i : i + 1] for i in range(rows.shape[0])], axis=1)


def tall(row):
    return jnp.concatenate(
        [row[:, i * LANE : (i + 1) * LANE] for i in range(row.shape[1] // LANE)], axis=0
    )


def iota(shape, dim):
    return lax.broadcasted_iota(I32, shape, dim)


def rolled(x, shift, axis):
    size = x.shape[axis]
    shift = shift % size
    return x if shift == 0 else pltpu.roll(x, shift, axis)


def lane_next(x):
    n = x.shape[1] // LANE
    turned = [pltpu.roll(x[:, i * LANE : (i + 1) * LANE], LANE - 1, 1) for i in range(n)]
    last = iota((1, LANE), 1) == LANE - 1
    return jnp.concatenate([jnp.where(last, turned[(i + 1) % n], turned[i]) for i in range(n)], axis=1)


def lane_before(x):
    n = x.shape[1] // LANE
    turned = [pltpu.roll(x[:, i * LANE : (i + 1) * LANE], 1, 1) for i in range(n)]
    first = iota((1, LANE), 1) == 0
    return jnp.concatenate([jnp.where(first, turned[i - 1], turned[i]) for i in range(n)], axis=1)


def dot_nn(a, b):
    return lax.dot_general(a, b, (((1,), (0,)), ((), ())), preferred_element_type=F32)


def dot_nt(a, b):
    return lax.dot_general(a, b, (((1,), (1,)), ((), ())), preferred_element_type=F32)


def hits(number_row, count):
    return iota((count, number_row.shape[1]), 0) == number_row


def chosen(mask, row):
    return jnp.where(mask, row, 0.0).astype(BF16)


def arrive(refs, count):
    hbm, outs, bufs, sems = refs[:count], refs[count : -count - 1], refs[-count - 1 : -1], refs[-1]
    copies = [pltpu.make_async_copy(a, b, sems.at[i]) for i, (a, b) in enumerate(zip(hbm, bufs))]
    for copy in copies:
        copy.start()
    return outs, bufs, copies


def prep_kernel(cap, owners, *refs):
    outs, bufs, copies = arrive(refs, 10)
    request, ints, laser_cells, laser_power, to_n, to_s, to_e, to_w, surface, corners = outs
    part, owner, cell, temp2d, cells_in, power_in, pos, vol, u, c = bufs
    layers, rows_x, rows_y = u.shape
    lane = iota((1, LANE), 1)
    for copy in copies[:8]:
        copy.wait()
    laser_cells[...] = cells_in[...]
    laser_power[...] = power_in[...]
    temp = wide(temp2d[...])
    part_row, owner_row, cell_row = wide(part[...]), wide(owner[...]), wide(cell[...])
    entries = part_row.shape[1]
    t_rows = temp2d.shape[0]
    own_hit = hits(owner_row, owners)
    own_f = jnp.where(own_hit, 1.0, 0.0).astype(F32)
    upper = jnp.where(iota((LANE, LANE), 0) <= iota((LANE, LANE), 1), 1.0, 0.0).astype(BF16)
    tiles = entries // LANE
    stacked = jnp.concatenate([own_f[:, i * LANE : (i + 1) * LANE] for i in range(tiles)], axis=0)
    within = dot_nn(stacked.astype(BF16), upper)
    before = jnp.full((owners, 1), -1.0, F32)
    ranks = []
    for i in range(tiles):
        here = within[i * owners : (i + 1) * owners]
        ranks.append(
            jnp.sum(own_f[:, i * LANE : (i + 1) * LANE] * (here + before), axis=0, keepdims=True)
        )
        before = before + here[:, LANE - 1 : LANE]
    rank_row = jnp.concatenate(ranks, axis=1).astype(I32)
    ints[...] = jnp.concatenate([part[...], owner[...], tall(rank_row)], axis=0)
    temp_t = jnp.transpose(jnp.concatenate(split3(temp2d[...]), axis=0)).astype(BF16)
    high_hit = jnp.where(hits(part_row // LANE, t_rows), 1.0, 0.0).astype(F32)
    candidates = dot_nn(temp_t, jnp.concatenate([high_hit] * 3, axis=0).astype(BF16))
    own_temp = jnp.sum(
        jnp.where(hits(part_row % LANE, LANE), candidates, 0.0), axis=0, keepdims=True
    )
    t_h, t_m, t_l = split3(own_temp)
    left = jnp.concatenate(
        [
            jnp.where(own_hit, row, 0.0)
            for row in ((cell_row // 64).astype(F32), (cell_row % 64).astype(F32), t_h, t_m, t_l)
        ]
        + [own_f],
        axis=0,
    ).astype(BF16)
    right = jnp.where(hits(rank_row, LANE), 1.0, 0.0).astype(BF16)
    out = dot_nt(left, right)
    piece = [out[i * owners : (i + 1) * owners] for i in range(6)]
    cells = piece[0] * 64.0 + piece[1] + (piece[5] - 1.0)
    temps = piece[2] + piece[3] + piece[4]
    rows = jnp.where(lane < cap, cells, rolled(temps, cap, 1))
    request[...] = jnp.zeros(request.shape, F32)
    for i in range(owners):
        request[i * SUBL : i * SUBL + 1, :] = rows[i : i + 1]
    for copy in copies[8:]:
        copy.wait()
    surface[...] = u[0]
    for z in range(layers):
        top_u, top_c = u[z, 0:SUBL, :], c[z, 0:SUBL, :]
        end_u, end_c = u[z, rows_x - SUBL :, :], c[z, rows_x - SUBL :, :]
        first = iota((SUBL, rows_y), 0) < HALO
        to_n[z] = jnp.where(first, top_u, rolled(top_c, HALO, 0))
        to_s[z] = jnp.where(first, rolled(end_c, HALO, 0), end_u)
    per = LANE // PAIR
    row_tiles = rows_x // SUBL
    low = lane % PAIR < HALO
    particles = temp.shape[1]
    for g in range(layers // per):
        for t in range(row_tiles):
            rows = slice(t * SUBL, (t + 1) * SUBL)
            acc_u = jnp.zeros((SUBL, LANE), F32)
            acc_c = jnp.zeros((SUBL, LANE), F32)
            for k in range(per):
                z = g * per + k
                place = (lane + HALO - PAIR * k) % LANE < PAIR
                edge_u = jnp.where(lane < LANE // 2, u[z, rows, 0:LANE], u[z, rows, rows_y - LANE :])
                edge_c = jnp.where(lane < LANE // 2, c[z, rows, 0:LANE], c[z, rows, rows_y - LANE :])
                acc_u = jnp.where(place, rolled(edge_u, PAIR * k, 1), acc_u)
                acc_c = jnp.where(place, rolled(edge_c, PAIR * k, 1), acc_c)
            acc_c = rolled(acc_c, HALO, 1)
            at = particles + (g * row_tiles + t) * LANE
            to_w[:, at : at + LANE] = jnp.where(low, acc_u, acc_c)
            to_e[:, at : at + LANE] = jnp.where(low, acc_c, acc_u)
    at = particles
    for n, strip in enumerate((to_w, to_e)):
        for m, (t, rows) in enumerate(
            ((0, slice(0, HALO)), (row_tiles - 1, slice(SUBL - HALO, SUBL)))
        ):
            first = (2 * n + m) * SUBL
            corners[first : first + SUBL, :] = jnp.concatenate(
                [
                    strip[rows, at + (g * row_tiles + t) * LANE : at + (g * row_tiles + t + 1) * LANE]
                    for g in range(layers // per)
                ],
                axis=0,
            )
    rows = jnp.concatenate(
        [pos[...], temp, wide(vol[...]), jnp.zeros((3, particles), F32)], axis=0
    )
    to_e[:, :particles] = rows
    to_w[:, :particles] = rows


def surface_kernel(cap, owners, grid_y, n_sph, n_fv, *refs):
    (slots, heated), bufs, copies = arrive(refs, 5)
    arrived, surface, laser_cells, laser_power, corners = bufs
    for copy in copies:
        copy.wait()
    rows_x, rows_y = surface.shape
    slot_rows = slots.shape[0] // owners
    lane = iota((1, LANE), 1)
    s, f = lax.axis_index("sph"), lax.axis_index("fv")
    fold = LANE // cap
    group = owners // fold
    full = jnp.concatenate([arrived[i * SUBL : i * SUBL + 1, :] for i in range(owners)], axis=0)
    cells = jnp.zeros((group, LANE), F32)
    temps = jnp.zeros((group, LANE), F32)
    for g in range(fold):
        rows = full[g * group : (g + 1) * group]
        place = (lane >= g * cap) & (lane < (g + 1) * cap)
        cells = jnp.where(place, rolled(rows, g * cap, 1), cells)
        temps = jnp.where(place, rolled(rows, (g - 1) * cap, 1), temps)
    cells = cells.astype(I32)
    used = cells >= 0
    y_tiles = rows_y // LANE
    cell_x, cell_y = cells // rows_y, cells % rows_y
    high = jnp.where(used, (cell_y // LANE) * rows_x + cell_x, -1)
    low = jnp.where(used, cell_y % LANE, -1)
    laser = laser_cells[...]
    laser_x = laser // grid_y - s * rows_x
    laser_y = laser % grid_y - f * rows_y
    mine = (laser_x >= 0) & (laser_x < rows_x) & (laser_y >= 0) & (laser_y < rows_y)
    l_high = jnp.where(mine, (laser_y // LANE) * rows_x + laser_x, -1)
    l_low = jnp.where(mine, laser_y % LANE, -1)
    here = surface[...]
    tall_surface = jnp.concatenate(
        [here[:, i * LANE : (i + 1) * LANE] for i in range(y_tiles)], axis=0
    )
    highs = y_tiles * rows_x
    surf_t = jnp.transpose(jnp.concatenate(split3(tall_surface), axis=0)).astype(BF16)
    flux = jnp.zeros((3 * highs, LANE), F32)
    contact_rows = []
    step = 2
    for p in range(0, group, step):
        hit_h = hits(wide(high[p : p + step]), highs)
        hit_l = hits(wide(low[p : p + step]), LANE)
        one = jnp.where(hit_h, 1.0, 0.0).astype(BF16)
        candidates = dot_nn(surf_t, jnp.concatenate([one] * 3, axis=0))
        ghost = jnp.sum(jnp.where(hit_l, candidates, 0.0), axis=0, keepdims=True)
        contact = jnp.where(
            wide(high[p : p + step]) >= 0, CONTACT_GAIN * (wide(temps[p : p + step]) - ghost), 0.0
        )
        contact_rows.append(contact)
        left = jnp.concatenate([chosen(hit_h, part) for part in split3(contact)], axis=0)
        flux = flux + dot_nt(left, jnp.where(hit_l, 1.0, 0.0).astype(BF16))
    hit_h, hit_l = hits(wide(l_high), highs), hits(wide(l_low), LANE)
    left = jnp.concatenate([chosen(hit_h, part) for part in split3(wide(laser_power[...]))], axis=0)
    flux = flux + dot_nt(left, jnp.where(hit_l, 1.0, 0.0).astype(BF16))
    flux = flux[:highs] + flux[highs : 2 * highs] + flux[2 * highs :]
    flux = jnp.concatenate([flux[i * rows_x : (i + 1) * rows_x] for i in range(y_tiles)], axis=1)
    hot = here + SURFACE_GAIN * flux
    heated[...] = hot
    contact = tall(jnp.concatenate(contact_rows, axis=1))
    slots[...] = jnp.zeros(slots.shape, F32)
    for g in range(fold):
        back = rolled(contact, -g * cap, 1)
        for i in range(group):
            at = (g * group + i + 1) * slot_rows - 1
            slots[at : at + 1, :] = back[i : i + 1]

    def send(ds, df, rows):
        ok = (s + ds >= 0) & (s + ds < n_sph) & (f + df >= 0) & (f + df < n_fv)

        @pl.when(ok)
        def _():
            at = ((s + ds) * n_fv + f + df) * slot_rows
            for i in range(rows.shape[0]):
                slots[pl.ds(at + i, 1), :] = rows[i : i + 1]

    send(-1, 0, by_tiles(hot[:HALO]))
    send(1, 0, by_tiles(hot[rows_x - HALO :]))
    row_tiles = rows_x // SUBL
    west = jnp.zeros((SUBL, LANE), F32)
    east = jnp.zeros((SUBL, LANE), F32)
    for t in range(row_tiles):
        rows = slice(t * SUBL, (t + 1) * SUBL)
        place = (lane >= t * HALO) & (lane < (t + 1) * HALO)
        west = jnp.where(place, rolled(hot[rows, 0:LANE], t * HALO, 1), west)
        east = jnp.where(place, rolled(hot[rows, rows_y - LANE :], (t + 1) * HALO, 1), east)
    send(0, -1, west)
    send(0, 1, east)
    sub = iota((SUBL, LANE), 0)
    for n, (df, tile, mark) in enumerate(
        ((-1, hot[:, 0:LANE], lane < HALO), (1, hot[:, rows_y - LANE :], lane >= LANE - HALO))
    ):
        for m, ds in enumerate((-1, 1)):
            static = corners[(2 * n + m) * SUBL : (2 * n + m + 1) * SUBL, :]
            end = tile[:SUBL] if ds < 0 else rolled(tile[rows_x - SUBL :], HALO, 0)
            send(ds, df, jnp.where(mark & (sub < HALO), end, static))


def by_tiles(x):
    return jnp.concatenate(
        [x[:, i * LANE : (i + 1) * LANE] for i in range(x.shape[1] // LANE)], axis=0
    )


def pair_kernel(n_fv, nbr, count, own, before, after, heat, left, right, inv_i, temp_i,
                inv_j, temp_j, accs):
    blocks, slots = nbr.shape
    particles = accs.shape[0]
    per = particles // blocks
    halves = per // LANE
    device = lax.axis_index("sph") * n_fv + lax.axis_index("fv")
    row = iota((SUBL, particles), 0)
    for at, ref in enumerate((before, own, after)):
        rows = ref[:, :particles]
        xyz = jnp.where(row < 3, rows, 0.0)
        norm = jnp.sum(xyz * xyz, axis=0, keepdims=True) * (-KERNEL_SCALE * LOG2E)
        t_row, v_row = rows[3:4], rows[4:5]
        inv = 1.0 / (1.0 + 0.5 * jnp.tanh(t_row))
        weight = jnp.log2(jnp.where(v_row > 0.0, v_row, 1.0) * (4.0 * KERNEL_SCALE))
        h, m, l = split3(jnp.where(row == 3, norm + weight, jnp.where(row == 4, 1.0, xyz)))
        j_side = jnp.concatenate([h, h, m, h, l, m], axis=0).astype(BF16)
        inv_rows = jnp.broadcast_to(inv, (SUBL, particles))
        temp_rows = jnp.broadcast_to(t_row, (SUBL, particles))
        for b in range(blocks):
            cols = slice(b * per, (b + 1) * per)
            right[at * blocks + b] = j_side[:, cols]
            inv_j[at * blocks + b] = inv_rows[:, cols]
            temp_j[at * blocks + b] = temp_rows[:, cols]
        if at == 1:
            scaled = xyz * (2 * KERNEL_SCALE * LOG2E)
            h, m, l = split3(jnp.where(row == 3, 1.0, jnp.where(row == 4, norm, scaled)))
            extra = jnp.where(row == 0, inv, jnp.where(row == 1, t_row, 0.0))
            turned = jnp.transpose(jnp.concatenate([h, m, h, l, h, m, extra, extra], axis=0))
            left[...] = turned[:, : 6 * SUBL].astype(BF16)
            inv_i[...] = jnp.broadcast_to(turned[:, 6 * SUBL : 6 * SUBL + 1], (particles, LANE))
            temp_i[...] = jnp.broadcast_to(turned[:, 6 * SUBL + 1 : 6 * SUBL + 2], (particles, LANE))
    nothing = 3 * blocks
    k_row = iota((6 * SUBL, per), 0)
    right[nothing] = jnp.where(k_row == 3, -16384.0, 0.0).astype(BF16)
    inv_j[nothing] = jnp.ones((SUBL, per), F32)
    temp_j[nothing] = jnp.zeros((SUBL, per), F32)
    accs[...] = jnp.zeros(accs.shape, F32)
    together = 4

    def one_block(b, carry):
        live = count[b]
        i0 = pl.multiple_of(b * per, per)

        def some_slots(n, carry):
            who = []
            for q in range(together):
                at = n * together + q
                local = nbr[b, jnp.minimum(at, slots - 1)] - (device - 1) * blocks
                who.append(jnp.where(at < live, local, nothing))
            exponents = [dot_nn(left[pl.ds(i0, per), :], right[k]) for k in who]
            invs = [[inv_j[k, :, i * LANE : (i + 1) * LANE] for i in range(halves)] for k in who]
            temps = [[temp_j[k, :, i * LANE : (i + 1) * LANE] for i in range(halves)] for k in who]
            for r in range(per // SUBL):
                here = pl.ds(i0 + r * SUBL, SUBL)
                own_inv, own_temp = inv_i[here, :], temp_i[here, :]
                acc = accs[here, :]
                for q in range(together):
                    for i in range(halves):
                        part = exponents[q][r * SUBL : (r + 1) * SUBL, i * LANE : (i + 1) * LANE]
                        kernel = jnp.exp2(part) * pl.reciprocal(invs[q][i] + own_inv, approx=True)
                        acc = acc + kernel * (temps[q][i] - own_temp)
                accs[here, :] = acc
            return carry

        return lax.fori_loop(0, (live + together - 1) // together, some_slots, carry)

    lax.fori_loop(0, blocks, one_block, 0)
    ones = jnp.ones((SUBL, LANE), BF16)
    total = sum(dot_nt(ones, part.astype(BF16)) for part in split3(accs[...]))
    heat[...] = tall(total[0:1])


def finish_kernel(cap, n_sph, n_fv, u, c, heated, from_n, from_s, from_w, from_e, got,
                  heat, own, ints, particle_out, u_out, field, other, coef, coef_r, cond, down):
    layers, rows_x, rows_y = u.shape
    owners = n_sph * n_fv
    slot_rows = got.shape[0] // owners
    s, f = lax.axis_index("sph"), lax.axis_index("fv")
    lane = iota((1, LANE), 1)
    ext_x, ext_y = rows_x + SUBL, rows_y + LANE
    row_tiles = rows_x // SUBL
    per = LANE // PAIR
    groups = layers // per
    scale = LAMBDA_STEP * 0.5 * 0.5

    def slot(ds, df):
        at = jnp.clip(s + ds, 0, n_sph - 1) * n_fv + jnp.clip(f + df, 0, n_fv - 1)
        return jnp.concatenate(
            [got[pl.ds(at * slot_rows + i, 1), :] for i in range(slot_rows - 1)], axis=0
        )

    def flag(ok):
        return jnp.where(ok, 1.0, 0.0).astype(F32)

    has_n, has_s = flag(s > 0), flag(s < n_sph - 1)
    has_w, has_e = flag(f > 0), flag(f < n_fv - 1)
    row_mask = jnp.where(iota((SUBL, 1), 0) < HALO, has_s, has_n)
    lane_mask = jnp.where(lane < LANE // 2, has_e, has_w)
    first = iota((SUBL, rows_y), 0) < HALO

    third = ints.shape[0] // 3
    part_row, owner_row, rank_row = (wide(ints[i * third : (i + 1) * third]) for i in range(3))
    back = jnp.concatenate(
        [got[(i + 1) * slot_rows - 1 : (i + 1) * slot_rows, :] for i in range(owners)], axis=0
    )
    temp2d = tall(own[3:4, : heat.shape[0] * LANE])
    back_t = jnp.transpose(jnp.concatenate(split3(back), axis=0)).astype(BF16)
    own_one = jnp.where(hits(owner_row, owners), 1.0, 0.0).astype(BF16)
    candidates = dot_nn(back_t, jnp.concatenate([own_one] * 3, axis=0))
    contact = jnp.sum(jnp.where(hits(rank_row, LANE), candidates, 0.0), axis=0, keepdims=True)
    t_rows = temp2d.shape[0]
    hit_h = hits(part_row // LANE, t_rows)
    lefts = jnp.concatenate([jnp.where(hit_h, p, 0.0) for p in split3(contact)], axis=0).astype(BF16)
    flux = dot_nt(lefts, jnp.where(hits(part_row % LANE, LANE), 1.0, 0.0).astype(BF16))
    flux = flux[:t_rows] + flux[t_rows : 2 * t_rows] + flux[2 * t_rows :]
    particle_out[...] = temp2d + SPH_STEP * heat[...] - PARTICLE_SHARE * flux

    low = lane % PAIR < HALO
    strips_u, strips_c = [], []
    start = from_e.shape[1] - groups * row_tiles * LANE
    corner_e = [slot(ds, 1) for ds in (1, -1)]
    corner_w = [slot(ds, -1) for ds in (1, -1)]
    for g in range(groups):
        tiles_u, tiles_c = [], []
        for t in range(row_tiles + 1):
            if t < row_tiles:
                at = start + (g * row_tiles + t) * LANE
                east, west = from_e[:, at : at + LANE], from_w[:, at : at + LANE]
            else:
                rows = slice(g * HALO, (g + 1) * HALO)
                east = jnp.concatenate([k[rows] for k in corner_e], axis=0)
                west = jnp.concatenate([k[rows] for k in corner_w], axis=0)
            tiles_u.append(jnp.where(low, east, west))
            tiles_c.append(jnp.where(low, west, east))
        strips_u.append(tiles_u)
        strips_c.append(tiles_c)
    for z in range(layers):
        g, k = z // per, z % per
        for t in range(row_tiles + 1):
            rows = slice(t * SUBL, (t + 1) * SUBL)
            mask = lane_mask if t < row_tiles else lane_mask * row_mask
            field[z, rows, rows_y:] = rolled(strips_u[g][t], -PAIR * k, 1) * mask
            coef[z, rows, rows_y:] = rolled(strips_c[g][t], -PAIR * k - HALO, 1) * (mask * scale)
        coef[z, :rows_x, :rows_y] = c[z] * scale
        coef[z, rows_x:, :rows_y] = rolled(jnp.where(first, from_n[z], from_s[z]), HALO, 0) * (row_mask * scale)
        if z > 0:
            field[z, :rows_x, :rows_y] = u[z]
            field[z, rows_x:, :rows_y] = jnp.where(first, from_s[z], from_n[z]) * row_mask
    field[0, :rows_x, :rows_y] = heated[...]
    south, north = slot(1, 0), slot(-1, 0)
    ends = jnp.concatenate(
        [
            jnp.concatenate([k[i * HALO : (i + 1) * HALO] for k in (south, north)], axis=0)
            for i in range(rows_y // LANE)
        ],
        axis=1,
    )
    field[0, rows_x:, :rows_y] = ends * row_mask
    east, west = slot(0, 1)[:SUBL], slot(0, -1)[:SUBL]
    for t in range(row_tiles):
        side = jnp.where(lane < LANE // 2, rolled(east, -t * HALO, 1), rolled(west, -HALO - t * HALO, 1))
        field[0, t * SUBL : (t + 1) * SUBL, rows_y:] = side * lane_mask

    def shift_coef(z, carry):
        coef_r[z] = lane_next(coef[z])
        return carry

    lax.fori_loop(0, layers, shift_coef, 0)
    tail_mask = jnp.concatenate([jnp.ones((1, rows_y), F32), lane_mask], axis=1) * row_mask
    lane_mask = jnp.broadcast_to(lane_mask, (rows_x, LANE))
    together = 4
    for section in range(SUB):
        source, target = (field, other) if section % 2 == 0 else (other, field)
        cond[...] = coef[0] * (2.0 + jnp.tanh(source[0]))
        down[...] = jnp.zeros((ext_x, ext_y), F32)

        def some_layers(z0, bottom, source=source, target=target, last=section == SUB - 1):
            here, here_k, from_above = source[z0], cond[...], down[...]
            for i in range(together):
                z = z0 + i
                if bottom and i == together - 1:
                    below = below_k = None
                    flux_z = -2.0 * here_k * here
                else:
                    below = source[z + 1]
                    below_k = coef[z + 1] * (2.0 + jnp.tanh(below))
                    flux_z = (here_k + below_k) * (below - here)
                flux_x = (here_k + rolled(here_k, -1, 0)) * (rolled(here, -1, 0) - here)
                side = lane_next(here)
                flux_y = (here_k + coef_r[z] * (2.0 + jnp.tanh(side))) * (side - here)
                new = here + (
                    (flux_x - rolled(flux_x, 1, 0))
                    + (flux_y - lane_before(flux_y))
                    + (flux_z - from_above)
                )
                if last:
                    u_out[z] = new[:rows_x, :rows_y]
                else:
                    target[z, :rows_x, :rows_y] = new[:rows_x, :rows_y]
                    target[z, :rows_x, rows_y:] = new[:rows_x, rows_y:] * lane_mask
                    target[z, rows_x:, :] = new[rows_x:] * tail_mask
                here, here_k, from_above = below, below_k, flux_z
            if not bottom:
                cond[...] = here_k
                down[...] = from_above

        def step(n, carry, some_layers=some_layers):
            some_layers(n * together, False)
            return carry

        lax.fori_loop(0, layers // together - 1, step, 0)
        some_layers(layers - together, True)


def call(kernel, outs, ins, scratch=(), specs=None, cost=None, limit=VMEM_LIMIT):
    vmem = pl.BlockSpec(memory_space=pltpu.VMEM)
    return pl.pallas_call(
        kernel,
        out_shape=outs,
        in_specs=specs or [vmem] * len(ins),
        out_specs=jax.tree.map(lambda _: vmem, outs),
        scratch_shapes=list(scratch),
        compiler_params=pltpu.CompilerParams(vmem_limit_bytes=limit),
        cost_estimate=cost,
    )(*ins)


def body(
    positions,
    particle_temp,
    volume,
    nbr_blocks,
    nbr_count,
    iface_part,
    iface_owner,
    iface_cell,
    substrate_temp,
    conduct,
    laser_cells,
    laser_power,
):
    blocks_here = nbr_count.shape[0]
    particles = particle_temp.shape[0]
    per_block = particles // blocks_here
    layers, rows_x, rows_y = substrate_temp.shape
    n_sph, n_fv = lax.axis_size("sph"), lax.axis_size("fv")
    owners = n_sph * n_fv
    entries = iface_part.shape[0]
    cap = max(2, (2 * entries + owners - 1) // owners)
    grid_y = rows_y * n_fv
    ring = ("sph", "fv")
    shape = jax.ShapeDtypeStruct

    def as_tiles(x):
        return x.reshape(-1, LANE)

    strip = rows_x * layers * PAIR // SUBL
    message = shape((SUBL, particles + strip), F32)
    edge = shape((layers, SUBL, rows_y), F32)
    hbm = pl.BlockSpec(memory_space=pltpu.HBM)
    vmem = pl.BlockSpec(memory_space=pltpu.VMEM)
    smem = pl.BlockSpec(memory_space=pltpu.SMEM)
    temp2d, lasers = as_tiles(particle_temp), (as_tiles(laser_cells), as_tiles(laser_power))

    def bring(inputs):
        return [pltpu.VMEM(x.shape, x.dtype) for x in inputs] + [pltpu.SemaphoreType.DMA((len(inputs),))]

    inputs = (as_tiles(iface_part), as_tiles(iface_owner), as_tiles(iface_cell), temp2d) + lasers
    inputs += (positions, as_tiles(volume), substrate_temp, conduct)
    top = shape((rows_x, rows_y), F32)
    request, ints, cells_in, power_in, to_n, to_s, to_e, to_w, surface, corners = call(
        functools.partial(prep_kernel, cap, owners),
        (shape((owners * SUBL, LANE), F32), shape((3 * entries // LANE, LANE), I32))
        + tuple(shape(x.shape, x.dtype) for x in lasers)
        + (edge, edge, message, message, top, shape((4 * SUBL, LANE), F32)),
        inputs,
        scratch=bring(inputs),
        specs=[hbm] * len(inputs),
        limit=FULL_VMEM,
    )
    arrived = lax.all_to_all(
        request.reshape(owners, SUBL, LANE), ring, split_axis=0, concat_axis=0, tiled=True
    ).reshape(request.shape)
    forth = [(i, i + 1) for i in range(n_sph - 1)]
    back = [(i + 1, i) for i in range(n_sph - 1)]
    from_n = lax.ppermute(to_s, "sph", forth)
    from_s = lax.ppermute(to_n, "sph", back)
    from_w = lax.ppermute(to_e, ring, [(i, i + 1) for i in range(owners - 1)])
    from_e = lax.ppermute(to_w, ring, [(i + 1, i) for i in range(owners - 1)])

    halo_rows = max(HALO * rows_y // LANE, layers * PAIR // LANE * HALO, SUBL)
    inputs = (arrived, surface, cells_in, power_in, corners)
    slots, heated = call(
        functools.partial(surface_kernel, cap, owners, grid_y, n_sph, n_fv),
        (shape((owners * (halo_rows + 1), LANE), F32), top),
        inputs,
        scratch=bring(inputs),
        specs=[hbm] * len(inputs),
        limit=FULL_VMEM,
    )
    slots, from_w, from_e = lax.optimization_barrier((slots, from_w, from_e))
    got = lax.all_to_all(slots.reshape(owners, -1), ring, split_axis=0, concat_axis=0, tiled=True)
    got = got.reshape(slots.shape)
    wide_j = pltpu.VMEM((3 * blocks_here + 1, SUBL, per_block), F32)
    wide_i = pltpu.VMEM((particles, LANE), F32)
    heat = call(
        functools.partial(pair_kernel, n_fv),
        shape((particles // LANE, LANE), F32),
        (nbr_blocks, nbr_count, to_e, from_w, from_e),
        scratch=(
            pltpu.VMEM((particles, 6 * SUBL), BF16),
            pltpu.VMEM((3 * blocks_here + 1, 6 * SUBL, per_block), BF16),
            wide_i, wide_i, wide_j, wide_j, wide_i,
        ),
        specs=[smem, smem] + [vmem] * 3,
        cost=pl.CostEstimate(
            flops=160 * blocks_here * per_block * per_block, bytes_accessed=1 << 20,
            transcendentals=1 << 22,
        ),
    )
    ext = (rows_x + SUBL, rows_y + LANE)
    cube = pltpu.VMEM((layers,) + ext, F32)
    particle_out, field = call(
        functools.partial(finish_kernel, cap, n_sph, n_fv),
        (shape((particles // LANE, LANE), F32), shape(substrate_temp.shape, F32)),
        (substrate_temp, conduct, heated, from_n, from_s, from_w, from_e, got, heat, to_e, ints),
        scratch=(cube, cube, cube, cube, pltpu.VMEM(ext, F32), pltpu.VMEM(ext, F32)),
    )
    return (particle_out.reshape(particles), field)


def solution(mesh):
    in_specs = (
        P(None, ("sph", "fv")),
        P(("sph", "fv")),
        P(("sph", "fv")),
        P(("sph", "fv"), None),
        P(("sph", "fv")),
        P(("sph", "fv")),
        P(("sph", "fv"), None),
        P(("sph", "fv")),
        P(None, "sph", "fv"),
        P(None, "sph", "fv"),
        P(),
        P(),
    )
    out_specs = (P(("sph", "fv")), P(None, "sph", "fv"))
    return jax.shard_map(body, mesh=mesh, in_specs=in_specs, out_specs=out_specs, check_vma=False)
```

```python
import functools

import jax
import jax.numpy as jnp
from jax import lax
from jax.experimental import pallas as pl
from jax.experimental.pallas import tpu as pltpu
from jax.sharding import PartitionSpec as P

SUB = 4
KERNEL_SCALE = 0.5
SPH_STEP = 0.05
CONTACT_GAIN = 1.0
PARTICLE_SHARE = 0.5
SURFACE_GAIN = 0.5
LAMBDA_STEP = 0.1

F32 = jnp.float32
BF16 = jnp.bfloat16
I32 = jnp.int32
LANE = 128
SUBL = 8
HALO = SUB
PAIR = 2 * HALO
LOG2E = 1.4426950408889634
VMEM_LIMIT = 48 * 1024 * 1024
FULL_VMEM = 63 * 1024 * 1024


def split3(x):
    high = x.astype(BF16).astype(F32)
    rest = x - high
    mid = rest.astype(BF16).astype(F32)
    low = (rest - mid).astype(BF16).astype(F32)
    return high, mid, low


def wide(rows):
    return jnp.concatenate([rows[i : i + 1] for i in range(rows.shape[0])], axis=1)


def tall(row):
    return jnp.concatenate(
        [row[:, i * LANE : (i + 1) * LANE] for i in range(row.shape[1] // LANE)], axis=0
    )


def iota(shape, dim):
    return lax.broadcasted_iota(I32, shape, dim)


def rolled(x, shift, axis):
    size = x.shape[axis]
    shift = shift % size
    return x if shift == 0 else pltpu.roll(x, shift, axis)


def lane_next(x):
    n = x.shape[1] // LANE
    turned = [pltpu.roll(x[:, i * LANE : (i + 1) * LANE], LANE - 1, 1) for i in range(n)]
    last = iota((1, LANE), 1) == LANE - 1
    return jnp.concatenate([jnp.where(last, turned[(i + 1) % n], turned[i]) for i in range(n)], axis=1)


def lane_before(x):
    n = x.shape[1] // LANE
    turned = [pltpu.roll(x[:, i * LANE : (i + 1) * LANE], 1, 1) for i in range(n)]
    first = iota((1, LANE), 1) == 0
    return jnp.concatenate([jnp.where(first, turned[i - 1], turned[i]) for i in range(n)], axis=1)


def dot_nn(a, b):
    return lax.dot_general(a, b, (((1,), (0,)), ((), ())), preferred_element_type=F32)


def dot_nt(a, b):
    return lax.dot_general(a, b, (((1,), (1,)), ((), ())), preferred_element_type=F32)


def hits(number_row, count):
    return iota((count, number_row.shape[1]), 0) == number_row


def chosen(mask, row):
    return jnp.where(mask, row, 0.0).astype(BF16)


def own_place(n_fv):
    return lax.axis_index("sph") * n_fv + lax.axis_index("fv")


def arrive(refs, count):
    hbm, outs, bufs, sems = refs[:count], refs[count : -count - 1], refs[-count - 1 : -1], refs[-1]
    copies = [pltpu.make_async_copy(a, b, sems.at[i]) for i, (a, b) in enumerate(zip(hbm, bufs))]
    for copy in copies:
        copy.start()
    return outs, bufs, copies


def prep_kernel(cap, owners, n_fv, *refs):
    outs, bufs, copies = arrive(refs, 10)
    request, ints, rows_a, rows_b, near_a, near_b, aux = outs
    even = own_place(n_fv) % 2 == 0
    even_row = lax.axis_index("sph") % 2 == 0
    part, owner, cell, temp2d, cells_in, power_in, pos, vol, u, c = bufs
    layers, rows_x, rows_y = u.shape
    lane = iota((1, LANE), 1)
    for copy in copies[:8]:
        copy.wait()
    temp = wide(temp2d[...])
    part_row, owner_row, cell_row = wide(part[...]), wide(owner[...]), wide(cell[...])
    entries = part_row.shape[1]
    t_rows = temp2d.shape[0]
    own_hit = hits(owner_row, owners)
    own_f = jnp.where(own_hit, 1.0, 0.0).astype(F32)
    upper = jnp.where(iota((LANE, LANE), 0) <= iota((LANE, LANE), 1), 1.0, 0.0).astype(BF16)
    tiles = entries // LANE
    stacked = jnp.concatenate([own_f[:, i * LANE : (i + 1) * LANE] for i in range(tiles)], axis=0)
    within = dot_nn(stacked.astype(BF16), upper)
    before = jnp.full((owners, 1), -1.0, F32)
    ranks = []
    for i in range(tiles):
        here = within[i * owners : (i + 1) * owners]
        ranks.append(
            jnp.sum(own_f[:, i * LANE : (i + 1) * LANE] * (here + before), axis=0, keepdims=True)
        )
        before = before + here[:, LANE - 1 : LANE]
    rank_row = jnp.concatenate(ranks, axis=1).astype(I32)
    ints[...] = jnp.concatenate([part[...], owner[...], tall(rank_row)], axis=0)
    temp_t = jnp.transpose(jnp.concatenate(split3(temp2d[...]), axis=0)).astype(BF16)
    high_hit = jnp.where(hits(part_row // LANE, t_rows), 1.0, 0.0).astype(F32)
    candidates = dot_nn(temp_t, jnp.concatenate([high_hit] * 3, axis=0).astype(BF16))
    own_temp = jnp.sum(
        jnp.where(hits(part_row % LANE, LANE), candidates, 0.0), axis=0, keepdims=True
    )
    t_h, t_m, t_l = split3(own_temp)
    left = jnp.concatenate(
        [
            jnp.where(own_hit, row, 0.0)
            for row in ((cell_row // 64).astype(F32), (cell_row % 64).astype(F32), t_h, t_m, t_l)
        ]
        + [own_f],
        axis=0,
    ).astype(BF16)
    right = jnp.where(hits(rank_row, LANE), 1.0, 0.0).astype(BF16)
    out = dot_nt(left, right)
    piece = [out[i * owners : (i + 1) * owners] for i in range(6)]
    cells = piece[0] * 64.0 + piece[1] + (piece[5] - 1.0)
    temps = piece[2] + piece[3] + piece[4]
    rows = jnp.where(lane < cap, cells, rolled(temps, cap, 1))
    request[...] = jnp.zeros(request.shape, F32)
    for i in range(owners):
        request[i * SUBL : i * SUBL + 1, :] = rows[i : i + 1]
    for copy in copies[8:]:
        copy.wait()
    top = by_tiles(u[0])
    track = cells_in.shape[0]
    corners = top.shape[0]
    aux[:corners, :] = top
    tracks = corners + 4 * SUBL
    aux[tracks : tracks + track, :] = cells_in[...].astype(F32)
    aux[tracks + track : tracks + 2 * track, :] = power_in[...]
    for z in range(layers):
        top_u, top_c = u[z, 0:SUBL, :], c[z, 0:SUBL, :]
        end_u, end_c = u[z, rows_x - SUBL :, :], c[z, rows_x - SUBL :, :]
        first = iota((SUBL, rows_y), 0) < HALO
        to_n = jnp.where(first, top_u, rolled(top_c, HALO, 0))
        to_s = jnp.where(first, rolled(end_c, HALO, 0), end_u)
        rows_a[z] = jnp.where(even_row, to_s, to_n)
        rows_b[z] = jnp.where(even_row, to_n, to_s)
    per = LANE // PAIR
    row_tiles = rows_x // SUBL
    low = lane % PAIR < HALO
    particles = temp.shape[1]
    for g in range(layers // per):
        for t in range(row_tiles):
            rows = slice(t * SUBL, (t + 1) * SUBL)
            acc_u = jnp.zeros((SUBL, LANE), F32)
            acc_c = jnp.zeros((SUBL, LANE), F32)
            for k in range(per):
                z = g * per + k
                place = (lane + HALO - PAIR * k) % LANE < PAIR
                edge_u = jnp.where(lane < LANE // 2, u[z, rows, 0:LANE], u[z, rows, rows_y - LANE :])
                edge_c = jnp.where(lane < LANE // 2, c[z, rows, 0:LANE], c[z, rows, rows_y - LANE :])
                acc_u = jnp.where(place, rolled(edge_u, PAIR * k, 1), acc_u)
                acc_c = jnp.where(place, rolled(edge_c, PAIR * k, 1), acc_c)
            acc_c = rolled(acc_c, HALO, 1)
            at = particles + (g * row_tiles + t) * LANE
            near_a[:, at : at + LANE] = jnp.where(low == even, acc_c, acc_u)
            near_b[:, at : at + LANE] = jnp.where(low == even, acc_u, acc_c)
    at = particles
    for n in range(2):
        for m, (t, rows) in enumerate(
            ((0, slice(0, HALO)), (row_tiles - 1, slice(SUBL - HALO, SUBL)))
        ):
            first = corners + (2 * n + m) * SUBL
            places = [at + (g * row_tiles + t) * LANE for g in range(layers // per)]
            tiles = [
                jnp.where(
                    even == (n == 0), near_b[rows, k : k + LANE], near_a[rows, k : k + LANE]
                )
                for k in places
            ]
            aux[first : first + SUBL, :] = jnp.concatenate(tiles, axis=0)
    rows = jnp.concatenate(
        [pos[...], temp, wide(vol[...]), jnp.zeros((3, particles), F32)], axis=0
    )
    near_a[:, :particles] = rows
    near_b[:, :particles] = rows


def surface_kernel(cap, owners, track, grid_y, n_sph, n_fv, arrived, aux, slots, heated):
    rows_x, rows_y = heated.shape
    highs = rows_x * rows_y // LANE
    corners = aux[highs : highs + 4 * SUBL, :]
    laser = aux[highs + 4 * SUBL : highs + 4 * SUBL + track, :].astype(I32)
    laser_power = aux[highs + 4 * SUBL + track :, :]
    slot_rows = slots.shape[0] // owners
    lane = iota((1, LANE), 1)
    s, f = lax.axis_index("sph"), lax.axis_index("fv")
    fold = LANE // cap
    group = owners // fold
    full = jnp.concatenate([arrived[i * SUBL : i * SUBL + 1, :] for i in range(owners)], axis=0)
    cells = jnp.zeros((group, LANE), F32)
    temps = jnp.zeros((group, LANE), F32)
    for g in range(fold):
        rows = full[g * group : (g + 1) * group]
        place = (lane >= g * cap) & (lane < (g + 1) * cap)
        cells = jnp.where(place, rolled(rows, g * cap, 1), cells)
        temps = jnp.where(place, rolled(rows, (g - 1) * cap, 1), temps)
    cells = cells.astype(I32)
    used = cells >= 0
    y_tiles = rows_y // LANE
    cell_x, cell_y = cells // rows_y, cells % rows_y
    high = jnp.where(used, (cell_y // LANE) * rows_x + cell_x, -1)
    low = jnp.where(used, cell_y % LANE, -1)
    laser_x = laser // grid_y - s * rows_x
    laser_y = laser % grid_y - f * rows_y
    mine = (laser_x >= 0) & (laser_x < rows_x) & (laser_y >= 0) & (laser_y < rows_y)
    l_high = jnp.where(mine, (laser_y // LANE) * rows_x + laser_x, -1)
    l_low = jnp.where(mine, laser_y % LANE, -1)
    tall_surface = aux[:highs, :]
    here = jnp.concatenate(
        [tall_surface[i * rows_x : (i + 1) * rows_x] for i in range(y_tiles)], axis=1
    )
    surf_t = jnp.transpose(jnp.concatenate(split3(tall_surface), axis=0)).astype(BF16)
    flux = jnp.zeros((3 * highs, LANE), F32)
    contact_rows = []
    step = 2
    for p in range(0, group, step):
        hit_h = hits(wide(high[p : p + step]), highs)
        hit_l = hits(wide(low[p : p + step]), LANE)
        one = jnp.where(hit_h, 1.0, 0.0).astype(BF16)
        candidates = dot_nn(surf_t, jnp.concatenate([one] * 3, axis=0))
        ghost = jnp.sum(jnp.where(hit_l, candidates, 0.0), axis=0, keepdims=True)
        contact = jnp.where(
            wide(high[p : p + step]) >= 0, CONTACT_GAIN * (wide(temps[p : p + step]) - ghost), 0.0
        )
        contact_rows.append(contact)
        left = jnp.concatenate([chosen(hit_h, part) for part in split3(contact)], axis=0)
        flux = flux + dot_nt(left, jnp.where(hit_l, 1.0, 0.0).astype(BF16))
    hit_h, hit_l = hits(wide(l_high), highs), hits(wide(l_low), LANE)
    left = jnp.concatenate([chosen(hit_h, part) for part in split3(wide(laser_power))], axis=0)
    flux = flux + dot_nt(left, jnp.where(hit_l, 1.0, 0.0).astype(BF16))
    flux = flux[:highs] + flux[highs : 2 * highs] + flux[2 * highs :]
    flux = jnp.concatenate([flux[i * rows_x : (i + 1) * rows_x] for i in range(y_tiles)], axis=1)
    hot = here + SURFACE_GAIN * flux
    heated[...] = hot
    contact = tall(jnp.concatenate(contact_rows, axis=1))
    slots[...] = jnp.zeros(slots.shape, F32)
    for g in range(fold):
        back = rolled(contact, -g * cap, 1)
        for i in range(group):
            at = (g * group + i + 1) * slot_rows - 1
            slots[at : at + 1, :] = back[i : i + 1]

    def send(ds, df, rows):
        ok = (s + ds >= 0) & (s + ds < n_sph) & (f + df >= 0) & (f + df < n_fv)

        @pl.when(ok)
        def _():
            at = ((s + ds) * n_fv + f + df) * slot_rows
            for i in range(rows.shape[0]):
                slots[pl.ds(at + i, 1), :] = rows[i : i + 1]

    send(-1, 0, by_tiles(hot[:HALO]))
    send(1, 0, by_tiles(hot[rows_x - HALO :]))
    row_tiles = rows_x // SUBL
    west = jnp.zeros((SUBL, LANE), F32)
    east = jnp.zeros((SUBL, LANE), F32)
    for t in range(row_tiles):
        rows = slice(t * SUBL, (t + 1) * SUBL)
        place = (lane >= t * HALO) & (lane < (t + 1) * HALO)
        west = jnp.where(place, rolled(hot[rows, 0:LANE], t * HALO, 1), west)
        east = jnp.where(place, rolled(hot[rows, rows_y - LANE :], (t + 1) * HALO, 1), east)
    send(0, -1, west)
    send(0, 1, east)
    sub = iota((SUBL, LANE), 0)
    for n, (df, tile, mark) in enumerate(
        ((-1, hot[:, 0:LANE], lane < HALO), (1, hot[:, rows_y - LANE :], lane >= LANE - HALO))
    ):
        for m, ds in enumerate((-1, 1)):
            static = corners[(2 * n + m) * SUBL : (2 * n + m + 1) * SUBL]
            end = tile[:SUBL] if ds < 0 else rolled(tile[rows_x - SUBL :], HALO, 0)
            send(ds, df, jnp.where(mark & (sub < HALO), end, static))


def by_tiles(x):
    return jnp.concatenate(
        [x[:, i * LANE : (i + 1) * LANE] for i in range(x.shape[1] // LANE)], axis=0
    )


def pair_kernel(n_fv, nbr, count, own, got_a, got_b, heat, left, right, inv_i, temp_i,
                inv_j, temp_j, accs):
    blocks, slots = nbr.shape
    particles = accs.shape[0]
    per = particles // blocks
    halves = per // LANE
    device = own_place(n_fv)
    even = device % 2 == 0
    row = iota((SUBL, particles), 0)
    for at in range(3):
        if at == 1:
            rows = own[:, :particles]
        else:
            rows = jnp.where(even == (at == 0), got_b[:, :particles], got_a[:, :particles])
        xyz = jnp.where(row < 3, rows, 0.0)
        norm = jnp.sum(xyz * xyz, axis=0, keepdims=True) * (-KERNEL_SCALE * LOG2E)
        t_row, v_row = rows[3:4], rows[4:5]
        inv = 1.0 / (1.0 + 0.5 * jnp.tanh(t_row))
        weight = jnp.log2(jnp.where(v_row > 0.0, v_row, 1.0) * (4.0 * KERNEL_SCALE))
        h, m, l = split3(jnp.where(row == 3, norm + weight, jnp.where(row == 4, 1.0, xyz)))
        j_side = jnp.concatenate([h, h, m, h, l, m], axis=0).astype(BF16)
        inv_rows = jnp.broadcast_to(inv, (SUBL, particles))
        temp_rows = jnp.broadcast_to(t_row, (SUBL, particles))
        for b in range(blocks):
            cols = slice(b * per, (b + 1) * per)
            right[at * blocks + b] = j_side[:, cols]
            inv_j[at * blocks + b] = inv_rows[:, cols]
            temp_j[at * blocks + b] = temp_rows[:, cols]
        if at == 1:
            scaled = xyz * (2 * KERNEL_SCALE * LOG2E)
            h, m, l = split3(jnp.where(row == 3, 1.0, jnp.where(row == 4, norm, scaled)))
            extra = jnp.where(row == 0, inv, jnp.where(row == 1, t_row, 0.0))
            turned = jnp.transpose(jnp.concatenate([h, m, h, l, h, m, extra, extra], axis=0))
            left[...] = turned[:, : 6 * SUBL].astype(BF16)
            inv_i[...] = jnp.broadcast_to(turned[:, 6 * SUBL : 6 * SUBL + 1], (particles, LANE))
            temp_i[...] = jnp.broadcast_to(turned[:, 6 * SUBL + 1 : 6 * SUBL + 2], (particles, LANE))
    nothing = 3 * blocks
    k_row = iota((6 * SUBL, per), 0)
    right[nothing] = jnp.where(k_row == 3, -16384.0, 0.0).astype(BF16)
    inv_j[nothing] = jnp.ones((SUBL, per), F32)
    temp_j[nothing] = jnp.zeros((SUBL, per), F32)
    accs[...] = jnp.zeros(accs.shape, F32)
    together = 4

    def one_block(b, carry):
        live = count[b]
        i0 = pl.multiple_of(b * per, per)

        def some_slots(n, carry):
            who = []
            for q in range(together):
                at = n * together + q
                local = nbr[b, jnp.minimum(at, slots - 1)] - (device - 1) * blocks
                who.append(jnp.where(at < live, local, nothing))
            exponents = [dot_nn(left[pl.ds(i0, per), :], right[k]) for k in who]
            invs = [[inv_j[k, :, i * LANE : (i + 1) * LANE] for i in range(halves)] for k in who]
            temps = [[temp_j[k, :, i * LANE : (i + 1) * LANE] for i in range(halves)] for k in who]
            for r in range(per // SUBL):
                here = pl.ds(i0 + r * SUBL, SUBL)
                own_inv, own_temp = inv_i[here, :], temp_i[here, :]
                acc = accs[here, :]
                for q in range(together):
                    for i in range(halves):
                        part = exponents[q][r * SUBL : (r + 1) * SUBL, i * LANE : (i + 1) * LANE]
                        kernel = jnp.exp2(part) * pl.reciprocal(invs[q][i] + own_inv, approx=True)
                        acc = acc + kernel * (temps[q][i] - own_temp)
                accs[here, :] = acc
            return carry

        return lax.fori_loop(0, (live + together - 1) // together, some_slots, carry)

    lax.fori_loop(0, blocks, one_block, 0)
    ones = jnp.ones((SUBL, LANE), BF16)
    total = sum(dot_nt(ones, part.astype(BF16)) for part in split3(accs[...]))
    heat[...] = tall(total[0:1])


def finish_kernel(cap, n_sph, n_fv, u, c, heated, rows_a, rows_b, near_a, near_b, got,
                  heat, own, ints, particle_out, u_out, field, other, coef, cond, row_flux, lane_flux, down, wrap):
    layers, rows_x, rows_y = u.shape
    owners = n_sph * n_fv
    slot_rows = got.shape[0] // owners
    s, f = lax.axis_index("sph"), lax.axis_index("fv")
    lane = iota((1, LANE), 1)
    row_tiles = rows_x // SUBL
    per = LANE // PAIR
    groups = layers // per
    scale = LAMBDA_STEP * 0.5 * 0.5

    def slot(ds, df):
        at = jnp.clip(s + ds, 0, n_sph - 1) * n_fv + jnp.clip(f + df, 0, n_fv - 1)
        return jnp.concatenate(
            [got[pl.ds(at * slot_rows + i, 1), :] for i in range(slot_rows - 1)], axis=0
        )

    def flag(ok):
        return jnp.where(ok, 1.0, 0.0).astype(F32)

    has_n, has_s = flag(s > 0), flag(s < n_sph - 1)
    has_w, has_e = flag(f > 0), flag(f < n_fv - 1)
    third = ints.shape[0] // 3
    part_row, owner_row, rank_row = (wide(ints[i * third : (i + 1) * third]) for i in range(3))
    back = jnp.concatenate(
        [got[(i + 1) * slot_rows - 1 : (i + 1) * slot_rows, :] for i in range(owners)], axis=0
    )
    temp2d = tall(own[3:4, : heat.shape[0] * LANE])
    back_t = jnp.transpose(jnp.concatenate(split3(back), axis=0)).astype(BF16)
    own_one = jnp.where(hits(owner_row, owners), 1.0, 0.0).astype(BF16)
    candidates = dot_nn(back_t, jnp.concatenate([own_one] * 3, axis=0))
    contact = jnp.sum(jnp.where(hits(rank_row, LANE), candidates, 0.0), axis=0, keepdims=True)
    t_rows = temp2d.shape[0]
    hit_h = hits(part_row // LANE, t_rows)
    lefts = jnp.concatenate([jnp.where(hit_h, p, 0.0) for p in split3(contact)], axis=0).astype(BF16)
    flux = dot_nt(lefts, jnp.where(hits(part_row % LANE, LANE), 1.0, 0.0).astype(BF16))
    flux = flux[:t_rows] + flux[t_rows : 2 * t_rows] + flux[2 * t_rows :]
    particle_out[...] = temp2d + SPH_STEP * heat[...] - PARTICLE_SHARE * flux

    slab = rows_x + 2 * HALO
    slabs = LANE // slab
    deep = (layers + slabs - 1) // slabs
    assert slabs * deep == layers + 1 and SUB % 2 == 0
    place = (lane + HALO) % LANE
    spot = place % slab
    in_group = place < slabs * slab
    sides = jnp.where(spot < HALO, has_n, jnp.where(spot < HALO + rows_x, 1.0, has_s))
    lane_mask = jnp.where(in_group, sides, 0.0)
    last_group = in_group & (place >= (slabs - 1) * slab)
    end_mask = jnp.where(last_group, 0.0, lane_mask)
    not_first = jnp.where(place >= slab, 1.0, 0.0)
    sub_first = iota((SUBL, 1), 0) < HALO

    even, even_row = own_place(n_fv) % 2 == 0, s % 2 == 0
    low = lane % PAIR < HALO
    start = near_a.shape[1] - groups * row_tiles * LANE
    corner_e = [slot(ds, 1) for ds in (1, -1)]
    corner_w = [slot(ds, -1) for ds in (1, -1)]
    east_0, west_0 = slot(0, 1)[:SUBL], slot(0, -1)[:SUBL]
    empty = jnp.zeros((LANE - rows_x - 2 * SUBL, LANE), F32)
    turned_u, turned_c = [], []
    for g in range(groups):
        tiles_u, tiles_c = [], []
        for t in range(row_tiles + 1):
            if t < row_tiles:
                at = start + (g * row_tiles + t) * LANE
                a, b = near_a[:, at : at + LANE], near_b[:, at : at + LANE]
                east, west = jnp.where(even, a, b), jnp.where(even, b, a)
            else:
                rows = slice(g * HALO, (g + 1) * HALO)
                east = jnp.concatenate([k[rows] for k in corner_e], axis=0)
                west = jnp.concatenate([k[rows] for k in corner_w], axis=0)
            tile = jnp.where(low, east, west)
            if g == 0 and t < row_tiles:
                tile = jnp.where(lane < HALO, rolled(east_0, -t * HALO, 1), tile)
                tile = jnp.where(lane >= LANE - HALO, rolled(west_0, -HALO - t * HALO, 1), tile)
            tiles_u.append(tile)
            tiles_c.append(jnp.where(low, west, east))
        for tiles, turned in ((tiles_u, turned_u), (tiles_c, turned_c)):
            ends = tiles.pop()
            tiles += [jnp.where(sub_first, ends, 0.0), empty, jnp.where(sub_first, 0.0, ends)]
            turned.append(jnp.transpose(jnp.concatenate(tiles, axis=0)))

    south, north = slot(1, 0), slot(-1, 0)
    ends_0 = jnp.concatenate(
        [
            jnp.concatenate([k[i * HALO : (i + 1) * HALO] for k in (south, north)], axis=0)
            for i in range(rows_y // LANE)
        ],
        axis=1,
    )
    nothing = jnp.zeros((SUBL, rows_y), F32)

    def side_tile(after, before, is_u):
        ok_after, ok_before = after is not None and after < layers, before is not None and before < layers
        a = b = nothing
        if ok_after:
            if is_u and after == 0:
                a = ends_0
            else:
                a = jnp.where(even_row, rows_a[after], rows_b[after])
        if ok_before:
            if is_u and before == 0:
                b = ends_0
            else:
                b = jnp.where(even_row, rows_b[before], rows_a[before])
        return jnp.where(sub_first, a, b) if is_u else rolled(jnp.where(sub_first, b, a), HALO, 0)

    first_row, tiles_y = SUBL, rows_y // SUBL + 2
    for i in range(deep):
        mask = lane_mask if i < deep - 1 else end_mask
        zs = [n * deep + i for n in range(slabs)]
        for is_u, ref, array, factor in ((True, field, u, mask), (False, coef, c, mask * scale)):
            rows = []
            for n, z in enumerate(zs):
                if z >= layers:
                    rows.append(jnp.zeros((rows_x, rows_y), F32))
                else:
                    rows.append(heated[...] if is_u and z == 0 else array[z])
                rows.append(side_tile(z, zs[n + 1] if n + 1 < slabs else None, is_u))
            if slabs * slab < LANE:
                rows.append(side_tile(None, zs[0], is_u))
            rows = jnp.concatenate(rows, axis=0)
            for b in range(rows_y // LANE):
                block = jnp.transpose(rows[:, b * LANE : (b + 1) * LANE])
                ref[i, first_row + b * LANE : first_row + (b + 1) * LANE, :] = block * factor
            before, after = jnp.zeros((SUBL, LANE), F32), jnp.zeros((SUBL, LANE), F32)
            for n, z in enumerate(zs):
                if z >= layers:
                    continue
                g, k = z // per, z % per
                if is_u:
                    e_at, w_at = k * PAIR, (k - 1) % per * PAIR
                    tile_e, tile_w = turned_u[g][e_at : e_at + PAIR], turned_u[g][w_at : w_at + PAIR]
                    after = after + rolled(tile_e, n * slab, 1)
                    before = before + rolled(tile_w, n * slab, 1)
                else:
                    tile = rolled(turned_c[g][k * PAIR : (k + 1) * PAIR], HALO, 0)
                    after = after + rolled(tile, n * slab, 1)
                    before = after
            ref[i, 0:SUBL, :] = before * (factor * has_w)
            ref[i, (tiles_y - 1) * SUBL : tiles_y * SUBL, :] = after * (factor * has_e)
            ref[i, tiles_y * SUBL :, :] = jnp.zeros((SUBL, LANE), F32)
        other[i, tiles_y * SUBL :, :] = jnp.zeros((SUBL, LANE), F32)
    cond[:, tiles_y * SUBL :, :] = jnp.zeros((cond.shape[0], SUBL, LANE), F32)
    row_flux[:, :SUBL, :] = jnp.zeros((row_flux.shape[0], SUBL, LANE), F32)

    def rows_of(t):
        return slice(t * SUBL, (t + 1) * SUBL)

    def some_layers(i0, count, source, target, end):
        def conductivity(n, t):
            return coef[i0 + n, rows_of(t), :] * (2.0 + jnp.tanh(source[i0 + n, rows_of(t), :]))

        tiles = range(tiles_y)
        spots = [(t, n) for t in tiles for n in range(count)]
        for t, n in spots:
            cond[n, rows_of(t), :] = conductivity(n, t)
        for t, n in spots:
            here, here_k = source[i0 + n, rows_of(t), :], cond[n, rows_of(t), :]
            lane_flux[n, rows_of(t), :] = (here_k + pltpu.roll(here_k, LANE - 1, 1)) * (
                pltpu.roll(here, LANE - 1, 1) - here
            )
        for t, n in spots:
            here, here_k = source[i0 + n, rows_of(t), :], cond[n, rows_of(t), :]
            next_row = slice(t * SUBL + 1, (t + 1) * SUBL + 1)
            row_flux[n, rows_of(t + 1), :] = (here_k + cond[n, next_row, :]) * (
                source[i0 + n, next_row, :] - here
            )
        for t in tiles:
            above = down[rows_of(t), :]
            here, here_k = source[i0, rows_of(t), :], cond[0, rows_of(t), :]
            for n in range(count):
                i = i0 + n
                wraps = end and n == count - 1
                if wraps:
                    flux_z = wrap[rows_of(t), :]
                else:
                    below = source[i + 1, rows_of(t), :]
                    below_k = conductivity(n + 1, t) if n + 1 == count else cond[n + 1, rows_of(t), :]
                    beside_k = below_k
                    if end and n == count - 2:
                        beside_k = jnp.where(last_group, here_k, below_k)
                    flux_z = (here_k + beside_k) * (below - here)
                from_y = row_flux[n, rows_of(t + 1), :] - row_flux[n, (t + 1) * SUBL - 1 : (t + 2) * SUBL - 1, :]
                flux_x = lane_flux[n, rows_of(t), :]
                from_x = flux_x - pltpu.roll(flux_x, 1, 1)
                new = here + ((from_x + from_y) + (flux_z - above))
                factor = end_mask if wraps else lane_mask
                if t == 0:
                    factor = factor * has_w
                if t == tiles_y - 1:
                    factor = factor * has_e
                target[i, rows_of(t), :] = new * factor
                above = flux_z
                if not wraps:
                    here, here_k = below, below_k
            if not end:
                down[rows_of(t), :] = above

    def substep(source, target):
        for t in range(tiles_y):
            last_u, first_u = source[deep - 1, rows_of(t), :], source[0, rows_of(t), :]
            last_k = coef[deep - 1, rows_of(t), :] * (2.0 + jnp.tanh(last_u))
            first_k = coef[0, rows_of(t), :] * (2.0 + jnp.tanh(first_u))
            flux = (first_k + pltpu.roll(last_k, slab, 1)) * (first_u - pltpu.roll(last_u, slab, 1))
            flux = flux * not_first
            down[rows_of(t), :] = flux
            wrap[rows_of(t), :] = pltpu.roll(flux, LANE - slab, 1)
        together = cond.shape[0]

        def step(n, carry):
            some_layers(n * together, together, source, target, False)
            return carry

        full = (deep - 2) // together
        lax.fori_loop(0, full, step, 0)
        some_layers(full * together, deep - full * together, source, target, True)

    def two_substeps(n, carry):
        substep(field, other)
        substep(other, field)
        return carry

    lax.fori_loop(0, SUB // 2, two_substeps, 0)
    for i in range(deep):
        rows = jnp.concatenate(
            [
                jnp.transpose(field[i, first_row + b * LANE : first_row + (b + 1) * LANE, :])
                for b in range(rows_y // LANE)
            ],
            axis=1,
        )
        for n in range(slabs):
            z = n * deep + i
            if z < layers:
                u_out[z] = rows[n * slab : n * slab + rows_x]


def call(kernel, outs, ins, scratch=(), specs=None, cost=None, limit=VMEM_LIMIT):
    vmem = pl.BlockSpec(memory_space=pltpu.VMEM)
    return pl.pallas_call(
        kernel,
        out_shape=outs,
        in_specs=specs or [vmem] * len(ins),
        out_specs=jax.tree.map(lambda _: vmem, outs),
        scratch_shapes=list(scratch),
        compiler_params=pltpu.CompilerParams(vmem_limit_bytes=limit),
        cost_estimate=cost,
    )(*ins)


def body(
    positions,
    particle_temp,
    volume,
    nbr_blocks,
    nbr_count,
    iface_part,
    iface_owner,
    iface_cell,
    substrate_temp,
    conduct,
    laser_cells,
    laser_power,
):
    blocks_here = nbr_count.shape[0]
    particles = particle_temp.shape[0]
    per_block = particles // blocks_here
    layers, rows_x, rows_y = substrate_temp.shape
    n_sph, n_fv = lax.axis_size("sph"), lax.axis_size("fv")
    owners = n_sph * n_fv
    entries = iface_part.shape[0]
    cap = max(2, (2 * entries + owners - 1) // owners)
    grid_y = rows_y * n_fv
    ring = ("sph", "fv")
    shape = jax.ShapeDtypeStruct

    def as_tiles(x):
        return x.reshape(-1, LANE)

    strip = rows_x * layers * PAIR // SUBL
    message = shape((SUBL, particles + strip), F32)
    edge = shape((layers, SUBL, rows_y), F32)
    hbm = pl.BlockSpec(memory_space=pltpu.HBM)
    vmem = pl.BlockSpec(memory_space=pltpu.VMEM)
    smem = pl.BlockSpec(memory_space=pltpu.SMEM)
    temp2d, lasers = as_tiles(particle_temp), (as_tiles(laser_cells), as_tiles(laser_power))

    def bring(inputs):
        return [pltpu.VMEM(x.shape, x.dtype) for x in inputs] + [pltpu.SemaphoreType.DMA((len(inputs),))]

    inputs = (as_tiles(iface_part), as_tiles(iface_owner), as_tiles(iface_cell), temp2d) + lasers
    inputs += (positions, as_tiles(volume), substrate_temp, conduct)
    top = shape((rows_x, rows_y), F32)
    track = lasers[0].shape[0]
    aux_rows = rows_x * rows_y // LANE + 4 * SUBL + 2 * track
    request, ints, to_rows_a, to_rows_b, to_near_a, to_near_b, aux = call(
        functools.partial(prep_kernel, cap, owners, n_fv),
        (shape((owners * SUBL, LANE), F32), shape((3 * entries // LANE, LANE), I32))
        + (edge, edge, message, message, shape((aux_rows, LANE), F32)),
        inputs,
        scratch=bring(inputs),
        specs=[hbm] * len(inputs),
        limit=FULL_VMEM,
    )
    arrived = lax.all_to_all(
        request.reshape(owners, SUBL, LANE), ring, split_axis=0, concat_axis=0, tiled=True
    ).reshape(request.shape)
    def exchange(x, axes, count, first):
        pairs = [(i, i + 1) for i in range(first, count - 1, 2)]
        return lax.ppermute(x, axes, pairs + [(b, a) for a, b in pairs])

    near_a = exchange(to_near_a, ring, owners, 0)
    near_b = exchange(to_near_b, ring, owners, 1)
    rows_a = exchange(to_rows_a, "sph", n_sph, 0)
    rows_b = exchange(to_rows_b, "sph", n_sph, 1)

    halo_rows = max(HALO * rows_y // LANE, layers * PAIR // LANE * HALO, SUBL)
    slots, heated = call(
        functools.partial(surface_kernel, cap, owners, track, grid_y, n_sph, n_fv),
        (shape((owners * (halo_rows + 1), LANE), F32), top),
        (arrived, aux),
    )
    slots, near_a, near_b = lax.optimization_barrier((slots, near_a, near_b))
    got = lax.all_to_all(slots.reshape(owners, -1), ring, split_axis=0, concat_axis=0, tiled=True)
    got = got.reshape(slots.shape)
    wide_j = pltpu.VMEM((3 * blocks_here + 1, SUBL, per_block), F32)
    wide_i = pltpu.VMEM((particles, LANE), F32)
    heat = call(
        functools.partial(pair_kernel, n_fv),
        shape((particles // LANE, LANE), F32),
        (nbr_blocks, nbr_count, to_near_a, near_a, near_b),
        scratch=(
            pltpu.VMEM((particles, 6 * SUBL), BF16),
            pltpu.VMEM((3 * blocks_here + 1, 6 * SUBL, per_block), BF16),
            wide_i, wide_i, wide_j, wide_j, wide_i,
        ),
        specs=[smem, smem] + [vmem] * 3,
        cost=pl.CostEstimate(
            flops=160 * blocks_here * per_block * per_block, bytes_accessed=1 << 20,
            transcendentals=1 << 22,
        ),
    )
    slabs = LANE // (rows_x + 2 * HALO)
    deep = (layers + slabs - 1) // slabs
    ext = (rows_y + 3 * SUBL, LANE)
    cube = pltpu.VMEM((deep,) + ext, F32)
    some = pltpu.VMEM((3,) + ext, F32)
    flat = pltpu.VMEM(ext, F32)
    particle_out, field = call(
        functools.partial(finish_kernel, cap, n_sph, n_fv),
        (shape((particles // LANE, LANE), F32), shape(substrate_temp.shape, F32)),
        (substrate_temp, conduct, heated, rows_a, rows_b, near_a, near_b, got, heat, to_near_a, ints),
        scratch=(cube, cube, cube, some, some, some, flat, flat),
    )
    return (particle_out.reshape(particles), field)


def solution(mesh):
    in_specs = (
        P(None, ("sph", "fv")),
        P(("sph", "fv")),
        P(("sph", "fv")),
        P(("sph", "fv"), None),
        P(("sph", "fv")),
        P(("sph", "fv")),
        P(("sph", "fv"), None),
        P(("sph", "fv")),
        P(None, "sph", "fv"),
        P(None, "sph", "fv"),
        P(),
        P(),
    )
    out_specs = (P(("sph", "fv")), P(None, "sph", "fv"))
    return jax.shard_map(body, mesh=mesh, in_specs=in_specs, out_specs=out_specs, check_vma=False)
```

```python
import functools

import jax
import jax.numpy as jnp
from jax import lax
from jax.experimental import pallas as pl
from jax.experimental.pallas import tpu as pltpu
from jax.sharding import PartitionSpec as P

SUB = 4
KERNEL_SCALE = 0.5
SPH_STEP = 0.05
CONTACT_GAIN = 1.0
PARTICLE_SHARE = 0.5
SURFACE_GAIN = 0.5
LAMBDA_STEP = 0.1

F32 = jnp.float32
BF16 = jnp.bfloat16
I32 = jnp.int32
LANE = 128
SUBL = 8
HALO = SUB
PAIR = 2 * HALO
LOG2E = 1.4426950408889634
VMEM_LIMIT = 48 * 1024 * 1024
FULL_VMEM = 63 * 1024 * 1024


def split3(x):
    high = x.astype(BF16).astype(F32)
    rest = x - high
    mid = rest.astype(BF16).astype(F32)
    low = (rest - mid).astype(BF16).astype(F32)
    return high, mid, low


def wide(rows):
    return jnp.concatenate([rows[i : i + 1] for i in range(rows.shape[0])], axis=1)


def tall(row):
    return jnp.concatenate(
        [row[:, i * LANE : (i + 1) * LANE] for i in range(row.shape[1] // LANE)], axis=0
    )


def iota(shape, dim):
    return lax.broadcasted_iota(I32, shape, dim)


def rolled(x, shift, axis):
    size = x.shape[axis]
    shift = shift % size
    return x if shift == 0 else pltpu.roll(x, shift, axis)


def lane_next(x):
    n = x.shape[1] // LANE
    turned = [pltpu.roll(x[:, i * LANE : (i + 1) * LANE], LANE - 1, 1) for i in range(n)]
    last = iota((1, LANE), 1) == LANE - 1
    return jnp.concatenate([jnp.where(last, turned[(i + 1) % n], turned[i]) for i in range(n)], axis=1)


def lane_before(x):
    n = x.shape[1] // LANE
    turned = [pltpu.roll(x[:, i * LANE : (i + 1) * LANE], 1, 1) for i in range(n)]
    first = iota((1, LANE), 1) == 0
    return jnp.concatenate([jnp.where(first, turned[i - 1], turned[i]) for i in range(n)], axis=1)


def dot_nn(a, b):
    return lax.dot_general(a, b, (((1,), (0,)), ((), ())), preferred_element_type=F32)


def dot_nt(a, b):
    return lax.dot_general(a, b, (((1,), (1,)), ((), ())), preferred_element_type=F32)


def hits(number_row, count):
    return iota((count, number_row.shape[1]), 0) == number_row


def chosen(mask, row):
    return jnp.where(mask, row, 0.0).astype(BF16)


def own_place(n_fv):
    return lax.axis_index("sph") * n_fv + lax.axis_index("fv")


def arrive(refs, count):
    hbm, outs, bufs, sems = refs[:count], refs[count : -count - 1], refs[-count - 1 : -1], refs[-1]
    copies = [pltpu.make_async_copy(a, b, sems.at[i]) for i, (a, b) in enumerate(zip(hbm, bufs))]
    for copy in copies:
        copy.start()
    return outs, bufs, copies


def prep_kernel(cap, owners, n_fv, *refs):
    outs, bufs, copies = arrive(refs, 10)
    request, ints, rows_a, rows_b, near_a, near_b, aux = outs
    even = own_place(n_fv) % 2 == 0
    even_row = lax.axis_index("sph") % 2 == 0
    part, owner, cell, temp2d, cells_in, power_in, pos, vol, u, c = bufs
    layers, rows_x, rows_y = u.shape
    lane = iota((1, LANE), 1)
    for copy in copies[:8]:
        copy.wait()
    temp = wide(temp2d[...])
    part_row, owner_row, cell_row = wide(part[...]), wide(owner[...]), wide(cell[...])
    entries = part_row.shape[1]
    t_rows = temp2d.shape[0]
    own_hit = hits(owner_row, owners)
    own_f = jnp.where(own_hit, 1.0, 0.0).astype(F32)
    upper = jnp.where(iota((LANE, LANE), 0) <= iota((LANE, LANE), 1), 1.0, 0.0).astype(BF16)
    tiles = entries // LANE
    stacked = jnp.concatenate([own_f[:, i * LANE : (i + 1) * LANE] for i in range(tiles)], axis=0)
    within = dot_nn(stacked.astype(BF16), upper)
    before = jnp.full((owners, 1), -1.0, F32)
    ranks = []
    for i in range(tiles):
        here = within[i * owners : (i + 1) * owners]
        ranks.append(
            jnp.sum(own_f[:, i * LANE : (i + 1) * LANE] * (here + before), axis=0, keepdims=True)
        )
        before = before + here[:, LANE - 1 : LANE]
    rank_row = jnp.concatenate(ranks, axis=1).astype(I32)
    ints[...] = jnp.concatenate([part[...], owner[...], tall(rank_row)], axis=0)
    temp_t = jnp.transpose(jnp.concatenate(split3(temp2d[...]), axis=0)).astype(BF16)
    high_hit = jnp.where(hits(part_row // LANE, t_rows), 1.0, 0.0).astype(F32)
    candidates = dot_nn(temp_t, jnp.concatenate([high_hit] * 3, axis=0).astype(BF16))
    own_temp = jnp.sum(
        jnp.where(hits(part_row % LANE, LANE), candidates, 0.0), axis=0, keepdims=True
    )
    t_h, t_m, t_l = split3(own_temp)
    left = jnp.concatenate(
        [
            jnp.where(own_hit, row, 0.0)
            for row in ((cell_row // 64).astype(F32), (cell_row % 64).astype(F32), t_h, t_m, t_l)
        ]
        + [own_f],
        axis=0,
    ).astype(BF16)
    right = jnp.where(hits(rank_row, LANE), 1.0, 0.0).astype(BF16)
    out = dot_nt(left, right)
    piece = [out[i * owners : (i + 1) * owners] for i in range(6)]
    cells = piece[0] * 64.0 + piece[1] + (piece[5] - 1.0)
    temps = piece[2] + piece[3] + piece[4]
    rows = jnp.where(lane < cap, cells, rolled(temps, cap, 1))
    request[...] = jnp.zeros(request.shape, F32)
    for i in range(owners):
        request[i * SUBL : i * SUBL + 1, :] = rows[i : i + 1]
    for copy in copies[8:]:
        copy.wait()
    top = by_tiles(u[0])
    track = cells_in.shape[0]
    corners = top.shape[0]
    aux[:corners, :] = top
    tracks = corners + 4 * SUBL
    aux[tracks : tracks + track, :] = cells_in[...].astype(F32)
    aux[tracks + track : tracks + 2 * track, :] = power_in[...]
    for z in range(layers):
        top_u, top_c = u[z, 0:SUBL, :], c[z, 0:SUBL, :]
        end_u, end_c = u[z, rows_x - SUBL :, :], c[z, rows_x - SUBL :, :]
        first = iota((SUBL, rows_y), 0) < HALO
        to_n = jnp.where(first, top_u, rolled(top_c, HALO, 0))
        to_s = jnp.where(first, rolled(end_c, HALO, 0), end_u)
        rows_a[z] = jnp.where(even_row, to_s, to_n)
        rows_b[z] = jnp.where(even_row, to_n, to_s)
    per = LANE // PAIR
    row_tiles = rows_x // SUBL
    low = lane % PAIR < HALO
    particles = temp.shape[1]
    for g in range(layers // per):
        for t in range(row_tiles):
            rows = slice(t * SUBL, (t + 1) * SUBL)
            acc_u = jnp.zeros((SUBL, LANE), F32)
            acc_c = jnp.zeros((SUBL, LANE), F32)
            for k in range(per):
                z = g * per + k
                place = (lane + HALO - PAIR * k) % LANE < PAIR
                edge_u = jnp.where(lane < LANE // 2, u[z, rows, 0:LANE], u[z, rows, rows_y - LANE :])
                edge_c = jnp.where(lane < LANE // 2, c[z, rows, 0:LANE], c[z, rows, rows_y - LANE :])
                acc_u = jnp.where(place, rolled(edge_u, PAIR * k, 1), acc_u)
                acc_c = jnp.where(place, rolled(edge_c, PAIR * k, 1), acc_c)
            acc_c = rolled(acc_c, HALO, 1)
            at = particles + (g * row_tiles + t) * LANE
            near_a[:, at : at + LANE] = jnp.where(low == even, acc_c, acc_u)
            near_b[:, at : at + LANE] = jnp.where(low == even, acc_u, acc_c)
    at = particles
    for n in range(2):
        for m, (t, rows) in enumerate(
            ((0, slice(0, HALO)), (row_tiles - 1, slice(SUBL - HALO, SUBL)))
        ):
            first = corners + (2 * n + m) * SUBL
            places = [at + (g * row_tiles + t) * LANE for g in range(layers // per)]
            tiles = [
                jnp.where(
                    even == (n == 0), near_b[rows, k : k + LANE], near_a[rows, k : k + LANE]
                )
                for k in places
            ]
            aux[first : first + SUBL, :] = jnp.concatenate(tiles, axis=0)
    rows = jnp.concatenate(
        [pos[...], temp, wide(vol[...]), jnp.zeros((3, particles), F32)], axis=0
    )
    near_a[:, :particles] = rows
    near_b[:, :particles] = rows


def surface_kernel(cap, owners, track, grid_y, n_sph, n_fv, arrived, aux, slots, heated):
    rows_x, rows_y = heated.shape
    highs = rows_x * rows_y // LANE
    corners = aux[highs : highs + 4 * SUBL, :]
    laser = aux[highs + 4 * SUBL : highs + 4 * SUBL + track, :].astype(I32)
    laser_power = aux[highs + 4 * SUBL + track :, :]
    slot_rows = slots.shape[0] // owners
    lane = iota((1, LANE), 1)
    s, f = lax.axis_index("sph"), lax.axis_index("fv")
    fold = LANE // cap
    group = owners // fold
    full = jnp.concatenate([arrived[i * SUBL : i * SUBL + 1, :] for i in range(owners)], axis=0)
    cells = jnp.zeros((group, LANE), F32)
    temps = jnp.zeros((group, LANE), F32)
    for g in range(fold):
        rows = full[g * group : (g + 1) * group]
        place = (lane >= g * cap) & (lane < (g + 1) * cap)
        cells = jnp.where(place, rolled(rows, g * cap, 1), cells)
        temps = jnp.where(place, rolled(rows, (g - 1) * cap, 1), temps)
    cells = cells.astype(I32)
    used = cells >= 0
    y_tiles = rows_y // LANE
    cell_x, cell_y = cells // rows_y, cells % rows_y
    high = jnp.where(used, (cell_y // LANE) * rows_x + cell_x, -1)
    low = jnp.where(used, cell_y % LANE, -1)
    laser_x = laser // grid_y - s * rows_x
    laser_y = laser % grid_y - f * rows_y
    mine = (laser_x >= 0) & (laser_x < rows_x) & (laser_y >= 0) & (laser_y < rows_y)
    l_high = jnp.where(mine, (laser_y // LANE) * rows_x + laser_x, -1)
    l_low = jnp.where(mine, laser_y % LANE, -1)
    tall_surface = aux[:highs, :]
    here = jnp.concatenate(
        [tall_surface[i * rows_x : (i + 1) * rows_x] for i in range(y_tiles)], axis=1
    )
    surf_t = jnp.transpose(jnp.concatenate(split3(tall_surface), axis=0)).astype(BF16)
    flux = jnp.zeros((3 * highs, LANE), F32)
    contact_rows = []
    step = 2
    for p in range(0, group, step):
        hit_h = hits(wide(high[p : p + step]), highs)
        hit_l = hits(wide(low[p : p + step]), LANE)
        one = jnp.where(hit_h, 1.0, 0.0).astype(BF16)
        candidates = dot_nn(surf_t, jnp.concatenate([one] * 3, axis=0))
        ghost = jnp.sum(jnp.where(hit_l, candidates, 0.0), axis=0, keepdims=True)
        contact = jnp.where(
            wide(high[p : p + step]) >= 0, CONTACT_GAIN * (wide(temps[p : p + step]) - ghost), 0.0
        )
        contact_rows.append(contact)
        left = jnp.concatenate([chosen(hit_h, part) for part in split3(contact)], axis=0)
        flux = flux + dot_nt(left, jnp.where(hit_l, 1.0, 0.0).astype(BF16))
    hit_h, hit_l = hits(wide(l_high), highs), hits(wide(l_low), LANE)
    left = jnp.concatenate([chosen(hit_h, part) for part in split3(wide(laser_power))], axis=0)
    flux = flux + dot_nt(left, jnp.where(hit_l, 1.0, 0.0).astype(BF16))
    flux = flux[:highs] + flux[highs : 2 * highs] + flux[2 * highs :]
    flux = jnp.concatenate([flux[i * rows_x : (i + 1) * rows_x] for i in range(y_tiles)], axis=1)
    hot = here + SURFACE_GAIN * flux
    heated[...] = hot
    contact = tall(jnp.concatenate(contact_rows, axis=1))
    slots[...] = jnp.zeros(slots.shape, F32)
    for g in range(fold):
        back = rolled(contact, -g * cap, 1)
        for i in range(group):
            at = (g * group + i + 1) * slot_rows - 1
            slots[at : at + 1, :] = back[i : i + 1]

    def send(ds, df, rows):
        ok = (s + ds >= 0) & (s + ds < n_sph) & (f + df >= 0) & (f + df < n_fv)

        @pl.when(ok)
        def _():
            at = ((s + ds) * n_fv + f + df) * slot_rows
            for i in range(rows.shape[0]):
                slots[pl.ds(at + i, 1), :] = rows[i : i + 1]

    send(-1, 0, by_tiles(hot[:HALO]))
    send(1, 0, by_tiles(hot[rows_x - HALO :]))
    row_tiles = rows_x // SUBL
    west = jnp.zeros((SUBL, LANE), F32)
    east = jnp.zeros((SUBL, LANE), F32)
    for t in range(row_tiles):
        rows = slice(t * SUBL, (t + 1) * SUBL)
        place = (lane >= t * HALO) & (lane < (t + 1) * HALO)
        west = jnp.where(place, rolled(hot[rows, 0:LANE], t * HALO, 1), west)
        east = jnp.where(place, rolled(hot[rows, rows_y - LANE :], (t + 1) * HALO, 1), east)
    send(0, -1, west)
    send(0, 1, east)
    sub = iota((SUBL, LANE), 0)
    for n, (df, tile, mark) in enumerate(
        ((-1, hot[:, 0:LANE], lane < HALO), (1, hot[:, rows_y - LANE :], lane >= LANE - HALO))
    ):
        for m, ds in enumerate((-1, 1)):
            static = corners[(2 * n + m) * SUBL : (2 * n + m + 1) * SUBL]
            end = tile[:SUBL] if ds < 0 else rolled(tile[rows_x - SUBL :], HALO, 0)
            send(ds, df, jnp.where(mark & (sub < HALO), end, static))


def by_tiles(x):
    return jnp.concatenate(
        [x[:, i * LANE : (i + 1) * LANE] for i in range(x.shape[1] // LANE)], axis=0
    )


def pair_kernel(n_fv, nbr, count, own, got_a, got_b, heat, left, right, inv_i, temp_i,
                inv_j, temp_j, accs):
    blocks, slots = nbr.shape
    particles = accs.shape[0]
    per = particles // blocks
    halves = per // LANE
    device = own_place(n_fv)
    even = device % 2 == 0
    row = iota((SUBL, particles), 0)
    for at in range(3):
        if at == 1:
            rows = own[:, :particles]
        else:
            rows = jnp.where(even == (at == 0), got_b[:, :particles], got_a[:, :particles])
        xyz = jnp.where(row < 3, rows, 0.0)
        norm = jnp.sum(xyz * xyz, axis=0, keepdims=True) * (-KERNEL_SCALE * LOG2E)
        t_row, v_row = rows[3:4], rows[4:5]
        inv = 1.0 / (1.0 + 0.5 * jnp.tanh(t_row))
        weight = jnp.log2(jnp.where(v_row > 0.0, v_row, 1.0) * (4.0 * KERNEL_SCALE))
        h, m, l = split3(jnp.where(row == 3, norm + weight, jnp.where(row == 4, 1.0, xyz)))
        j_side = jnp.concatenate([h, h, m, h, l, m], axis=0).astype(BF16)
        inv_rows = jnp.broadcast_to(inv, (SUBL, particles))
        temp_rows = jnp.broadcast_to(t_row, (SUBL, particles))
        for b in range(blocks):
            cols = slice(b * per, (b + 1) * per)
            right[at * blocks + b] = j_side[:, cols]
            inv_j[at * blocks + b] = inv_rows[:, cols]
            temp_j[at * blocks + b] = temp_rows[:, cols]
        if at == 1:
            scaled = xyz * (2 * KERNEL_SCALE * LOG2E)
            h, m, l = split3(jnp.where(row == 3, 1.0, jnp.where(row == 4, norm, scaled)))
            extra = jnp.where(row == 0, inv, jnp.where(row == 1, t_row, 0.0))
            turned = jnp.transpose(jnp.concatenate([h, m, h, l, h, m, extra, extra], axis=0))
            left[...] = turned[:, : 6 * SUBL].astype(BF16)
            inv_i[...] = jnp.broadcast_to(turned[:, 6 * SUBL : 6 * SUBL + 1], (particles, LANE))
            temp_i[...] = jnp.broadcast_to(turned[:, 6 * SUBL + 1 : 6 * SUBL + 2], (particles, LANE))
    nothing = 3 * blocks
    k_row = iota((6 * SUBL, per), 0)
    right[nothing] = jnp.where(k_row == 3, -16384.0, 0.0).astype(BF16)
    inv_j[nothing] = jnp.ones((SUBL, per), F32)
    temp_j[nothing] = jnp.zeros((SUBL, per), F32)
    accs[...] = jnp.zeros(accs.shape, F32)
    together = 4

    def one_block(b, carry):
        live = count[b]
        i0 = pl.multiple_of(b * per, per)

        def some_slots(n, carry):
            who = []
            for q in range(together):
                at = n * together + q
                local = nbr[b, jnp.minimum(at, slots - 1)] - (device - 1) * blocks
                who.append(jnp.where(at < live, local, nothing))
            exponents = [dot_nn(left[pl.ds(i0, per), :], right[k]) for k in who]
            invs = [[inv_j[k, :, i * LANE : (i + 1) * LANE] for i in range(halves)] for k in who]
            temps = [[temp_j[k, :, i * LANE : (i + 1) * LANE] for i in range(halves)] for k in who]
            for r in range(per // SUBL):
                here = pl.ds(i0 + r * SUBL, SUBL)
                own_inv, own_temp = inv_i[here, :], temp_i[here, :]
                acc = accs[here, :]
                for q in range(together):
                    for i in range(halves):
                        part = exponents[q][r * SUBL : (r + 1) * SUBL, i * LANE : (i + 1) * LANE]
                        kernel = jnp.exp2(part) * pl.reciprocal(invs[q][i] + own_inv, approx=True)
                        acc = acc + kernel * (temps[q][i] - own_temp)
                accs[here, :] = acc
            return carry

        return lax.fori_loop(0, (live + together - 1) // together, some_slots, carry)

    lax.fori_loop(0, blocks, one_block, 0)
    for n in range(particles // LANE):
        turned = jnp.transpose(accs[n * LANE : (n + 1) * LANE, :])
        heat[n : n + 1, :] = jnp.sum(turned, axis=0, keepdims=True)


def finish_kernel(cap, n_sph, n_fv, u, c, heated, rows_a, rows_b, near_a, near_b, got,
                  heat, own, ints, particle_out, u_out, field, other, coef, coef_side, cond, row_flux, lane_flux, down, wrap):
    layers, rows_x, rows_y = u.shape
    owners = n_sph * n_fv
    slot_rows = got.shape[0] // owners
    s, f = lax.axis_index("sph"), lax.axis_index("fv")
    lane = iota((1, LANE), 1)
    row_tiles = rows_x // SUBL
    per = LANE // PAIR
    groups = layers // per
    scale = LAMBDA_STEP * 0.5 * 0.5

    def slot(ds, df):
        at = jnp.clip(s + ds, 0, n_sph - 1) * n_fv + jnp.clip(f + df, 0, n_fv - 1)
        return jnp.concatenate(
            [got[pl.ds(at * slot_rows + i, 1), :] for i in range(slot_rows - 1)], axis=0
        )

    def flag(ok):
        return jnp.where(ok, 1.0, 0.0).astype(F32)

    has_n, has_s = flag(s > 0), flag(s < n_sph - 1)
    has_w, has_e = flag(f > 0), flag(f < n_fv - 1)
    third = ints.shape[0] // 3
    part_row, owner_row, rank_row = (wide(ints[i * third : (i + 1) * third]) for i in range(3))
    back = jnp.concatenate(
        [got[(i + 1) * slot_rows - 1 : (i + 1) * slot_rows, :] for i in range(owners)], axis=0
    )
    temp2d = tall(own[3:4, : heat.shape[0] * LANE])
    back_t = jnp.transpose(jnp.concatenate(split3(back), axis=0)).astype(BF16)
    own_one = jnp.where(hits(owner_row, owners), 1.0, 0.0).astype(BF16)
    candidates = dot_nn(back_t, jnp.concatenate([own_one] * 3, axis=0))
    contact = jnp.sum(jnp.where(hits(rank_row, LANE), candidates, 0.0), axis=0, keepdims=True)
    t_rows = temp2d.shape[0]
    hit_h = hits(part_row // LANE, t_rows)
    lefts = jnp.concatenate([jnp.where(hit_h, p, 0.0) for p in split3(contact)], axis=0).astype(BF16)
    flux = dot_nt(lefts, jnp.where(hits(part_row % LANE, LANE), 1.0, 0.0).astype(BF16))
    flux = flux[:t_rows] + flux[t_rows : 2 * t_rows] + flux[2 * t_rows :]
    particle_out[...] = temp2d + SPH_STEP * heat[...] - PARTICLE_SHARE * flux

    slab = rows_x + 2 * HALO
    slabs = LANE // slab
    deep = (layers + slabs - 1) // slabs
    assert slabs * deep == layers + 1 and SUB % 2 == 0
    place = (lane + HALO) % LANE
    spot = place % slab
    in_group = place < slabs * slab
    sides = jnp.where(spot < HALO, has_n, jnp.where(spot < HALO + rows_x, 1.0, has_s))
    lane_mask = jnp.where(in_group, sides, 0.0)
    last_group = in_group & (place >= (slabs - 1) * slab)
    end_mask = jnp.where(last_group, 0.0, lane_mask)
    not_first = jnp.where(place >= slab, 1.0, 0.0)
    sub_first = iota((SUBL, 1), 0) < HALO

    even, even_row = own_place(n_fv) % 2 == 0, s % 2 == 0
    low = lane % PAIR < HALO
    start = near_a.shape[1] - groups * row_tiles * LANE
    corner_e = [slot(ds, 1) for ds in (1, -1)]
    corner_w = [slot(ds, -1) for ds in (1, -1)]
    east_0, west_0 = slot(0, 1)[:SUBL], slot(0, -1)[:SUBL]
    empty = jnp.zeros((LANE - rows_x - 2 * SUBL, LANE), F32)
    turned_u, turned_c = [], []
    for g in range(groups):
        tiles_u, tiles_c = [], []
        for t in range(row_tiles + 1):
            if t < row_tiles:
                at = start + (g * row_tiles + t) * LANE
                a, b = near_a[:, at : at + LANE], near_b[:, at : at + LANE]
                east, west = jnp.where(even, a, b), jnp.where(even, b, a)
            else:
                rows = slice(g * HALO, (g + 1) * HALO)
                east = jnp.concatenate([k[rows] for k in corner_e], axis=0)
                west = jnp.concatenate([k[rows] for k in corner_w], axis=0)
            tile = jnp.where(low, east, west)
            if g == 0 and t < row_tiles:
                tile = jnp.where(lane < HALO, rolled(east_0, -t * HALO, 1), tile)
                tile = jnp.where(lane >= LANE - HALO, rolled(west_0, -HALO - t * HALO, 1), tile)
            tiles_u.append(tile)
            tiles_c.append(jnp.where(low, west, east))
        for tiles, turned in ((tiles_u, turned_u), (tiles_c, turned_c)):
            ends = tiles.pop()
            tiles += [jnp.where(sub_first, ends, 0.0), empty, jnp.where(sub_first, 0.0, ends)]
            turned.append(jnp.transpose(jnp.concatenate(tiles, axis=0)))

    south, north = slot(1, 0), slot(-1, 0)
    ends_0 = jnp.concatenate(
        [
            jnp.concatenate([k[i * HALO : (i + 1) * HALO] for k in (south, north)], axis=0)
            for i in range(rows_y // LANE)
        ],
        axis=1,
    )
    nothing = jnp.zeros((SUBL, rows_y), F32)

    def side_tile(after, before, is_u):
        ok_after, ok_before = after is not None and after < layers, before is not None and before < layers
        a = b = nothing
        if ok_after:
            if is_u and after == 0:
                a = ends_0
            else:
                a = jnp.where(even_row, rows_a[after], rows_b[after])
        if ok_before:
            if is_u and before == 0:
                b = ends_0
            else:
                b = jnp.where(even_row, rows_b[before], rows_a[before])
        return jnp.where(sub_first, a, b) if is_u else rolled(jnp.where(sub_first, b, a), HALO, 0)

    first_row, tiles_y = SUBL, rows_y // SUBL + 2
    for i in range(deep):
        mask = lane_mask if i < deep - 1 else end_mask
        zs = [n * deep + i for n in range(slabs)]
        for is_u, ref, array, factor in ((True, field, u, mask), (False, coef, c, mask * scale)):
            rows = []
            for n, z in enumerate(zs):
                if z >= layers:
                    rows.append(jnp.zeros((rows_x, rows_y), F32))
                else:
                    rows.append(heated[...] if is_u and z == 0 else array[z])
                rows.append(side_tile(z, zs[n + 1] if n + 1 < slabs else None, is_u))
            if slabs * slab < LANE:
                rows.append(side_tile(None, zs[0], is_u))
            rows = jnp.concatenate(rows, axis=0)
            for b in range(rows_y // LANE):
                block = jnp.transpose(rows[:, b * LANE : (b + 1) * LANE])
                ref[i, first_row + b * LANE : first_row + (b + 1) * LANE, :] = block * factor
            before, after = jnp.zeros((SUBL, LANE), F32), jnp.zeros((SUBL, LANE), F32)
            for n, z in enumerate(zs):
                if z >= layers:
                    continue
                g, k = z // per, z % per
                if is_u:
                    e_at, w_at = k * PAIR, (k - 1) % per * PAIR
                    tile_e, tile_w = turned_u[g][e_at : e_at + PAIR], turned_u[g][w_at : w_at + PAIR]
                    after = after + rolled(tile_e, n * slab, 1)
                    before = before + rolled(tile_w, n * slab, 1)
                else:
                    tile = rolled(turned_c[g][k * PAIR : (k + 1) * PAIR], HALO, 0)
                    after = after + rolled(tile, n * slab, 1)
                    before = after
            ref[i, 0:SUBL, :] = before * (factor * has_w)
            ref[i, (tiles_y - 1) * SUBL : tiles_y * SUBL, :] = after * (factor * has_e)
            ref[i, tiles_y * SUBL :, :] = jnp.zeros((SUBL, LANE), F32)
        other[i, tiles_y * SUBL :, :] = jnp.zeros((SUBL, LANE), F32)
    cond[:, tiles_y * SUBL :, :] = jnp.zeros((cond.shape[0], SUBL, LANE), F32)
    row_flux[:, :SUBL, :] = jnp.zeros((row_flux.shape[0], SUBL, LANE), F32)

    for i in range(deep):
        for t in range(tiles_y):
            rows = slice(t * SUBL, (t + 1) * SUBL)
            coef_side[i, rows, :] = pltpu.roll(coef[i, rows, :], LANE - 1, 1)

    def rows_of(t):
        return slice(t * SUBL, (t + 1) * SUBL)

    def some_layers(i0, count, source, target, end):
        def conductivity(n, t):
            return coef[i0 + n, rows_of(t), :] * (2.0 + jnp.tanh(source[i0 + n, rows_of(t), :]))

        tiles = range(tiles_y)
        spots = [(t, n) for t in tiles for n in range(count)]
        for t, n in spots:
            cond[n, rows_of(t), :] = conductivity(n, t)
        for t, n in spots:
            here, here_k = source[i0 + n, rows_of(t), :], cond[n, rows_of(t), :]
            side = pltpu.roll(here, LANE - 1, 1)
            side_k = coef_side[i0 + n, rows_of(t), :] * (2.0 + jnp.tanh(side))
            lane_flux[n, rows_of(t), :] = (here_k + side_k) * (side - here)
        for t, n in spots:
            here, here_k = source[i0 + n, rows_of(t), :], cond[n, rows_of(t), :]
            next_row = slice(t * SUBL + 1, (t + 1) * SUBL + 1)
            row_flux[n, rows_of(t + 1), :] = (here_k + cond[n, next_row, :]) * (
                source[i0 + n, next_row, :] - here
            )
        for t in tiles:
            above = down[rows_of(t), :]
            here, here_k = source[i0, rows_of(t), :], cond[0, rows_of(t), :]
            for n in range(count):
                i = i0 + n
                wraps = end and n == count - 1
                if wraps:
                    flux_z = wrap[rows_of(t), :]
                else:
                    below = source[i + 1, rows_of(t), :]
                    below_k = conductivity(n + 1, t) if n + 1 == count else cond[n + 1, rows_of(t), :]
                    beside_k = below_k
                    if end and n == count - 2:
                        beside_k = jnp.where(last_group, here_k, below_k)
                    flux_z = (here_k + beside_k) * (below - here)
                from_y = row_flux[n, rows_of(t + 1), :] - row_flux[n, (t + 1) * SUBL - 1 : (t + 2) * SUBL - 1, :]
                flux_x = lane_flux[n, rows_of(t), :]
                from_x = flux_x - pltpu.roll(flux_x, 1, 1)
                new = here + ((from_x + from_y) + (flux_z - above))
                factor = end_mask if wraps else lane_mask
                if t == 0:
                    factor = factor * has_w
                if t == tiles_y - 1:
                    factor = factor * has_e
                target[i, rows_of(t), :] = new * factor
                above = flux_z
                if not wraps:
                    here, here_k = below, below_k
            if not end:
                down[rows_of(t), :] = above

    def substep(source, target):
        for t in range(tiles_y):
            last_u, first_u = source[deep - 1, rows_of(t), :], source[0, rows_of(t), :]
            last_k = coef[deep - 1, rows_of(t), :] * (2.0 + jnp.tanh(last_u))
            first_k = coef[0, rows_of(t), :] * (2.0 + jnp.tanh(first_u))
            flux = (first_k + pltpu.roll(last_k, slab, 1)) * (first_u - pltpu.roll(last_u, slab, 1))
            flux = flux * not_first
            down[rows_of(t), :] = flux
            wrap[rows_of(t), :] = pltpu.roll(flux, LANE - slab, 1)
        together = cond.shape[0]

        def step(n, carry):
            some_layers(n * together, together, source, target, False)
            return carry

        full = (deep - 2) // together
        lax.fori_loop(0, full, step, 0)
        some_layers(full * together, deep - full * together, source, target, True)

    def two_substeps(n, carry):
        substep(field, other)
        substep(other, field)
        return carry

    lax.fori_loop(0, SUB // 2, two_substeps, 0)
    for i in range(deep):
        rows = jnp.concatenate(
            [
                jnp.transpose(field[i, first_row + b * LANE : first_row + (b + 1) * LANE, :])
                for b in range(rows_y // LANE)
            ],
            axis=1,
        )
        for n in range(slabs):
            z = n * deep + i
            if z < layers:
                u_out[z] = rows[n * slab : n * slab + rows_x]


def call(kernel, outs, ins, scratch=(), specs=None, cost=None, limit=VMEM_LIMIT):
    vmem = pl.BlockSpec(memory_space=pltpu.VMEM)
    return pl.pallas_call(
        kernel,
        out_shape=outs,
        in_specs=specs or [vmem] * len(ins),
        out_specs=jax.tree.map(lambda _: vmem, outs),
        scratch_shapes=list(scratch),
        compiler_params=pltpu.CompilerParams(vmem_limit_bytes=limit),
        cost_estimate=cost,
    )(*ins)


def body(
    positions,
    particle_temp,
    volume,
    nbr_blocks,
    nbr_count,
    iface_part,
    iface_owner,
    iface_cell,
    substrate_temp,
    conduct,
    laser_cells,
    laser_power,
):
    blocks_here = nbr_count.shape[0]
    particles = particle_temp.shape[0]
    per_block = particles // blocks_here
    layers, rows_x, rows_y = substrate_temp.shape
    n_sph, n_fv = lax.axis_size("sph"), lax.axis_size("fv")
    owners = n_sph * n_fv
    entries = iface_part.shape[0]
    cap = max(2, (2 * entries + owners - 1) // owners)
    grid_y = rows_y * n_fv
    ring = ("sph", "fv")
    shape = jax.ShapeDtypeStruct

    def as_tiles(x):
        return x.reshape(-1, LANE)

    strip = rows_x * layers * PAIR // SUBL
    message = shape((SUBL, particles + strip), F32)
    edge = shape((layers, SUBL, rows_y), F32)
    hbm = pl.BlockSpec(memory_space=pltpu.HBM)
    vmem = pl.BlockSpec(memory_space=pltpu.VMEM)
    smem = pl.BlockSpec(memory_space=pltpu.SMEM)
    temp2d, lasers = as_tiles(particle_temp), (as_tiles(laser_cells), as_tiles(laser_power))

    def bring(inputs):
        return [pltpu.VMEM(x.shape, x.dtype) for x in inputs] + [pltpu.SemaphoreType.DMA((len(inputs),))]

    inputs = (as_tiles(iface_part), as_tiles(iface_owner), as_tiles(iface_cell), temp2d) + lasers
    inputs += (positions, as_tiles(volume), substrate_temp, conduct)
    top = shape((rows_x, rows_y), F32)
    track = lasers[0].shape[0]
    aux_rows = rows_x * rows_y // LANE + 4 * SUBL + 2 * track
    request, ints, to_rows_a, to_rows_b, to_near_a, to_near_b, aux = call(
        functools.partial(prep_kernel, cap, owners, n_fv),
        (shape((owners * SUBL, LANE), F32), shape((3 * entries // LANE, LANE), I32))
        + (edge, edge, message, message, shape((aux_rows, LANE), F32)),
        inputs,
        scratch=bring(inputs),
        specs=[hbm] * len(inputs),
        limit=FULL_VMEM,
    )
    arrived = lax.all_to_all(
        request.reshape(owners, SUBL, LANE), ring, split_axis=0, concat_axis=0, tiled=True
    ).reshape(request.shape)
    def exchange(x, axes, count, first):
        pairs = [(i, i + 1) for i in range(first, count - 1, 2)]
        return lax.ppermute(x, axes, pairs + [(b, a) for a, b in pairs])

    near_a = exchange(to_near_a, ring, owners, 0)
    near_b = exchange(to_near_b, ring, owners, 1)
    to_rows_a, to_rows_b, near_a, near_b = lax.optimization_barrier(
        (to_rows_a, to_rows_b, near_a, near_b)
    )
    rows_a = exchange(to_rows_a, "sph", n_sph, 0)
    rows_b = exchange(to_rows_b, "sph", n_sph, 1)

    halo_rows = max(HALO * rows_y // LANE, layers * PAIR // LANE * HALO, SUBL)
    slots, heated = call(
        functools.partial(surface_kernel, cap, owners, track, grid_y, n_sph, n_fv),
        (shape((owners * (halo_rows + 1), LANE), F32), top),
        (arrived, aux),
    )
    got = lax.all_to_all(slots.reshape(owners, -1), ring, split_axis=0, concat_axis=0, tiled=True)
    got = got.reshape(slots.shape)
    wide_j = pltpu.VMEM((3 * blocks_here + 1, SUBL, per_block), F32)
    wide_i = pltpu.VMEM((particles, LANE), F32)
    heat = call(
        functools.partial(pair_kernel, n_fv),
        shape((particles // LANE, LANE), F32),
        (nbr_blocks, nbr_count, to_near_a, near_a, near_b),
        scratch=(
            pltpu.VMEM((particles, 6 * SUBL), BF16),
            pltpu.VMEM((3 * blocks_here + 1, 6 * SUBL, per_block), BF16),
            wide_i, wide_i, wide_j, wide_j, wide_i,
        ),
        specs=[smem, smem] + [vmem] * 3,
        cost=pl.CostEstimate(
            flops=160 * blocks_here * per_block * per_block, bytes_accessed=1 << 20,
            transcendentals=1 << 22,
        ),
    )
    slabs = LANE // (rows_x + 2 * HALO)
    deep = (layers + slabs - 1) // slabs
    ext = (rows_y + 3 * SUBL, LANE)
    cube = pltpu.VMEM((deep,) + ext, F32)
    some = pltpu.VMEM((3,) + ext, F32)
    flat = pltpu.VMEM(ext, F32)
    particle_out, field = call(
        functools.partial(finish_kernel, cap, n_sph, n_fv),
        (shape((particles // LANE, LANE), F32), shape(substrate_temp.shape, F32)),
        (substrate_temp, conduct, heated, rows_a, rows_b, near_a, near_b, got, heat, to_near_a, ints),
        scratch=(cube, cube, cube, cube, some, some, some, flat, flat),
    )
    return (particle_out.reshape(particles), field)


def solution(mesh):
    in_specs = (
        P(None, ("sph", "fv")),
        P(("sph", "fv")),
        P(("sph", "fv")),
        P(("sph", "fv"), None),
        P(("sph", "fv")),
        P(("sph", "fv")),
        P(("sph", "fv"), None),
        P(("sph", "fv")),
        P(None, "sph", "fv"),
        P(None, "sph", "fv"),
        P(),
        P(),
    )
    out_specs = (P(("sph", "fv")), P(None, "sph", "fv"))
    return jax.shard_map(body, mesh=mesh, in_specs=in_specs, out_specs=out_specs, check_vma=False)
```

```python
import functools

import jax
import jax.numpy as jnp
from jax import lax
from jax.experimental import pallas as pl
from jax.experimental.pallas import tpu as pltpu
from jax.sharding import PartitionSpec as P

SUB = 4
KERNEL_SCALE = 0.5
SPH_STEP = 0.05
CONTACT_GAIN = 1.0
PARTICLE_SHARE = 0.5
SURFACE_GAIN = 0.5
LAMBDA_STEP = 0.1

F32 = jnp.float32
BF16 = jnp.bfloat16
I32 = jnp.int32
LANE = 128
SUBL = 8
HALO = SUB
PAIR = 2 * HALO
SPREAD = 5
MANY, FEW = 8, 4
LOG2E = 1.4426950408889634
VMEM_LIMIT = 48 * 1024 * 1024
FULL_VMEM = 63 * 1024 * 1024


def split3(x):
    high = x.astype(BF16).astype(F32)
    rest = x - high
    mid = rest.astype(BF16).astype(F32)
    low = (rest - mid).astype(BF16).astype(F32)
    return high, mid, low


def wide(rows):
    return jnp.concatenate([rows[i : i + 1] for i in range(rows.shape[0])], axis=1)


def tall(row):
    return jnp.concatenate(
        [row[:, i * LANE : (i + 1) * LANE] for i in range(row.shape[1] // LANE)], axis=0
    )


def iota(shape, dim):
    return lax.broadcasted_iota(I32, shape, dim)


def rolled(x, shift, axis):
    size = x.shape[axis]
    shift = shift % size
    return x if shift == 0 else pltpu.roll(x, shift, axis)


def lane_next(x):
    n = x.shape[1] // LANE
    turned = [pltpu.roll(x[:, i * LANE : (i + 1) * LANE], LANE - 1, 1) for i in range(n)]
    last = iota((1, LANE), 1) == LANE - 1
    return jnp.concatenate([jnp.where(last, turned[(i + 1) % n], turned[i]) for i in range(n)], axis=1)


def lane_before(x):
    n = x.shape[1] // LANE
    turned = [pltpu.roll(x[:, i * LANE : (i + 1) * LANE], 1, 1) for i in range(n)]
    first = iota((1, LANE), 1) == 0
    return jnp.concatenate([jnp.where(first, turned[i - 1], turned[i]) for i in range(n)], axis=1)


def dot_nn(a, b):
    return lax.dot_general(a, b, (((1,), (0,)), ((), ())), preferred_element_type=F32)


def dot_nt(a, b):
    return lax.dot_general(a, b, (((1,), (1,)), ((), ())), preferred_element_type=F32)


def hits(number_row, count):
    return iota((count, number_row.shape[1]), 0) == number_row


def chosen(mask, row):
    return jnp.where(mask, row, 0.0).astype(BF16)


def own_place(n_fv):
    return lax.axis_index("sph") * n_fv + lax.axis_index("fv")


def arrive(refs, count):
    hbm, outs, bufs, sems = refs[:count], refs[count : -count - 1], refs[-count - 1 : -1], refs[-1]
    copies = [pltpu.make_async_copy(a, b, sems.at[i]) for i, (a, b) in enumerate(zip(hbm, bufs))]
    for copy in copies:
        copy.start()
    return outs, bufs, copies


def prep_kernel(cap, owners, n_fv, *refs):
    outs, bufs, copies = arrive(refs, 10)
    request, ints, rows_a, rows_b, near_a, near_b, aux = outs
    even = own_place(n_fv) % 2 == 0
    even_row = lax.axis_index("sph") % 2 == 0
    part, owner, cell, temp2d, cells_in, power_in, pos, vol, u, c = bufs
    layers, rows_x, rows_y = u.shape
    lane = iota((1, LANE), 1)
    for copy in copies[:8]:
        copy.wait()
    temp = wide(temp2d[...])
    part_row, owner_row, cell_row = wide(part[...]), wide(owner[...]), wide(cell[...])
    entries = part_row.shape[1]
    t_rows = temp2d.shape[0]
    own_hit = hits(owner_row, owners)
    own_f = jnp.where(own_hit, 1.0, 0.0).astype(F32)
    upper = jnp.where(iota((LANE, LANE), 0) <= iota((LANE, LANE), 1), 1.0, 0.0).astype(BF16)
    tiles = entries // LANE
    stacked = jnp.concatenate([own_f[:, i * LANE : (i + 1) * LANE] for i in range(tiles)], axis=0)
    within = dot_nn(stacked.astype(BF16), upper)
    before = jnp.full((owners, 1), -1.0, F32)
    ranks = []
    for i in range(tiles):
        here = within[i * owners : (i + 1) * owners]
        ranks.append(
            jnp.sum(own_f[:, i * LANE : (i + 1) * LANE] * (here + before), axis=0, keepdims=True)
        )
        before = before + here[:, LANE - 1 : LANE]
    rank_row = jnp.concatenate(ranks, axis=1).astype(I32)
    ints[...] = jnp.concatenate([part[...], owner[...], tall(rank_row)], axis=0)
    temp_t = jnp.transpose(jnp.concatenate(split3(temp2d[...]), axis=0)).astype(BF16)
    high_hit = jnp.where(hits(part_row // LANE, t_rows), 1.0, 0.0).astype(F32)
    candidates = dot_nn(temp_t, jnp.concatenate([high_hit] * 3, axis=0).astype(BF16))
    own_temp = jnp.sum(
        jnp.where(hits(part_row % LANE, LANE), candidates, 0.0), axis=0, keepdims=True
    )
    t_h, t_m, t_l = split3(own_temp)
    left = jnp.concatenate(
        [
            jnp.where(own_hit, row, 0.0)
            for row in ((cell_row // 64).astype(F32), (cell_row % 64).astype(F32), t_h, t_m, t_l)
        ]
        + [own_f],
        axis=0,
    ).astype(BF16)
    right = jnp.where(hits(rank_row, LANE), 1.0, 0.0).astype(BF16)
    out = dot_nt(left, right)
    piece = [out[i * owners : (i + 1) * owners] for i in range(6)]
    cells = piece[0] * 64.0 + piece[1] + (piece[5] - 1.0)
    temps = piece[2] + piece[3] + piece[4]
    rows = jnp.where(lane < cap, cells, rolled(temps, cap, 1))
    request[...] = jnp.zeros(request.shape, F32)
    for i in range(owners):
        request[i * SPREAD : i * SPREAD + 1, :] = rows[i : i + 1]
    for copy in copies[8:]:
        copy.wait()
    top = by_tiles(u[0])
    track = cells_in.shape[0]
    corners = top.shape[0]
    aux[:corners, :] = top
    tracks = corners + 4 * SUBL
    aux[tracks : tracks + track, :] = cells_in[...].astype(F32)
    aux[tracks + track : tracks + 2 * track, :] = power_in[...]
    for z in range(layers):
        top_u, top_c = u[z, 0:SUBL, :], c[z, 0:SUBL, :]
        end_u, end_c = u[z, rows_x - SUBL :, :], c[z, rows_x - SUBL :, :]
        first = iota((SUBL, rows_y), 0) < HALO
        to_n = jnp.where(first, top_u, rolled(top_c, HALO, 0))
        to_s = jnp.where(first, rolled(end_c, HALO, 0), end_u)
        rows_a[z] = jnp.where(even_row, to_s, to_n)
        rows_b[z] = jnp.where(even_row, to_n, to_s)
    per = LANE // PAIR
    row_tiles = rows_x // SUBL
    low = lane % PAIR < HALO
    particles = temp.shape[1]
    for g in range(layers // per):
        for t in range(row_tiles):
            rows = slice(t * SUBL, (t + 1) * SUBL)
            acc_u = jnp.zeros((SUBL, LANE), F32)
            acc_c = jnp.zeros((SUBL, LANE), F32)
            for k in range(per):
                z = g * per + k
                place = (lane + HALO - PAIR * k) % LANE < PAIR
                edge_u = jnp.where(lane < LANE // 2, u[z, rows, 0:LANE], u[z, rows, rows_y - LANE :])
                edge_c = jnp.where(lane < LANE // 2, c[z, rows, 0:LANE], c[z, rows, rows_y - LANE :])
                acc_u = jnp.where(place, rolled(edge_u, PAIR * k, 1), acc_u)
                acc_c = jnp.where(place, rolled(edge_c, PAIR * k, 1), acc_c)
            acc_c = rolled(acc_c, HALO, 1)
            at = particles + (g * row_tiles + t) * LANE
            near_a[:, at : at + LANE] = jnp.where(low == even, acc_c, acc_u)
            near_b[:, at : at + LANE] = jnp.where(low == even, acc_u, acc_c)
    at = particles
    for n in range(2):
        for m, (t, rows) in enumerate(
            ((0, slice(0, HALO)), (row_tiles - 1, slice(SUBL - HALO, SUBL)))
        ):
            first = corners + (2 * n + m) * SUBL
            places = [at + (g * row_tiles + t) * LANE for g in range(layers // per)]
            tiles = [
                jnp.where(
                    even == (n == 0), near_b[rows, k : k + LANE], near_a[rows, k : k + LANE]
                )
                for k in places
            ]
            aux[first : first + SUBL, :] = jnp.concatenate(tiles, axis=0)
    rows = jnp.concatenate(
        [pos[...], temp, wide(vol[...]), jnp.zeros((3, particles), F32)], axis=0
    )
    near_a[:, :particles] = rows
    near_b[:, :particles] = rows


def surface_kernel(cap, owners, track, grid_y, n_sph, n_fv, arrived, aux, slots, heated):
    rows_x, rows_y = heated.shape
    highs = rows_x * rows_y // LANE
    corners = aux[highs : highs + 4 * SUBL, :]
    laser = aux[highs + 4 * SUBL : highs + 4 * SUBL + track, :].astype(I32)
    laser_power = aux[highs + 4 * SUBL + track :, :]
    slot_rows = slots.shape[0] // owners
    lane = iota((1, LANE), 1)
    s, f = lax.axis_index("sph"), lax.axis_index("fv")
    fold = LANE // cap
    group = owners // fold
    full = jnp.concatenate([arrived[i * SPREAD : i * SPREAD + 1, :] for i in range(owners)], axis=0)
    cells = jnp.zeros((group, LANE), F32)
    temps = jnp.zeros((group, LANE), F32)
    for g in range(fold):
        rows = full[g * group : (g + 1) * group]
        place = (lane >= g * cap) & (lane < (g + 1) * cap)
        cells = jnp.where(place, rolled(rows, g * cap, 1), cells)
        temps = jnp.where(place, rolled(rows, (g - 1) * cap, 1), temps)
    cells = cells.astype(I32)
    used = cells >= 0
    y_tiles = rows_y // LANE
    cell_x, cell_y = cells // rows_y, cells % rows_y
    high = jnp.where(used, (cell_y // LANE) * rows_x + cell_x, -1)
    low = jnp.where(used, cell_y % LANE, -1)
    laser_x = laser // grid_y - s * rows_x
    laser_y = laser % grid_y - f * rows_y
    mine = (laser_x >= 0) & (laser_x < rows_x) & (laser_y >= 0) & (laser_y < rows_y)
    l_high = jnp.where(mine, (laser_y // LANE) * rows_x + laser_x, -1)
    l_low = jnp.where(mine, laser_y % LANE, -1)
    tall_surface = aux[:highs, :]
    here = jnp.concatenate(
        [tall_surface[i * rows_x : (i + 1) * rows_x] for i in range(y_tiles)], axis=1
    )
    surf_t = jnp.transpose(jnp.concatenate(split3(tall_surface), axis=0)).astype(BF16)
    flux = jnp.zeros((3 * highs, LANE), F32)
    contact_rows = []
    step = 2
    for p in range(0, group, step):
        hit_h = hits(wide(high[p : p + step]), highs)
        hit_l = hits(wide(low[p : p + step]), LANE)
        one = jnp.where(hit_h, 1.0, 0.0).astype(BF16)
        candidates = dot_nn(surf_t, jnp.concatenate([one] * 3, axis=0))
        ghost = jnp.sum(jnp.where(hit_l, candidates, 0.0), axis=0, keepdims=True)
        contact = jnp.where(
            wide(high[p : p + step]) >= 0, CONTACT_GAIN * (wide(temps[p : p + step]) - ghost), 0.0
        )
        contact_rows.append(contact)
        left = jnp.concatenate([chosen(hit_h, part) for part in split3(contact)], axis=0)
        flux = flux + dot_nt(left, jnp.where(hit_l, 1.0, 0.0).astype(BF16))
    hit_h, hit_l = hits(wide(l_high), highs), hits(wide(l_low), LANE)
    left = jnp.concatenate([chosen(hit_h, part) for part in split3(wide(laser_power))], axis=0)
    flux = flux + dot_nt(left, jnp.where(hit_l, 1.0, 0.0).astype(BF16))
    flux = flux[:highs] + flux[highs : 2 * highs] + flux[2 * highs :]
    flux = jnp.concatenate([flux[i * rows_x : (i + 1) * rows_x] for i in range(y_tiles)], axis=1)
    hot = here + SURFACE_GAIN * flux
    heated[...] = hot
    contact = tall(jnp.concatenate(contact_rows, axis=1))
    slots[...] = jnp.zeros(slots.shape, F32)
    for g in range(fold):
        back = rolled(contact, -g * cap, 1)
        for i in range(group):
            at = (g * group + i + 1) * slot_rows - 1
            slots[at : at + 1, :] = back[i : i + 1]

    def send(ds, df, rows):
        ok = (s + ds >= 0) & (s + ds < n_sph) & (f + df >= 0) & (f + df < n_fv)

        @pl.when(ok)
        def _():
            at = ((s + ds) * n_fv + f + df) * slot_rows
            for i in range(rows.shape[0]):
                slots[pl.ds(at + i, 1), :] = rows[i : i + 1]

    send(-1, 0, by_tiles(hot[:HALO]))
    send(1, 0, by_tiles(hot[rows_x - HALO :]))
    row_tiles = rows_x // SUBL
    west = jnp.zeros((SUBL, LANE), F32)
    east = jnp.zeros((SUBL, LANE), F32)
    for t in range(row_tiles):
        rows = slice(t * SUBL, (t + 1) * SUBL)
        place = (lane >= t * HALO) & (lane < (t + 1) * HALO)
        west = jnp.where(place, rolled(hot[rows, 0:LANE], t * HALO, 1), west)
        east = jnp.where(place, rolled(hot[rows, rows_y - LANE :], (t + 1) * HALO, 1), east)
    send(0, -1, west)
    send(0, 1, east)
    sub = iota((SUBL, LANE), 0)
    for n, (df, tile, mark) in enumerate(
        ((-1, hot[:, 0:LANE], lane < HALO), (1, hot[:, rows_y - LANE :], lane >= LANE - HALO))
    ):
        for m, ds in enumerate((-1, 1)):
            static = corners[(2 * n + m) * SUBL : (2 * n + m + 1) * SUBL]
            end = tile[:SUBL] if ds < 0 else rolled(tile[rows_x - SUBL :], HALO, 0)
            send(ds, df, jnp.where(mark & (sub < HALO), end, static))


def by_tiles(x):
    return jnp.concatenate(
        [x[:, i * LANE : (i + 1) * LANE] for i in range(x.shape[1] // LANE)], axis=0
    )


def pair_kernel(n_fv, nbr, count, own, got_a, got_b, heat, left, right, inv_i, temp_i,
                inv_j, temp_j, accs):
    blocks, slots = nbr.shape
    particles = accs.shape[0]
    per = particles // blocks
    halves = per // LANE
    device = own_place(n_fv)
    even = device % 2 == 0
    row = iota((SUBL, particles), 0)
    for at in range(3):
        if at == 1:
            rows = own[:, :particles]
        else:
            rows = jnp.where(even == (at == 0), got_b[:, :particles], got_a[:, :particles])
        xyz = jnp.where(row < 3, rows, 0.0)
        norm = jnp.sum(xyz * xyz, axis=0, keepdims=True) * (-KERNEL_SCALE * LOG2E)
        t_row, v_row = rows[3:4], rows[4:5]
        inv = 1.0 / (1.0 + 0.5 * jnp.tanh(t_row))
        weight = jnp.log2(jnp.where(v_row > 0.0, v_row, 1.0) * (4.0 * KERNEL_SCALE))
        h, m, l = split3(jnp.where(row == 3, norm + weight, jnp.where(row == 4, 1.0, xyz)))
        j_side = jnp.concatenate([h, h, m, h, l, m], axis=0).astype(BF16)
        inv_rows = jnp.broadcast_to(inv, (SUBL, particles))
        temp_rows = jnp.broadcast_to(t_row, (SUBL, particles))
        for b in range(blocks):
            cols = slice(b * per, (b + 1) * per)
            right[at * blocks + b] = j_side[:, cols]
            inv_j[at * blocks + b] = inv_rows[:, cols]
            temp_j[at * blocks + b] = temp_rows[:, cols]
        if at == 1:
            scaled = xyz * (2 * KERNEL_SCALE * LOG2E)
            h, m, l = split3(jnp.where(row == 3, 1.0, jnp.where(row == 4, norm, scaled)))
            extra = jnp.where(row == 0, inv, jnp.where(row == 1, t_row, 0.0))
            turned = jnp.transpose(jnp.concatenate([h, m, h, l, h, m, extra, extra], axis=0))
            left[...] = turned[:, : 6 * SUBL].astype(BF16)
            inv_i[...] = jnp.broadcast_to(turned[:, 6 * SUBL : 6 * SUBL + 1], (particles, LANE))
            temp_i[...] = jnp.broadcast_to(turned[:, 6 * SUBL + 1 : 6 * SUBL + 2], (particles, LANE))
    nothing = 3 * blocks
    k_row = iota((6 * SUBL, per), 0)
    right[nothing] = jnp.where(k_row == 3, -16384.0, 0.0).astype(BF16)
    inv_j[nothing] = jnp.ones((SUBL, per), F32)
    temp_j[nothing] = jnp.zeros((SUBL, per), F32)
    accs[...] = jnp.zeros(accs.shape, F32)
    def one_block(b, carry):
        live = count[b]
        i0 = pl.multiple_of(b * per, per)

        def some_slots(first, together):
            who = []
            for q in range(together):
                at = first + q
                local = nbr[b, jnp.minimum(at, slots - 1)] - (device - 1) * blocks
                who.append(jnp.where(at < live, local, nothing))
            exponents = [dot_nn(left[pl.ds(i0, per), :], right[k]) for k in who]
            invs = [[inv_j[k, :, i * LANE : (i + 1) * LANE] for i in range(halves)] for k in who]
            temps = [[temp_j[k, :, i * LANE : (i + 1) * LANE] for i in range(halves)] for k in who]
            for r in range(per // SUBL):
                here = pl.ds(i0 + r * SUBL, SUBL)
                own_inv, own_temp = inv_i[here, :], temp_i[here, :]
                acc = accs[here, :]
                for q in range(together):
                    for i in range(halves):
                        part = exponents[q][r * SUBL : (r + 1) * SUBL, i * LANE : (i + 1) * LANE]
                        kernel = jnp.exp2(part) * pl.reciprocal(invs[q][i] + own_inv, approx=True)
                        acc = acc + kernel * (temps[q][i] - own_temp)
                accs[here, :] = acc

        def many(n, carry):
            some_slots(n * MANY, MANY)
            return carry

        def few(n, carry):
            some_slots(n * FEW, FEW)
            return carry

        rounds = (live + MANY - FEW - 1) // MANY
        lax.fori_loop(0, rounds, many, 0)
        lax.fori_loop(rounds * (MANY // FEW), (live + FEW - 1) // FEW, few, 0)
        return carry

    lax.fori_loop(0, blocks, one_block, 0)
    for n in range(particles // LANE):
        turned = jnp.transpose(accs[n * LANE : (n + 1) * LANE, :])
        heat[n : n + 1, :] = jnp.sum(turned, axis=0, keepdims=True)


def finish_kernel(cap, n_sph, n_fv, u, c, heated, rows_a, rows_b, near_a, near_b, got,
                  heat, own, ints, particle_out, u_out, field, other, coef, coef_side, cond, row_flux, lane_flux, down, wrap):
    layers, rows_x, rows_y = u.shape
    owners = n_sph * n_fv
    slot_rows = got.shape[0] // owners
    s, f = lax.axis_index("sph"), lax.axis_index("fv")
    lane = iota((1, LANE), 1)
    row_tiles = rows_x // SUBL
    per = LANE // PAIR
    groups = layers // per
    scale = LAMBDA_STEP * 0.5 * 0.5

    def slot(ds, df):
        at = jnp.clip(s + ds, 0, n_sph - 1) * n_fv + jnp.clip(f + df, 0, n_fv - 1)
        return jnp.concatenate(
            [got[pl.ds(at * slot_rows + i, 1), :] for i in range(slot_rows - 1)], axis=0
        )

    def flag(ok):
        return jnp.where(ok, 1.0, 0.0).astype(F32)

    has_n, has_s = flag(s > 0), flag(s < n_sph - 1)
    has_w, has_e = flag(f > 0), flag(f < n_fv - 1)
    third = ints.shape[0] // 3
    part_row, owner_row, rank_row = (wide(ints[i * third : (i + 1) * third]) for i in range(3))
    back = jnp.concatenate(
        [got[(i + 1) * slot_rows - 1 : (i + 1) * slot_rows, :] for i in range(owners)], axis=0
    )
    temp2d = tall(own[3:4, : heat.shape[0] * LANE])
    back_t = jnp.transpose(jnp.concatenate(split3(back), axis=0)).astype(BF16)
    own_one = jnp.where(hits(owner_row, owners), 1.0, 0.0).astype(BF16)
    candidates = dot_nn(back_t, jnp.concatenate([own_one] * 3, axis=0))
    contact = jnp.sum(jnp.where(hits(rank_row, LANE), candidates, 0.0), axis=0, keepdims=True)
    t_rows = temp2d.shape[0]
    hit_h = hits(part_row // LANE, t_rows)
    lefts = jnp.concatenate([jnp.where(hit_h, p, 0.0) for p in split3(contact)], axis=0).astype(BF16)
    flux = dot_nt(lefts, jnp.where(hits(part_row % LANE, LANE), 1.0, 0.0).astype(BF16))
    flux = flux[:t_rows] + flux[t_rows : 2 * t_rows] + flux[2 * t_rows :]
    particle_out[...] = temp2d + SPH_STEP * heat[...] - PARTICLE_SHARE * flux

    slab = rows_x + 2 * HALO
    slabs = LANE // slab
    deep = (layers + slabs - 1) // slabs
    assert slabs * deep == layers + 1 and SUB % 2 == 0
    place = (lane + HALO) % LANE
    spot = place % slab
    in_group = place < slabs * slab
    sides = jnp.where(spot < HALO, has_n, jnp.where(spot < HALO + rows_x, 1.0, has_s))
    lane_mask = jnp.where(in_group, sides, 0.0)
    last_group = in_group & (place >= (slabs - 1) * slab)
    end_mask = jnp.where(last_group, 0.0, lane_mask)
    not_first = jnp.where(place >= slab, 1.0, 0.0)
    sub_first = iota((SUBL, 1), 0) < HALO

    even, even_row = own_place(n_fv) % 2 == 0, s % 2 == 0
    low = lane % PAIR < HALO
    start = near_a.shape[1] - groups * row_tiles * LANE
    corner_e = [slot(ds, 1) for ds in (1, -1)]
    corner_w = [slot(ds, -1) for ds in (1, -1)]
    east_0, west_0 = slot(0, 1)[:SUBL], slot(0, -1)[:SUBL]
    empty = jnp.zeros((LANE - rows_x - 2 * SUBL, LANE), F32)
    turned_u, turned_c = [], []
    for g in range(groups):
        tiles_u, tiles_c = [], []
        for t in range(row_tiles + 1):
            if t < row_tiles:
                at = start + (g * row_tiles + t) * LANE
                a, b = near_a[:, at : at + LANE], near_b[:, at : at + LANE]
                east, west = jnp.where(even, a, b), jnp.where(even, b, a)
            else:
                rows = slice(g * HALO, (g + 1) * HALO)
                east = jnp.concatenate([k[rows] for k in corner_e], axis=0)
                west = jnp.concatenate([k[rows] for k in corner_w], axis=0)
            tile = jnp.where(low, east, west)
            if g == 0 and t < row_tiles:
                tile = jnp.where(lane < HALO, rolled(east_0, -t * HALO, 1), tile)
                tile = jnp.where(lane >= LANE - HALO, rolled(west_0, -HALO - t * HALO, 1), tile)
            tiles_u.append(tile)
            tiles_c.append(jnp.where(low, west, east))
        for tiles, turned in ((tiles_u, turned_u), (tiles_c, turned_c)):
            ends = tiles.pop()
            tiles += [jnp.where(sub_first, ends, 0.0), empty, jnp.where(sub_first, 0.0, ends)]
            turned.append(jnp.transpose(jnp.concatenate(tiles, axis=0)))

    south, north = slot(1, 0), slot(-1, 0)
    ends_0 = jnp.concatenate(
        [
            jnp.concatenate([k[i * HALO : (i + 1) * HALO] for k in (south, north)], axis=0)
            for i in range(rows_y // LANE)
        ],
        axis=1,
    )
    nothing = jnp.zeros((SUBL, rows_y), F32)

    def side_tile(after, before, is_u):
        ok_after, ok_before = after is not None and after < layers, before is not None and before < layers
        a = b = nothing
        if ok_after:
            if is_u and after == 0:
                a = ends_0
            else:
                a = jnp.where(even_row, rows_a[after], rows_b[after])
        if ok_before:
            if is_u and before == 0:
                b = ends_0
            else:
                b = jnp.where(even_row, rows_b[before], rows_a[before])
        return jnp.where(sub_first, a, b) if is_u else rolled(jnp.where(sub_first, b, a), HALO, 0)

    first_row, tiles_y = SUBL, rows_y // SUBL + 2
    for i in range(deep):
        mask = lane_mask if i < deep - 1 else end_mask
        zs = [n * deep + i for n in range(slabs)]
        for is_u, ref, array, factor in ((True, field, u, mask), (False, coef, c, mask * scale)):
            rows = []
            for n, z in enumerate(zs):
                if z >= layers:
                    rows.append(jnp.zeros((rows_x, rows_y), F32))
                else:
                    rows.append(heated[...] if is_u and z == 0 else array[z])
                rows.append(side_tile(z, zs[n + 1] if n + 1 < slabs else None, is_u))
            if slabs * slab < LANE:
                rows.append(side_tile(None, zs[0], is_u))
            rows = jnp.concatenate(rows, axis=0)
            for b in range(rows_y // LANE):
                block = jnp.transpose(rows[:, b * LANE : (b + 1) * LANE])
                ref[i, first_row + b * LANE : first_row + (b + 1) * LANE, :] = block * factor
            before, after = jnp.zeros((SUBL, LANE), F32), jnp.zeros((SUBL, LANE), F32)
            for n, z in enumerate(zs):
                if z >= layers:
                    continue
                g, k = z // per, z % per
                if is_u:
                    e_at, w_at = k * PAIR, (k - 1) % per * PAIR
                    tile_e, tile_w = turned_u[g][e_at : e_at + PAIR], turned_u[g][w_at : w_at + PAIR]
                    after = after + rolled(tile_e, n * slab, 1)
                    before = before + rolled(tile_w, n * slab, 1)
                else:
                    tile = rolled(turned_c[g][k * PAIR : (k + 1) * PAIR], HALO, 0)
                    after = after + rolled(tile, n * slab, 1)
                    before = after
            ref[i, 0:SUBL, :] = before * (factor * has_w)
            ref[i, (tiles_y - 1) * SUBL : tiles_y * SUBL, :] = after * (factor * has_e)
            ref[i, tiles_y * SUBL :, :] = jnp.zeros((SUBL, LANE), F32)
        other[i, tiles_y * SUBL :, :] = jnp.zeros((SUBL, LANE), F32)
    cond[:, tiles_y * SUBL :, :] = jnp.zeros((cond.shape[0], SUBL, LANE), F32)
    row_flux[:, :SUBL, :] = jnp.zeros((row_flux.shape[0], SUBL, LANE), F32)

    for i in range(deep):
        for t in range(tiles_y):
            rows = slice(t * SUBL, (t + 1) * SUBL)
            coef_side[i, rows, :] = pltpu.roll(coef[i, rows, :], LANE - 1, 1)

    def rows_of(t):
        return slice(t * SUBL, (t + 1) * SUBL)

    def some_layers(i0, count, source, target, end):
        def conductivity(n, t):
            return coef[i0 + n, rows_of(t), :] * (2.0 + jnp.tanh(source[i0 + n, rows_of(t), :]))

        tiles = range(tiles_y)
        spots = [(t, n) for t in tiles for n in range(count)]
        for t, n in spots:
            cond[n, rows_of(t), :] = conductivity(n, t)
        for t, n in spots:
            here, here_k = source[i0 + n, rows_of(t), :], cond[n, rows_of(t), :]
            side = pltpu.roll(here, LANE - 1, 1)
            side_k = coef_side[i0 + n, rows_of(t), :] * (2.0 + jnp.tanh(side))
            lane_flux[n, rows_of(t), :] = (here_k + side_k) * (side - here)
        for t, n in spots:
            here, here_k = source[i0 + n, rows_of(t), :], cond[n, rows_of(t), :]
            next_row = slice(t * SUBL + 1, (t + 1) * SUBL + 1)
            row_flux[n, rows_of(t + 1), :] = (here_k + cond[n, next_row, :]) * (
                source[i0 + n, next_row, :] - here
            )
        for t in tiles:
            above = down[rows_of(t), :]
            here, here_k = source[i0, rows_of(t), :], cond[0, rows_of(t), :]
            for n in range(count):
                i = i0 + n
                wraps = end and n == count - 1
                if wraps:
                    flux_z = wrap[rows_of(t), :]
                else:
                    below = source[i + 1, rows_of(t), :]
                    below_k = conductivity(n + 1, t) if n + 1 == count else cond[n + 1, rows_of(t), :]
                    beside_k = below_k
                    if end and n == count - 2:
                        beside_k = jnp.where(last_group, here_k, below_k)
                    flux_z = (here_k + beside_k) * (below - here)
                from_y = row_flux[n, rows_of(t + 1), :] - row_flux[n, (t + 1) * SUBL - 1 : (t + 2) * SUBL - 1, :]
                flux_x = lane_flux[n, rows_of(t), :]
                from_x = flux_x - pltpu.roll(flux_x, 1, 1)
                new = here + ((from_x + from_y) + (flux_z - above))
                factor = end_mask if wraps else lane_mask
                if t == 0:
                    factor = factor * has_w
                if t == tiles_y - 1:
                    factor = factor * has_e
                target[i, rows_of(t), :] = new * factor
                above = flux_z
                if not wraps:
                    here, here_k = below, below_k
            if not end:
                down[rows_of(t), :] = above

    def substep(source, target):
        for t in range(tiles_y):
            last_u, first_u = source[deep - 1, rows_of(t), :], source[0, rows_of(t), :]
            last_k = coef[deep - 1, rows_of(t), :] * (2.0 + jnp.tanh(last_u))
            first_k = coef[0, rows_of(t), :] * (2.0 + jnp.tanh(first_u))
            flux = (first_k + pltpu.roll(last_k, slab, 1)) * (first_u - pltpu.roll(last_u, slab, 1))
            flux = flux * not_first
            down[rows_of(t), :] = flux
            wrap[rows_of(t), :] = pltpu.roll(flux, LANE - slab, 1)
        together = cond.shape[0]

        def step(n, carry):
            some_layers(n * together, together, source, target, False)
            return carry

        full = (deep - 2) // together
        lax.fori_loop(0, full, step, 0)
        some_layers(full * together, deep - full * together, source, target, True)

    def two_substeps(n, carry):
        substep(field, other)
        substep(other, field)
        return carry

    lax.fori_loop(0, SUB // 2, two_substeps, 0)
    for i in range(deep):
        rows = jnp.concatenate(
            [
                jnp.transpose(field[i, first_row + b * LANE : first_row + (b + 1) * LANE, :])
                for b in range(rows_y // LANE)
            ],
            axis=1,
        )
        for n in range(slabs):
            z = n * deep + i
            if z < layers:
                u_out[z] = rows[n * slab : n * slab + rows_x]


def call(kernel, outs, ins, scratch=(), specs=None, cost=None, limit=VMEM_LIMIT):
    vmem = pl.BlockSpec(memory_space=pltpu.VMEM)
    return pl.pallas_call(
        kernel,
        out_shape=outs,
        in_specs=specs or [vmem] * len(ins),
        out_specs=jax.tree.map(lambda _: vmem, outs),
        scratch_shapes=list(scratch),
        compiler_params=pltpu.CompilerParams(vmem_limit_bytes=limit),
        cost_estimate=cost,
    )(*ins)


def body(
    positions,
    particle_temp,
    volume,
    nbr_blocks,
    nbr_count,
    iface_part,
    iface_owner,
    iface_cell,
    substrate_temp,
    conduct,
    laser_cells,
    laser_power,
):
    blocks_here = nbr_count.shape[0]
    particles = particle_temp.shape[0]
    per_block = particles // blocks_here
    layers, rows_x, rows_y = substrate_temp.shape
    n_sph, n_fv = lax.axis_size("sph"), lax.axis_size("fv")
    owners = n_sph * n_fv
    entries = iface_part.shape[0]
    cap = max(2, (2 * entries + owners - 1) // owners)
    grid_y = rows_y * n_fv
    ring = ("sph", "fv")
    shape = jax.ShapeDtypeStruct

    def as_tiles(x):
        return x.reshape(-1, LANE)

    strip = rows_x * layers * PAIR // SUBL
    message = shape((SUBL, particles + strip), F32)
    edge = shape((layers, SUBL, rows_y), F32)
    hbm = pl.BlockSpec(memory_space=pltpu.HBM)
    vmem = pl.BlockSpec(memory_space=pltpu.VMEM)
    smem = pl.BlockSpec(memory_space=pltpu.SMEM)
    temp2d, lasers = as_tiles(particle_temp), (as_tiles(laser_cells), as_tiles(laser_power))

    def bring(inputs):
        return [pltpu.VMEM(x.shape, x.dtype) for x in inputs] + [pltpu.SemaphoreType.DMA((len(inputs),))]

    inputs = (as_tiles(iface_part), as_tiles(iface_owner), as_tiles(iface_cell), temp2d) + lasers
    inputs += (positions, as_tiles(volume), substrate_temp, conduct)
    top = shape((rows_x, rows_y), F32)
    track = lasers[0].shape[0]
    aux_rows = rows_x * rows_y // LANE + 4 * SUBL + 2 * track
    request, ints, to_rows_a, to_rows_b, to_near_a, to_near_b, aux = call(
        functools.partial(prep_kernel, cap, owners, n_fv),
        (shape((owners * SPREAD, LANE), F32), shape((3 * entries // LANE, LANE), I32))
        + (edge, edge, message, message, shape((aux_rows, LANE), F32)),
        inputs,
        scratch=bring(inputs),
        specs=[hbm] * len(inputs),
        limit=FULL_VMEM,
    )
    arrived = lax.all_to_all(
        request.reshape(owners, SPREAD * LANE), ring, split_axis=0, concat_axis=0, tiled=True
    ).reshape(request.shape)
    def exchange(x, axes, count, first):
        pairs = [(i, i + 1) for i in range(first, count - 1, 2)]
        return lax.ppermute(x, axes, pairs + [(b, a) for a, b in pairs])

    near_a = exchange(to_near_a, ring, owners, 0)
    near_b = exchange(to_near_b, ring, owners, 1)
    to_rows_a, to_rows_b, near_a, near_b = lax.optimization_barrier(
        (to_rows_a, to_rows_b, near_a, near_b)
    )
    rows_a = exchange(to_rows_a, "sph", n_sph, 0)
    rows_b = exchange(to_rows_b, "sph", n_sph, 1)

    halo_rows = max(HALO * rows_y // LANE, layers * PAIR // LANE * HALO, SUBL)
    slots, heated = call(
        functools.partial(surface_kernel, cap, owners, track, grid_y, n_sph, n_fv),
        (shape((owners * (halo_rows + 1), LANE), F32), top),
        (arrived, aux),
    )
    got = lax.all_to_all(slots.reshape(owners, -1), ring, split_axis=0, concat_axis=0, tiled=True)
    got = got.reshape(slots.shape)
    wide_j = pltpu.VMEM((3 * blocks_here + 1, SUBL, per_block), F32)
    wide_i = pltpu.VMEM((particles, LANE), F32)
    heat = call(
        functools.partial(pair_kernel, n_fv),
        shape((particles // LANE, LANE), F32),
        (nbr_blocks, nbr_count, to_near_a, near_a, near_b),
        scratch=(
            pltpu.VMEM((particles, 6 * SUBL), BF16),
            pltpu.VMEM((3 * blocks_here + 1, 6 * SUBL, per_block), BF16),
            wide_i, wide_i, wide_j, wide_j, wide_i,
        ),
        specs=[smem, smem] + [vmem] * 3,
        cost=pl.CostEstimate(
            flops=160 * blocks_here * per_block * per_block, bytes_accessed=1 << 20,
            transcendentals=1 << 22,
        ),
    )
    slabs = LANE // (rows_x + 2 * HALO)
    deep = (layers + slabs - 1) // slabs
    ext = (rows_y + 3 * SUBL, LANE)
    cube = pltpu.VMEM((deep,) + ext, F32)
    some = pltpu.VMEM((3,) + ext, F32)
    flat = pltpu.VMEM(ext, F32)
    particle_out, field = call(
        functools.partial(finish_kernel, cap, n_sph, n_fv),
        (shape((particles // LANE, LANE), F32), shape(substrate_temp.shape, F32)),
        (substrate_temp, conduct, heated, rows_a, rows_b, near_a, near_b, got, heat, to_near_a, ints),
        scratch=(cube, cube, cube, cube, some, some, some, flat, flat),
    )
    return (particle_out.reshape(particles), field)


def solution(mesh):
    in_specs = (
        P(None, ("sph", "fv")),
        P(("sph", "fv")),
        P(("sph", "fv")),
        P(("sph", "fv"), None),
        P(("sph", "fv")),
        P(("sph", "fv")),
        P(("sph", "fv"), None),
        P(("sph", "fv")),
        P(None, "sph", "fv"),
        P(None, "sph", "fv"),
        P(),
        P(),
    )
    out_specs = (P(("sph", "fv")), P(None, "sph", "fv"))
    return jax.shard_map(body, mesh=mesh, in_specs=in_specs, out_specs=out_specs, check_vma=False)
```

```python
import functools

import jax
import jax.numpy as jnp
from jax import lax
from jax.experimental import pallas as pl
from jax.experimental.pallas import tpu as pltpu
from jax.sharding import PartitionSpec as P

SUB = 4
KERNEL_SCALE = 0.5
SPH_STEP = 0.05
CONTACT_GAIN = 1.0
PARTICLE_SHARE = 0.5
SURFACE_GAIN = 0.5
LAMBDA_STEP = 0.1

F32 = jnp.float32
BF16 = jnp.bfloat16
I32 = jnp.int32
LANE = 128
SUBL = 8
HALO = SUB
PAIR = 2 * HALO
SPREAD = 5
MANY, FEW = 16, 4
LOG2E = 1.4426950408889634
VMEM_LIMIT = 48 * 1024 * 1024
FULL_VMEM = 63 * 1024 * 1024


def split3(x):
    high = x.astype(BF16).astype(F32)
    rest = x - high
    mid = rest.astype(BF16).astype(F32)
    low = (rest - mid).astype(BF16).astype(F32)
    return high, mid, low


def wide(rows):
    return jnp.concatenate([rows[i : i + 1] for i in range(rows.shape[0])], axis=1)


def tall(row):
    return jnp.concatenate(
        [row[:, i * LANE : (i + 1) * LANE] for i in range(row.shape[1] // LANE)], axis=0
    )


def iota(shape, dim):
    return lax.broadcasted_iota(I32, shape, dim)


def rolled(x, shift, axis):
    size = x.shape[axis]
    shift = shift % size
    return x if shift == 0 else pltpu.roll(x, shift, axis)


def lane_next(x):
    n = x.shape[1] // LANE
    turned = [pltpu.roll(x[:, i * LANE : (i + 1) * LANE], LANE - 1, 1) for i in range(n)]
    last = iota((1, LANE), 1) == LANE - 1
    return jnp.concatenate([jnp.where(last, turned[(i + 1) % n], turned[i]) for i in range(n)], axis=1)


def lane_before(x):
    n = x.shape[1] // LANE
    turned = [pltpu.roll(x[:, i * LANE : (i + 1) * LANE], 1, 1) for i in range(n)]
    first = iota((1, LANE), 1) == 0
    return jnp.concatenate([jnp.where(first, turned[i - 1], turned[i]) for i in range(n)], axis=1)


def dot_nn(a, b):
    return lax.dot_general(a, b, (((1,), (0,)), ((), ())), preferred_element_type=F32)


def dot_nt(a, b):
    return lax.dot_general(a, b, (((1,), (1,)), ((), ())), preferred_element_type=F32)


def hits(number_row, count):
    return iota((count, number_row.shape[1]), 0) == number_row


def chosen(mask, row):
    return jnp.where(mask, row, 0.0).astype(BF16)


def own_place(n_fv):
    return lax.axis_index("sph") * n_fv + lax.axis_index("fv")


def arrive(refs, count):
    hbm, outs, bufs, sems = refs[:count], refs[count : -count - 1], refs[-count - 1 : -1], refs[-1]
    copies = [pltpu.make_async_copy(a, b, sems.at[i]) for i, (a, b) in enumerate(zip(hbm, bufs))]
    for copy in copies:
        copy.start()
    return outs, bufs, copies


def prep_kernel(cap, owners, n_fv, *refs):
    outs, bufs, copies = arrive(refs, 10)
    request, ints, rows_a, rows_b, near_a, near_b, aux = outs
    even = own_place(n_fv) % 2 == 0
    even_row = lax.axis_index("sph") % 2 == 0
    part, owner, cell, temp2d, cells_in, power_in, pos, vol, u, c = bufs
    layers, rows_x, rows_y = u.shape
    lane = iota((1, LANE), 1)
    for copy in copies[:8]:
        copy.wait()
    temp = wide(temp2d[...])
    part_row, owner_row, cell_row = wide(part[...]), wide(owner[...]), wide(cell[...])
    entries = part_row.shape[1]
    t_rows = temp2d.shape[0]
    own_hit = hits(owner_row, owners)
    own_f = jnp.where(own_hit, 1.0, 0.0).astype(F32)
    upper = jnp.where(iota((LANE, LANE), 0) <= iota((LANE, LANE), 1), 1.0, 0.0).astype(BF16)
    tiles = entries // LANE
    stacked = jnp.concatenate([own_f[:, i * LANE : (i + 1) * LANE] for i in range(tiles)], axis=0)
    within = dot_nn(stacked.astype(BF16), upper)
    before = jnp.full((owners, 1), -1.0, F32)
    ranks = []
    for i in range(tiles):
        here = within[i * owners : (i + 1) * owners]
        ranks.append(
            jnp.sum(own_f[:, i * LANE : (i + 1) * LANE] * (here + before), axis=0, keepdims=True)
        )
        before = before + here[:, LANE - 1 : LANE]
    rank_row = jnp.concatenate(ranks, axis=1).astype(I32)
    ints[...] = jnp.concatenate([part[...], owner[...], tall(rank_row)], axis=0)
    temp_t = jnp.transpose(jnp.concatenate(split3(temp2d[...]), axis=0)).astype(BF16)
    high_hit = jnp.where(hits(part_row // LANE, t_rows), 1.0, 0.0).astype(F32)
    candidates = dot_nn(temp_t, jnp.concatenate([high_hit] * 3, axis=0).astype(BF16))
    own_temp = jnp.sum(
        jnp.where(hits(part_row % LANE, LANE), candidates, 0.0), axis=0, keepdims=True
    )
    t_h, t_m, t_l = split3(own_temp)
    left = jnp.concatenate(
        [
            jnp.where(own_hit, row, 0.0)
            for row in ((cell_row // 64).astype(F32), (cell_row % 64).astype(F32), t_h, t_m, t_l)
        ]
        + [own_f],
        axis=0,
    ).astype(BF16)
    right = jnp.where(hits(rank_row, LANE), 1.0, 0.0).astype(BF16)
    out = dot_nt(left, right)
    piece = [out[i * owners : (i + 1) * owners] for i in range(6)]
    cells = piece[0] * 64.0 + piece[1] + (piece[5] - 1.0)
    temps = piece[2] + piece[3] + piece[4]
    rows = jnp.where(lane < cap, cells, rolled(temps, cap, 1))
    request[...] = jnp.zeros(request.shape, F32)
    for i in range(owners):
        request[i * SPREAD : i * SPREAD + 1, :] = rows[i : i + 1]
    for copy in copies[8:]:
        copy.wait()
    top = by_tiles(u[0])
    track = cells_in.shape[0]
    corners = top.shape[0]
    aux[:corners, :] = top
    tracks = corners + 4 * SUBL
    aux[tracks : tracks + track, :] = cells_in[...].astype(F32)
    aux[tracks + track : tracks + 2 * track, :] = power_in[...]
    for z in range(layers):
        top_u, top_c = u[z, 0:SUBL, :], c[z, 0:SUBL, :]
        end_u, end_c = u[z, rows_x - SUBL :, :], c[z, rows_x - SUBL :, :]
        first = iota((SUBL, rows_y), 0) < HALO
        to_n = jnp.where(first, top_u, rolled(top_c, HALO, 0))
        to_s = jnp.where(first, rolled(end_c, HALO, 0), end_u)
        rows_a[z] = jnp.where(even_row, to_s, to_n)
        rows_b[z] = jnp.where(even_row, to_n, to_s)
    per = LANE // PAIR
    row_tiles = rows_x // SUBL
    low = lane % PAIR < HALO
    particles = temp.shape[1]
    for g in range(layers // per):
        for t in range(row_tiles):
            rows = slice(t * SUBL, (t + 1) * SUBL)
            acc_u = jnp.zeros((SUBL, LANE), F32)
            acc_c = jnp.zeros((SUBL, LANE), F32)
            for k in range(per):
                z = g * per + k
                place = (lane + HALO - PAIR * k) % LANE < PAIR
                edge_u = jnp.where(lane < LANE // 2, u[z, rows, 0:LANE], u[z, rows, rows_y - LANE :])
                edge_c = jnp.where(lane < LANE // 2, c[z, rows, 0:LANE], c[z, rows, rows_y - LANE :])
                acc_u = jnp.where(place, rolled(edge_u, PAIR * k, 1), acc_u)
                acc_c = jnp.where(place, rolled(edge_c, PAIR * k, 1), acc_c)
            acc_c = rolled(acc_c, HALO, 1)
            at = particles + (g * row_tiles + t) * LANE
            near_a[:, at : at + LANE] = jnp.where(low == even, acc_c, acc_u)
            near_b[:, at : at + LANE] = jnp.where(low == even, acc_u, acc_c)
    at = particles
    for n in range(2):
        for m, (t, rows) in enumerate(
            ((0, slice(0, HALO)), (row_tiles - 1, slice(SUBL - HALO, SUBL)))
        ):
            first = corners + (2 * n + m) * SUBL
            places = [at + (g * row_tiles + t) * LANE for g in range(layers // per)]
            tiles = [
                jnp.where(
                    even == (n == 0), near_b[rows, k : k + LANE], near_a[rows, k : k + LANE]
                )
                for k in places
            ]
            aux[first : first + SUBL, :] = jnp.concatenate(tiles, axis=0)
    rows = jnp.concatenate(
        [pos[...], temp, wide(vol[...]), jnp.zeros((3, particles), F32)], axis=0
    )
    near_a[:, :particles] = rows
    near_b[:, :particles] = rows


def surface_kernel(cap, owners, track, grid_y, n_sph, n_fv, arrived, aux, slots, heated):
    rows_x, rows_y = heated.shape
    highs = rows_x * rows_y // LANE
    corners = aux[highs : highs + 4 * SUBL, :]
    laser = aux[highs + 4 * SUBL : highs + 4 * SUBL + track, :].astype(I32)
    laser_power = aux[highs + 4 * SUBL + track :, :]
    slot_rows = slots.shape[0] // owners
    lane = iota((1, LANE), 1)
    s, f = lax.axis_index("sph"), lax.axis_index("fv")
    fold = LANE // cap
    group = owners // fold
    full = jnp.concatenate([arrived[i * SPREAD : i * SPREAD + 1, :] for i in range(owners)], axis=0)
    cells = jnp.zeros((group, LANE), F32)
    temps = jnp.zeros((group, LANE), F32)
    for g in range(fold):
        rows = full[g * group : (g + 1) * group]
        place = (lane >= g * cap) & (lane < (g + 1) * cap)
        cells = jnp.where(place, rolled(rows, g * cap, 1), cells)
        temps = jnp.where(place, rolled(rows, (g - 1) * cap, 1), temps)
    cells = cells.astype(I32)
    used = cells >= 0
    y_tiles = rows_y // LANE
    cell_x, cell_y = cells // rows_y, cells % rows_y
    high = jnp.where(used, (cell_y // LANE) * rows_x + cell_x, -1)
    low = jnp.where(used, cell_y % LANE, -1)
    laser_x = laser // grid_y - s * rows_x
    laser_y = laser % grid_y - f * rows_y
    mine = (laser_x >= 0) & (laser_x < rows_x) & (laser_y >= 0) & (laser_y < rows_y)
    l_high = jnp.where(mine, (laser_y // LANE) * rows_x + laser_x, -1)
    l_low = jnp.where(mine, laser_y % LANE, -1)
    tall_surface = aux[:highs, :]
    here = jnp.concatenate(
        [tall_surface[i * rows_x : (i + 1) * rows_x] for i in range(y_tiles)], axis=1
    )
    surf_t = jnp.transpose(jnp.concatenate(split3(tall_surface), axis=0)).astype(BF16)
    flux = jnp.zeros((3 * highs, LANE), F32)
    contact_rows = []
    step = 2
    for p in range(0, group, step):
        hit_h = hits(wide(high[p : p + step]), highs)
        hit_l = hits(wide(low[p : p + step]), LANE)
        one = jnp.where(hit_h, 1.0, 0.0).astype(BF16)
        candidates = dot_nn(surf_t, jnp.concatenate([one] * 3, axis=0))
        ghost = jnp.sum(jnp.where(hit_l, candidates, 0.0), axis=0, keepdims=True)
        contact = jnp.where(
            wide(high[p : p + step]) >= 0, CONTACT_GAIN * (wide(temps[p : p + step]) - ghost), 0.0
        )
        contact_rows.append(contact)
        left = jnp.concatenate([chosen(hit_h, part) for part in split3(contact)], axis=0)
        flux = flux + dot_nt(left, jnp.where(hit_l, 1.0, 0.0).astype(BF16))
    hit_h, hit_l = hits(wide(l_high), highs), hits(wide(l_low), LANE)
    left = jnp.concatenate([chosen(hit_h, part) for part in split3(wide(laser_power))], axis=0)
    flux = flux + dot_nt(left, jnp.where(hit_l, 1.0, 0.0).astype(BF16))
    flux = flux[:highs] + flux[highs : 2 * highs] + flux[2 * highs :]
    flux = jnp.concatenate([flux[i * rows_x : (i + 1) * rows_x] for i in range(y_tiles)], axis=1)
    hot = here + SURFACE_GAIN * flux
    heated[...] = hot
    contact = tall(jnp.concatenate(contact_rows, axis=1))
    slots[...] = jnp.zeros(slots.shape, F32)
    for g in range(fold):
        back = rolled(contact, -g * cap, 1)
        for i in range(group):
            at = (g * group + i + 1) * slot_rows - 1
            slots[at : at + 1, :] = back[i : i + 1]

    def send(ds, df, rows):
        ok = (s + ds >= 0) & (s + ds < n_sph) & (f + df >= 0) & (f + df < n_fv)

        @pl.when(ok)
        def _():
            at = ((s + ds) * n_fv + f + df) * slot_rows
            for i in range(rows.shape[0]):
                slots[pl.ds(at + i, 1), :] = rows[i : i + 1]

    send(-1, 0, by_tiles(hot[:HALO]))
    send(1, 0, by_tiles(hot[rows_x - HALO :]))
    row_tiles = rows_x // SUBL
    west = jnp.zeros((SUBL, LANE), F32)
    east = jnp.zeros((SUBL, LANE), F32)
    for t in range(row_tiles):
        rows = slice(t * SUBL, (t + 1) * SUBL)
        place = (lane >= t * HALO) & (lane < (t + 1) * HALO)
        west = jnp.where(place, rolled(hot[rows, 0:LANE], t * HALO, 1), west)
        east = jnp.where(place, rolled(hot[rows, rows_y - LANE :], (t + 1) * HALO, 1), east)
    send(0, -1, west)
    send(0, 1, east)
    sub = iota((SUBL, LANE), 0)
    for n, (df, tile, mark) in enumerate(
        ((-1, hot[:, 0:LANE], lane < HALO), (1, hot[:, rows_y - LANE :], lane >= LANE - HALO))
    ):
        for m, ds in enumerate((-1, 1)):
            static = corners[(2 * n + m) * SUBL : (2 * n + m + 1) * SUBL]
            end = tile[:SUBL] if ds < 0 else rolled(tile[rows_x - SUBL :], HALO, 0)
            send(ds, df, jnp.where(mark & (sub < HALO), end, static))


def by_tiles(x):
    return jnp.concatenate(
        [x[:, i * LANE : (i + 1) * LANE] for i in range(x.shape[1] // LANE)], axis=0
    )


def pair_kernel(n_fv, nbr, count, own, got_a, got_b, heat, left, right, inv_i, temp_i,
                inv_j, temp_j, accs):
    blocks, slots = nbr.shape
    particles = accs.shape[0]
    per = particles // blocks
    halves = per // LANE
    device = own_place(n_fv)
    even = device % 2 == 0
    row = iota((SUBL, particles), 0)
    for at in range(3):
        if at == 1:
            rows = own[:, :particles]
        else:
            rows = jnp.where(even == (at == 0), got_b[:, :particles], got_a[:, :particles])
        xyz = jnp.where(row < 3, rows, 0.0)
        norm = jnp.sum(xyz * xyz, axis=0, keepdims=True) * (-KERNEL_SCALE * LOG2E)
        t_row, v_row = rows[3:4], rows[4:5]
        inv = 1.0 / (1.0 + 0.5 * jnp.tanh(t_row))
        weight = jnp.log2(jnp.where(v_row > 0.0, v_row, 1.0) * (4.0 * KERNEL_SCALE))
        h, m, l = split3(jnp.where(row == 3, norm + weight, jnp.where(row == 4, 1.0, xyz)))
        j_side = jnp.concatenate([h, h, m, h, l, m], axis=0).astype(BF16)
        inv_rows = jnp.broadcast_to(inv, (SUBL, particles))
        temp_rows = jnp.broadcast_to(t_row, (SUBL, particles))
        for b in range(blocks):
            cols = slice(b * per, (b + 1) * per)
            right[at * blocks + b] = j_side[:, cols]
            inv_j[at * blocks + b] = inv_rows[:, cols]
            temp_j[at * blocks + b] = temp_rows[:, cols]
        if at == 1:
            scaled = xyz * (2 * KERNEL_SCALE * LOG2E)
            h, m, l = split3(jnp.where(row == 3, 1.0, jnp.where(row == 4, norm, scaled)))
            extra = jnp.where(row == 0, inv, jnp.where(row == 1, t_row, 0.0))
            turned = jnp.transpose(jnp.concatenate([h, m, h, l, h, m, extra, extra], axis=0))
            left[...] = turned[:, : 6 * SUBL].astype(BF16)
            inv_i[...] = jnp.broadcast_to(turned[:, 6 * SUBL : 6 * SUBL + 1], (particles, LANE))
            temp_i[...] = jnp.broadcast_to(turned[:, 6 * SUBL + 1 : 6 * SUBL + 2], (particles, LANE))
    nothing = 3 * blocks
    k_row = iota((6 * SUBL, per), 0)
    right[nothing] = jnp.where(k_row == 3, -16384.0, 0.0).astype(BF16)
    inv_j[nothing] = jnp.ones((SUBL, per), F32)
    temp_j[nothing] = jnp.zeros((SUBL, per), F32)
    accs[...] = jnp.zeros(accs.shape, F32)
    def one_block(b, carry):
        live = count[b]
        i0 = pl.multiple_of(b * per, per)

        def some_slots(first, together):
            who = []
            for q in range(together):
                at = first + q
                local = nbr[b, jnp.minimum(at, slots - 1)] - (device - 1) * blocks
                who.append(jnp.where(at < live, local, nothing))
            exponents = [dot_nn(left[pl.ds(i0, per), :], right[k]) for k in who]
            invs = [[inv_j[k, :, i * LANE : (i + 1) * LANE] for i in range(halves)] for k in who]
            temps = [[temp_j[k, :, i * LANE : (i + 1) * LANE] for i in range(halves)] for k in who]
            for r in range(per // SUBL):
                here = pl.ds(i0 + r * SUBL, SUBL)
                own_inv, own_temp = inv_i[here, :], temp_i[here, :]
                acc = accs[here, :]
                for q in range(together):
                    for i in range(halves):
                        part = exponents[q][r * SUBL : (r + 1) * SUBL, i * LANE : (i + 1) * LANE]
                        kernel = jnp.exp2(part) * pl.reciprocal(invs[q][i] + own_inv, approx=True)
                        acc = acc + kernel * (temps[q][i] - own_temp)
                accs[here, :] = acc

        def many(n, carry):
            some_slots(n * MANY, MANY)
            return carry

        def few(n, carry):
            some_slots(n * FEW, FEW)
            return carry

        rounds = (live + MANY - FEW - 1) // MANY
        lax.fori_loop(0, rounds, many, 0)
        lax.fori_loop(rounds * (MANY // FEW), (live + FEW - 1) // FEW, few, 0)
        return carry

    lax.fori_loop(0, blocks, one_block, 0)
    for n in range(particles // LANE):
        turned = jnp.transpose(accs[n * LANE : (n + 1) * LANE, :])
        heat[n : n + 1, :] = jnp.sum(turned, axis=0, keepdims=True)


def finish_kernel(cap, n_sph, n_fv, u, c, heated, rows_a, rows_b, near_a, near_b, got,
                  heat, own, ints, particle_out, u_out, field, other, coef, coef_side, cond, row_flux, lane_flux, down, wrap):
    layers, rows_x, rows_y = u.shape
    owners = n_sph * n_fv
    slot_rows = got.shape[0] // owners
    s, f = lax.axis_index("sph"), lax.axis_index("fv")
    lane = iota((1, LANE), 1)
    row_tiles = rows_x // SUBL
    per = LANE // PAIR
    groups = layers // per
    scale = LAMBDA_STEP * 0.5 * 0.5

    def slot(ds, df):
        at = jnp.clip(s + ds, 0, n_sph - 1) * n_fv + jnp.clip(f + df, 0, n_fv - 1)
        return jnp.concatenate(
            [got[pl.ds(at * slot_rows + i, 1), :] for i in range(slot_rows - 1)], axis=0
        )

    def flag(ok):
        return jnp.where(ok, 1.0, 0.0).astype(F32)

    has_n, has_s = flag(s > 0), flag(s < n_sph - 1)
    has_w, has_e = flag(f > 0), flag(f < n_fv - 1)
    third = ints.shape[0] // 3
    part_row, owner_row, rank_row = (wide(ints[i * third : (i + 1) * third]) for i in range(3))
    back = jnp.concatenate(
        [got[(i + 1) * slot_rows - 1 : (i + 1) * slot_rows, :] for i in range(owners)], axis=0
    )
    temp2d = tall(own[3:4, : heat.shape[0] * LANE])
    back_t = jnp.transpose(jnp.concatenate(split3(back), axis=0)).astype(BF16)
    own_one = jnp.where(hits(owner_row, owners), 1.0, 0.0).astype(BF16)
    candidates = dot_nn(back_t, jnp.concatenate([own_one] * 3, axis=0))
    contact = jnp.sum(jnp.where(hits(rank_row, LANE), candidates, 0.0), axis=0, keepdims=True)
    t_rows = temp2d.shape[0]
    hit_h = hits(part_row // LANE, t_rows)
    lefts = jnp.concatenate([jnp.where(hit_h, p, 0.0) for p in split3(contact)], axis=0).astype(BF16)
    flux = dot_nt(lefts, jnp.where(hits(part_row % LANE, LANE), 1.0, 0.0).astype(BF16))
    flux = flux[:t_rows] + flux[t_rows : 2 * t_rows] + flux[2 * t_rows :]
    particle_out[...] = temp2d + SPH_STEP * heat[...] - PARTICLE_SHARE * flux

    slab = rows_x + 2 * HALO
    slabs = LANE // slab
    deep = (layers + slabs - 1) // slabs
    assert slabs * deep == layers + 1 and SUB % 2 == 0
    place = (lane + HALO) % LANE
    spot = place % slab
    in_group = place < slabs * slab
    sides = jnp.where(spot < HALO, has_n, jnp.where(spot < HALO + rows_x, 1.0, has_s))
    lane_mask = jnp.where(in_group, sides, 0.0)
    last_group = in_group & (place >= (slabs - 1) * slab)
    end_mask = jnp.where(last_group, 0.0, lane_mask)
    not_first = jnp.where(place >= slab, 1.0, 0.0)
    sub_first = iota((SUBL, 1), 0) < HALO

    even, even_row = own_place(n_fv) % 2 == 0, s % 2 == 0
    low = lane % PAIR < HALO
    start = near_a.shape[1] - groups * row_tiles * LANE
    corner_e = [slot(ds, 1) for ds in (1, -1)]
    corner_w = [slot(ds, -1) for ds in (1, -1)]
    east_0, west_0 = slot(0, 1)[:SUBL], slot(0, -1)[:SUBL]
    empty = jnp.zeros((LANE - rows_x - 2 * SUBL, LANE), F32)
    turned_u, turned_c = [], []
    for g in range(groups):
        tiles_u, tiles_c = [], []
        for t in range(row_tiles + 1):
            if t < row_tiles:
                at = start + (g * row_tiles + t) * LANE
                a, b = near_a[:, at : at + LANE], near_b[:, at : at + LANE]
                east, west = jnp.where(even, a, b), jnp.where(even, b, a)
            else:
                rows = slice(g * HALO, (g + 1) * HALO)
                east = jnp.concatenate([k[rows] for k in corner_e], axis=0)
                west = jnp.concatenate([k[rows] for k in corner_w], axis=0)
            tile = jnp.where(low, east, west)
            if g == 0 and t < row_tiles:
                tile = jnp.where(lane < HALO, rolled(east_0, -t * HALO, 1), tile)
                tile = jnp.where(lane >= LANE - HALO, rolled(west_0, -HALO - t * HALO, 1), tile)
            tiles_u.append(tile)
            tiles_c.append(jnp.where(low, west, east))
        for tiles, turned in ((tiles_u, turned_u), (tiles_c, turned_c)):
            ends = tiles.pop()
            tiles += [jnp.where(sub_first, ends, 0.0), empty, jnp.where(sub_first, 0.0, ends)]
            turned.append(jnp.transpose(jnp.concatenate(tiles, axis=0)))

    south, north = slot(1, 0), slot(-1, 0)
    ends_0 = jnp.concatenate(
        [
            jnp.concatenate([k[i * HALO : (i + 1) * HALO] for k in (south, north)], axis=0)
            for i in range(rows_y // LANE)
        ],
        axis=1,
    )
    nothing = jnp.zeros((SUBL, rows_y), F32)

    def side_tile(after, before, is_u):
        ok_after, ok_before = after is not None and after < layers, before is not None and before < layers
        a = b = nothing
        if ok_after:
            if is_u and after == 0:
                a = ends_0
            else:
                a = jnp.where(even_row, rows_a[after], rows_b[after])
        if ok_before:
            if is_u and before == 0:
                b = ends_0
            else:
                b = jnp.where(even_row, rows_b[before], rows_a[before])
        return jnp.where(sub_first, a, b) if is_u else rolled(jnp.where(sub_first, b, a), HALO, 0)

    first_row, tiles_y = SUBL, rows_y // SUBL + 2
    for i in range(deep):
        mask = lane_mask if i < deep - 1 else end_mask
        zs = [n * deep + i for n in range(slabs)]
        for is_u, ref, array, factor in ((True, field, u, mask), (False, coef, c, mask * scale)):
            rows = []
            for n, z in enumerate(zs):
                if z >= layers:
                    rows.append(jnp.zeros((rows_x, rows_y), F32))
                else:
                    rows.append(heated[...] if is_u and z == 0 else array[z])
                rows.append(side_tile(z, zs[n + 1] if n + 1 < slabs else None, is_u))
            if slabs * slab < LANE:
                rows.append(side_tile(None, zs[0], is_u))
            rows = jnp.concatenate(rows, axis=0)
            for b in range(rows_y // LANE):
                block = jnp.transpose(rows[:, b * LANE : (b + 1) * LANE])
                ref[i, first_row + b * LANE : first_row + (b + 1) * LANE, :] = block * factor
            before, after = jnp.zeros((SUBL, LANE), F32), jnp.zeros((SUBL, LANE), F32)
            for n, z in enumerate(zs):
                if z >= layers:
                    continue
                g, k = z // per, z % per
                if is_u:
                    e_at, w_at = k * PAIR, (k - 1) % per * PAIR
                    tile_e, tile_w = turned_u[g][e_at : e_at + PAIR], turned_u[g][w_at : w_at + PAIR]
                    after = after + rolled(tile_e, n * slab, 1)
                    before = before + rolled(tile_w, n * slab, 1)
                else:
                    tile = rolled(turned_c[g][k * PAIR : (k + 1) * PAIR], HALO, 0)
                    after = after + rolled(tile, n * slab, 1)
                    before = after
            ref[i, 0:SUBL, :] = before * (factor * has_w)
            ref[i, (tiles_y - 1) * SUBL : tiles_y * SUBL, :] = after * (factor * has_e)
            ref[i, tiles_y * SUBL :, :] = jnp.zeros((SUBL, LANE), F32)
        other[i, tiles_y * SUBL :, :] = jnp.zeros((SUBL, LANE), F32)
    cond[:, tiles_y * SUBL :, :] = jnp.zeros((cond.shape[0], SUBL, LANE), F32)
    row_flux[:, :SUBL, :] = jnp.zeros((row_flux.shape[0], SUBL, LANE), F32)

    for i in range(deep):
        for t in range(tiles_y):
            rows = slice(t * SUBL, (t + 1) * SUBL)
            coef_side[i, rows, :] = pltpu.roll(coef[i, rows, :], LANE - 1, 1)

    def rows_of(t):
        return slice(t * SUBL, (t + 1) * SUBL)

    def some_layers(i0, count, source, target, end):
        def conductivity(n, t):
            return coef[i0 + n, rows_of(t), :] * (2.0 + jnp.tanh(source[i0 + n, rows_of(t), :]))

        tiles = range(tiles_y)
        spots = [(t, n) for t in tiles for n in range(count)]
        for t, n in spots:
            cond[n, rows_of(t), :] = conductivity(n, t)
        for t, n in spots:
            here, here_k = source[i0 + n, rows_of(t), :], cond[n, rows_of(t), :]
            side = pltpu.roll(here, LANE - 1, 1)
            side_k = coef_side[i0 + n, rows_of(t), :] * (2.0 + jnp.tanh(side))
            lane_flux[n, rows_of(t), :] = (here_k + side_k) * (side - here)
        for t, n in spots:
            here, here_k = source[i0 + n, rows_of(t), :], cond[n, rows_of(t), :]
            next_row = slice(t * SUBL + 1, (t + 1) * SUBL + 1)
            row_flux[n, rows_of(t + 1), :] = (here_k + cond[n, next_row, :]) * (
                source[i0 + n, next_row, :] - here
            )
        for t in tiles:
            above = down[rows_of(t), :]
            here, here_k = source[i0, rows_of(t), :], cond[0, rows_of(t), :]
            for n in range(count):
                i = i0 + n
                wraps = end and n == count - 1
                if wraps:
                    flux_z = wrap[rows_of(t), :]
                else:
                    below = source[i + 1, rows_of(t), :]
                    below_k = conductivity(n + 1, t) if n + 1 == count else cond[n + 1, rows_of(t), :]
                    beside_k = below_k
                    if end and n == count - 2:
                        beside_k = jnp.where(last_group, here_k, below_k)
                    flux_z = (here_k + beside_k) * (below - here)
                from_y = row_flux[n, rows_of(t + 1), :] - row_flux[n, (t + 1) * SUBL - 1 : (t + 2) * SUBL - 1, :]
                flux_x = lane_flux[n, rows_of(t), :]
                from_x = flux_x - pltpu.roll(flux_x, 1, 1)
                new = here + ((from_x + from_y) + (flux_z - above))
                factor = end_mask if wraps else lane_mask
                if t == 0:
                    factor = factor * has_w
                if t == tiles_y - 1:
                    factor = factor * has_e
                target[i, rows_of(t), :] = new * factor
                above = flux_z
                if not wraps:
                    here, here_k = below, below_k
            if not end:
                down[rows_of(t), :] = above

    def substep(source, target):
        for t in range(tiles_y):
            last_u, first_u = source[deep - 1, rows_of(t), :], source[0, rows_of(t), :]
            last_k = coef[deep - 1, rows_of(t), :] * (2.0 + jnp.tanh(last_u))
            first_k = coef[0, rows_of(t), :] * (2.0 + jnp.tanh(first_u))
            flux = (first_k + pltpu.roll(last_k, slab, 1)) * (first_u - pltpu.roll(last_u, slab, 1))
            flux = flux * not_first
            down[rows_of(t), :] = flux
            wrap[rows_of(t), :] = pltpu.roll(flux, LANE - slab, 1)
        together = cond.shape[0]

        def step(n, carry):
            some_layers(n * together, together, source, target, False)
            return carry

        full = (deep - 2) // together
        lax.fori_loop(0, full, step, 0)
        some_layers(full * together, deep - full * together, source, target, True)

    def two_substeps(n, carry):
        substep(field, other)
        substep(other, field)
        return carry

    lax.fori_loop(0, SUB // 2, two_substeps, 0)
    for i in range(deep):
        rows = jnp.concatenate(
            [
                jnp.transpose(field[i, first_row + b * LANE : first_row + (b + 1) * LANE, :])
                for b in range(rows_y // LANE)
            ],
            axis=1,
        )
        for n in range(slabs):
            z = n * deep + i
            if z < layers:
                u_out[z] = rows[n * slab : n * slab + rows_x]


def call(kernel, outs, ins, scratch=(), specs=None, cost=None, limit=VMEM_LIMIT):
    vmem = pl.BlockSpec(memory_space=pltpu.VMEM)
    return pl.pallas_call(
        kernel,
        out_shape=outs,
        in_specs=specs or [vmem] * len(ins),
        out_specs=jax.tree.map(lambda _: vmem, outs),
        scratch_shapes=list(scratch),
        compiler_params=pltpu.CompilerParams(vmem_limit_bytes=limit),
        cost_estimate=cost,
    )(*ins)


def body(
    positions,
    particle_temp,
    volume,
    nbr_blocks,
    nbr_count,
    iface_part,
    iface_owner,
    iface_cell,
    substrate_temp,
    conduct,
    laser_cells,
    laser_power,
):
    blocks_here = nbr_count.shape[0]
    particles = particle_temp.shape[0]
    per_block = particles // blocks_here
    layers, rows_x, rows_y = substrate_temp.shape
    n_sph, n_fv = lax.axis_size("sph"), lax.axis_size("fv")
    owners = n_sph * n_fv
    entries = iface_part.shape[0]
    cap = max(2, (2 * entries + owners - 1) // owners)
    grid_y = rows_y * n_fv
    ring = ("sph", "fv")
    shape = jax.ShapeDtypeStruct

    def as_tiles(x):
        return x.reshape(-1, LANE)

    strip = rows_x * layers * PAIR // SUBL
    message = shape((SUBL, particles + strip), F32)
    edge = shape((layers, SUBL, rows_y), F32)
    hbm = pl.BlockSpec(memory_space=pltpu.HBM)
    vmem = pl.BlockSpec(memory_space=pltpu.VMEM)
    smem = pl.BlockSpec(memory_space=pltpu.SMEM)
    temp2d, lasers = as_tiles(particle_temp), (as_tiles(laser_cells), as_tiles(laser_power))

    def bring(inputs):
        return [pltpu.VMEM(x.shape, x.dtype) for x in inputs] + [pltpu.SemaphoreType.DMA((len(inputs),))]

    inputs = (as_tiles(iface_part), as_tiles(iface_owner), as_tiles(iface_cell), temp2d) + lasers
    inputs += (positions, as_tiles(volume), substrate_temp, conduct)
    top = shape((rows_x, rows_y), F32)
    track = lasers[0].shape[0]
    aux_rows = rows_x * rows_y // LANE + 4 * SUBL + 2 * track
    request, ints, to_rows_a, to_rows_b, to_near_a, to_near_b, aux = call(
        functools.partial(prep_kernel, cap, owners, n_fv),
        (shape((owners * SPREAD, LANE), F32), shape((3 * entries // LANE, LANE), I32))
        + (edge, edge, message, message, shape((aux_rows, LANE), F32)),
        inputs,
        scratch=bring(inputs),
        specs=[hbm] * len(inputs),
        limit=FULL_VMEM,
    )
    arrived = lax.all_to_all(
        request.reshape(owners, SPREAD * LANE), ring, split_axis=0, concat_axis=0, tiled=True
    ).reshape(request.shape)
    def exchange(x, axes, count, first):
        pairs = [(i, i + 1) for i in range(first, count - 1, 2)]
        return lax.ppermute(x, axes, pairs + [(b, a) for a, b in pairs])

    near_a = exchange(to_near_a, ring, owners, 0)
    near_b = exchange(to_near_b, ring, owners, 1)
    to_rows_a, to_rows_b, near_a, near_b = lax.optimization_barrier(
        (to_rows_a, to_rows_b, near_a, near_b)
    )
    rows_a = exchange(to_rows_a, "sph", n_sph, 0)
    rows_b = exchange(to_rows_b, "sph", n_sph, 1)

    halo_rows = max(HALO * rows_y // LANE, layers * PAIR // LANE * HALO, SUBL)
    slots, heated = call(
        functools.partial(surface_kernel, cap, owners, track, grid_y, n_sph, n_fv),
        (shape((owners * (halo_rows + 1), LANE), F32), top),
        (arrived, aux),
    )
    got = lax.all_to_all(slots.reshape(owners, -1), ring, split_axis=0, concat_axis=0, tiled=True)
    got = got.reshape(slots.shape)
    wide_j = pltpu.VMEM((3 * blocks_here + 1, SUBL, per_block), F32)
    wide_i = pltpu.VMEM((particles, LANE), F32)
    heat = call(
        functools.partial(pair_kernel, n_fv),
        shape((particles // LANE, LANE), F32),
        (nbr_blocks, nbr_count, to_near_a, near_a, near_b),
        scratch=(
            pltpu.VMEM((particles, 6 * SUBL), BF16),
            pltpu.VMEM((3 * blocks_here + 1, 6 * SUBL, per_block), BF16),
            wide_i, wide_i, wide_j, wide_j, wide_i,
        ),
        specs=[smem, smem] + [vmem] * 3,
        cost=pl.CostEstimate(
            flops=160 * blocks_here * per_block * per_block, bytes_accessed=1 << 20,
            transcendentals=1 << 22,
        ),
    )
    slabs = LANE // (rows_x + 2 * HALO)
    deep = (layers + slabs - 1) // slabs
    ext = (rows_y + 3 * SUBL, LANE)
    cube = pltpu.VMEM((deep,) + ext, F32)
    some = pltpu.VMEM((3,) + ext, F32)
    flat = pltpu.VMEM(ext, F32)
    particle_out, field = call(
        functools.partial(finish_kernel, cap, n_sph, n_fv),
        (shape((particles // LANE, LANE), F32), shape(substrate_temp.shape, F32)),
        (substrate_temp, conduct, heated, rows_a, rows_b, near_a, near_b, got, heat, to_near_a, ints),
        scratch=(cube, cube, cube, cube, some, some, some, flat, flat),
    )
    return (particle_out.reshape(particles), field)


def solution(mesh):
    in_specs = (
        P(None, ("sph", "fv")),
        P(("sph", "fv")),
        P(("sph", "fv")),
        P(("sph", "fv"), None),
        P(("sph", "fv")),
        P(("sph", "fv")),
        P(("sph", "fv"), None),
        P(("sph", "fv")),
        P(None, "sph", "fv"),
        P(None, "sph", "fv"),
        P(),
        P(),
    )
    out_specs = (P(("sph", "fv")), P(None, "sph", "fv"))
    return jax.shard_map(body, mesh=mesh, in_specs=in_specs, out_specs=out_specs, check_vma=False)
```
